32 devices in a mesh: wide: 8 (over z, y), narrow: 4 (over x, core).
Axes of the slice: x: 2, y: 2, z: 4, core: 2. Of those that a mesh axis runs over, the one named last changes fastest.
Arguments:
- tokens: bfloat16 [16, 32, 32, 768], P('wide', 'narrow'), may hold values from -6 to 6
- cotangent: bfloat16 [16, 32, 32, 768], P('wide', 'narrow'), may hold values from -6 to 6
- conditioning: bfloat16 [8, 4608], P('wide'), may hold values from -4 to 4
- aspect: int32 [16, 2], replicated, may hold values from 16 to 32, as said below
- bucket: int32 [16], replicated, may hold values from 0 to 7, as said below
- qkv_weight: bfloat16 [768, 2304], replicated, may hold values from -0.21875 to 0.21875
- attn_kernel: bfloat16 [3, 3, 2304], replicated, may hold values from -2 to 2
- out_weight: bfloat16 [768, 768], replicated, may hold values from -2 to 2
- up_weight: bfloat16 [768, 3072], replicated, may hold values from -0.21875 to 0.21875
- ffn_kernel: bfloat16 [3, 3, 3072], replicated, may hold values from -2 to 2
- down_weight: bfloat16 [3072, 768], replicated, may hold values from -0.109375 to 0.109375
Outputs:
- block_out: bfloat16 [16, 32, 32, 768], P('wide', 'narrow')
- tokens_grad: bfloat16 [16, 32, 32, 768], P('wide', 'narrow')
- cond_grad: float32 [8, 3840], P('wide')
- shift_grad: float32 [8, 768], P('wide')
- qkv_grad: float32 [768, 2304], replicated
- attn_kernel_grad: float32 [3, 3, 2304], replicated
- out_grad: float32 [768, 768], replicated
- up_grad: float32 [768, 3072], replicated
- ffn_kernel_grad: float32 [3, 3, 3072], replicated
- down_grad: float32 [3072, 768], replicated
The draws below stay inside these ranges and needn't reach their ends.
Inputs may be any that keep to these rules, and one draw needn't show every extreme that they name: In each aligned block of 2 items one item has aspect[i, 0] = 32; some item has a side of 16. bucket[i] is i // 2 or i // 2 + 1; the last 2 items have bucket 8 - 1; some bucket holds 4 items.
All inputs are finite; a program needn't handle non-finite values.
Results may differ from the reference program's by a relative error of at most 0.015.
The reference program's roundings to bfloat16 on the way count: a program that leaves them out, or rounds other values in their place, can miss the bound.
Values may be sent and summed in bfloat16 or wider, within the bound.
No kernel may reach another device: no remote copies, remote signals or barrier semaphores. Data moves between devices by JAX's collectives and lax.ppermute only.
A program may use at most 256 MiB of HBM per device.

```python
import jax
import jax.numpy as jnp
from jax import lax

D = 768
HEAD_DIM = 64
FF = 3072
GRID = 32
ITEM_DEV = 2
ITEMS = 16
BUCKETS = 8


def draw_aspect(key, part):
    key = jax.random.fold_in(key, 7)
    side_key, tall_key, short_key = jax.random.split(key, 3)
    sides = jax.random.randint(side_key, (ITEMS, 2), GRID // 2, GRID + 1)
    places = jnp.arange(ITEMS)
    group_count = ITEMS // ITEM_DEV
    tall_pick = jax.random.randint(tall_key, (group_count,), 0, ITEM_DEV)
    tall_place = jnp.arange(group_count) * ITEM_DEV + tall_pick
    is_tall = jnp.any(places[:, None] == tall_place[None, :], axis=1)
    second = jax.random.randint(short_key, (), 0, ITEMS)
    heights = jnp.where(is_tall, GRID, sides[:, 0])
    breadth = jnp.where(places == second, GRID // 2, sides[:, 1])
    return jnp.stack([heights, breadth], 1).astype(jnp.int32)


def draw_bucket(key, part):
    key = jax.random.fold_in(key, 11)
    step_key, host_key = jax.random.split(key, 2)
    places = jnp.arange(ITEMS)
    owner = places // ITEM_DEV
    steps_right = jax.random.randint(step_key, (ITEMS,), 0, 2)
    host = jax.random.randint(host_key, (), 2, BUCKETS - 1)
    steps_right = jnp.where(owner == host - 1, 1, steps_right)
    steps_right = jnp.where(owner == host, 0, steps_right)
    steps_right = jnp.where(places == 0, 0, steps_right)
    steps_right = jnp.where(owner == BUCKETS - 1, 0, steps_right)
    return (owner + steps_right).astype(jnp.int32)


def block_levels(stream_key, shape, cuts, least, high):
    gain, own = 1.0, jax.random.fold_in(stream_key, 6)
    for axis_at, parts in cuts:
        steps = jnp.exp(jax.random.uniform(jax.random.fold_in(own, axis_at), (parts,), jnp.float32, least / len(cuts), high / len(cuts)))
        gain = gain * jnp.repeat(steps, shape[axis_at] // parts).reshape([-1 if axis == axis_at else 1 for axis in range(len(shape))])
    return gain


def gaussian(rng, extent, scale, reach, cuts=(), kind=jnp.bfloat16):
    loudness = block_levels(rng, extent, cuts, -0.22, 0.18) if cuts else 1.0
    array = jax.random.normal(rng, extent, jnp.float32) * scale * loudness
    return jnp.minimum(jnp.maximum(array, -reach), reach).astype(kind)


def setup_inputs(seed: int = 0) -> dict:
    streams_of = jax.random.split(jax.random.key(seed), 12)
    tokens = gaussian(streams_of[0], (ITEMS, GRID, GRID, D), 1.0, 6.0, ((0, 8), (1, 4)))
    cotangent = gaussian(streams_of[1], (ITEMS, GRID, GRID, D), 1.0, 6.0, ((0, 8), (1, 4)))
    conditioning = gaussian(streams_of[2], (BUCKETS, 6 * D), 0.7, 4.0, ((0, 8),))
    aspect = draw_aspect(jax.random.fold_in(streams_of[11], 71), 0)
    bucket = draw_bucket(jax.random.fold_in(streams_of[11], 71), 0)
    qkv_weight = gaussian(streams_of[5], (D, 3 * D), D ** -0.5, 0.21875)
    attn_kernel = gaussian(streams_of[6], (3, 3, 3 * D), 9 ** -0.5, 2.0)
    out_weight = gaussian(streams_of[7], (D, D), (max(D // 96, 1)) ** -0.5, 2.0)
    up_weight = gaussian(streams_of[8], (D, FF), D ** -0.5, 0.21875)
    ffn_kernel = gaussian(streams_of[9], (3, 3, FF), 9 ** -0.5, 2.0)
    down_weight = gaussian(streams_of[10], (FF, D), FF ** -0.5, 0.109375)
    return {"tokens": tokens, "cotangent": cotangent, "conditioning": conditioning, "aspect": aspect, "bucket": bucket, "qkv_weight": qkv_weight, "attn_kernel": attn_kernel, "out_weight": out_weight, "up_weight": up_weight, "ffn_kernel": ffn_kernel, "down_weight": down_weight}


@jax.custom_vjp
def low(v):
    return lax.optimization_barrier(v.astype(jnp.bfloat16)).astype(jnp.float32)

@jax.custom_vjp
def low_back(v):
    return v

def low_keep(v):
    return (low(v), None)

def low_pass(kept, grad):
    return (grad,)

def back_keep(v):
    return (v, None)

def back_low(kept, grad):
    return (low(grad),)
low.defvjp(low_keep, low_pass)
low_back.defvjp(back_keep, back_low)
masked_score = -1000000000.0
norm_epsilon = 1e-06

def modulate(values, shift, scale):
    center = values - lax.optimization_barrier(jnp.mean(values, axis=-1, keepdims=True))
    spread_sq = lax.optimization_barrier(jnp.mean(center * center, axis=-1, keepdims=True))
    return center * lax.rsqrt(spread_sq + norm_epsilon) * (1.0 + scale) + shift

def project(values, matrix):
    flat = values.reshape(-1, values.shape[-1])
    result = jnp.dot(flat, matrix, precision=lax.Precision.HIGHEST, preferred_element_type=jnp.float32)
    return result.reshape(values.shape[:-1] + (matrix.shape[1],))

def depthwise(values, kernel):
    padded = jnp.pad(values, ((1, 1), (1, 1), (0, 0)))
    total = jnp.zeros(values.shape, jnp.float32)
    for row_off in range(3):
        for col_off in range(3):
            total = total + kernel[row_off, col_off] * padded[row_off:row_off + GRID, col_off:col_off + GRID]
    return total

def to_groups(values):
    half = GRID // 2
    chans = values.shape[-1]
    split = values.reshape(half, 2, half, 2, chans).transpose(1, 3, 0, 2, 4)
    return split.reshape(4, half * half, chans)

def from_groups(values):
    half = GRID // 2
    chans = values.shape[-1]
    split = values.reshape(2, 2, half, half, chans).transpose(2, 0, 3, 1, 4)
    return split.reshape(GRID, GRID, chans)

def grid_mask(sides):
    places = jnp.arange(GRID)
    return ((places[:, None] < sides[0]) & (places[None, :] < sides[1])).astype(jnp.float32)

def forward_item(values, modul, weights, token_mask):
    qkv_w, attn_k, out_w, up_w, ffn_k, down_w = weights
    shift_one, scale_one, gate_one, shift_two, scale_two, gate_two = jnp.split(modul, 6)
    base = values * token_mask[:, :, None]
    normed_one = low(modulate(base, shift_one, scale_one))
    qkv = low_back(low(project(normed_one, qkv_w)))
    conv_qkv = low_back(low(depthwise(qkv, attn_k)))
    grouped = to_groups(conv_qkv)
    key_live = to_groups(token_mask[:, :, None])[:, :, 0] > 0.5
    heads = D // HEAD_DIM
    count = grouped.shape[1]
    queries = grouped[:, :, :D].reshape(4, count, heads, HEAD_DIM)
    keys_part = grouped[:, :, D:2 * D].reshape(4, count, heads, HEAD_DIM)
    value_part = grouped[:, :, 2 * D:].reshape(4, count, heads, HEAD_DIM)
    score = jnp.einsum('gqhd,gkhd->ghqk', queries, keys_part, precision=lax.Precision.HIGHEST) * HEAD_DIM ** (-0.5)
    score = low_back(jnp.where(key_live[:, None, None, :], score, masked_score))
    prob = low(jax.nn.softmax(score, axis=-1))
    mixed = jnp.einsum('ghqk,gkhd->gqhd', prob, value_part, precision=lax.Precision.HIGHEST).reshape(4, count, D)
    mixed = low_back(low(mixed))
    attended = low_back(project(from_groups(mixed), out_w))
    middle = base + gate_one * attended
    normed_two = low(modulate(middle, shift_two, scale_two))
    hidden = low_back(low(project(normed_two, up_w)))
    conv_hidden = low_back(depthwise(hidden, ffn_k))
    activated = low(jax.nn.gelu(conv_hidden))
    branch = low_back(project(activated, down_w))
    return token_mask[:, :, None] * (middle + gate_two * branch)

def reference(tokens, cotangent, conditioning, aspect, bucket, qkv_weight, attn_kernel, out_weight, up_weight, ffn_kernel, down_weight):
    params = tuple((w.astype(jnp.float32) for w in (qkv_weight, attn_kernel, out_weight, up_weight, ffn_kernel, down_weight)))
    table = conditioning.astype(jnp.float32)

    def one_item(carry, item):
        grads, cond_acc = carry
        values, seeds, sides, owner = item
        token_mask = grid_mask(sides)
        modul = lax.dynamic_index_in_dim(table, owner, 0, keepdims=False)

        def layer_forward(inputs, modul_in, weights):
            return forward_item(inputs, modul_in, weights, token_mask)
        result, back = jax.vjp(layer_forward, values.astype(jnp.float32), modul, params)
        factor = GRID * GRID / (sides[0] * sides[1]).astype(jnp.float32)
        d_values, d_modul, d_weights = back(seeds.astype(jnp.float32) * factor)
        pick = (jnp.arange(BUCKETS) == owner).astype(jnp.float32)
        cond_acc = cond_acc + pick[:, None] * d_modul[None, :]
        grads = tuple((acc + new for acc, new in zip(grads, d_weights)))
        return ((grads, cond_acc), (result.astype(jnp.bfloat16), d_values.astype(jnp.bfloat16)))
    start = (tuple((jnp.zeros(p.shape, jnp.float32) for p in params)), jnp.zeros(table.shape, jnp.float32))
    (grads, cond_acc), (outputs, input_grads) = lax.scan(one_item, start, (tokens, cotangent, aspect, bucket))
    cond_grad = jnp.concatenate([cond_acc[:, :3 * D], cond_acc[:, 4 * D:]], 1)
    shift_grad = cond_acc[:, 3 * D:4 * D]
    return (outputs, input_grads, cond_grad, shift_grad, grads[0], grads[1], grads[2], grads[3], grads[4], grads[5])
```

```python
import functools

import jax
import jax.numpy as jnp
from jax import lax
from jax.experimental import pallas as pl
from jax.experimental.pallas import tpu as pltpu
from jax.sharding import PartitionSpec as P

HEAD_DIM = 64
LANES = 128
GROUPS = 4
MARGIN = 16

masked_score = -1000000000.0
norm_epsilon = 1e-06
gelu_root = 0.7978845608028654
gelu_cube = 0.044715

BF = jnp.bfloat16
F32 = jnp.float32
VMEM_LIMIT = 60 * 1024 * 1024


def dot(left, right, left_dim=1, right_dim=0):
    return lax.dot_general(
        left, right, (((left_dim,), (right_dim,)), ((), ())), preferred_element_type=F32
    )


def iota(shape, dim):
    return lax.broadcasted_iota(jnp.int32, shape, dim)


def phase_rows(rows, start):
    return start + iota((rows, 1), 0)


def live_rows(token, height, breadth):
    row = 2 * ((token >> 4) & 15) + (token >> 9)
    col = 2 * (token & 15) + ((token >> 8) & 1)
    return ((row < height) & (col < breadth)).astype(F32)


def to_phase_matrix():
    row = iota((256, 256), 0)
    col = iota((256, 256), 1)
    grid_row = 2 * ((row >> 4) & 3) + (row >> 7)
    grid_col = 2 * (row & 15) + ((row >> 6) & 1)
    return (col == grid_row * 32 + grid_col).astype(F32).astype(BF)


def normal(values):
    center = values - jnp.mean(values, axis=-1, keepdims=True)
    scale = lax.rsqrt(jnp.mean(center * center, axis=-1, keepdims=True) + norm_epsilon)
    return center * scale, scale


def col_sum(values):
    return jnp.sum(values, axis=0, keepdims=True)


def clear_margins(held):
    zero = jnp.zeros((2 * GROUPS, MARGIN, LANES), F32)
    held[:, 0:MARGIN, :] = zero
    held[:, MARGIN + 256 : 2 * MARGIN + 256, :] = zero


def hold(held, group_of):
    place = iota((256, LANES), 0) & 15
    for g in range(GROUPS):
        values = group_of(g)
        held[2 * g, MARGIN : MARGIN + 256, :] = values
        if g % 2:
            moved = jnp.where(place == 0, 0.0, pltpu.roll(values, 1, 0))
        else:
            moved = jnp.where(place == 15, 0.0, pltpu.roll(values, 255, 0))
        held[2 * g + 1, MARGIN : MARGIN + 256, :] = moved


def taps(g):
    alpha, beta = g // 2, g % 2
    out = []
    for a in range(3):
        for b in range(3):
            row = alpha + a - 1
            col = beta + b - 1
            src = 2 * (row % 2) + col % 2
            out.append((a, b, 2 * src + (0 if 0 <= col <= 1 else 1), MARGIN * (row // 2)))
    return out


STEP = 64


def convolve(held, kernel, write, flip=False):
    weights = [[kernel[3 * a + b : 3 * a + b + 1, :] for b in range(3)] for a in range(3)]

    def at(i, carry):
        start = pl.multiple_of(i * STEP, STEP)
        for g in range(GROUPS):
            total = None
            for a, b, src, off in taps(g):
                weight = weights[2 - a][2 - b] if flip else weights[a][b]
                part = weight * held[src, pl.ds(MARGIN + off + start, STEP), :]
                total = part if total is None else total + part
            write(g, start, total)
        return carry

    lax.fori_loop(0, 256 // STEP, at, 0)


def convolve_back(held, kernel, source, write):
    weights = [[kernel[3 * a + b : 3 * a + b + 1, :] for b in range(3)] for a in range(3)]

    def at(i, sums):
        start = pl.multiple_of(i * STEP, STEP)
        sums = list(sums)
        for g in range(GROUPS):
            total = None
            given = source(g, start)
            for a, b, src, off in taps(g):
                window = held[src, pl.ds(MARGIN + off + start, STEP), :]
                part = weights[2 - a][2 - b] * window
                total = part if total is None else total + part
                at_tap = 3 * (2 - a) + 2 - b
                prod = given * window
                sums[at_tap] = sums[at_tap] + jnp.sum(prod.reshape(STEP // 8, 8, LANES), axis=0)
            write(g, start, total)
        return tuple(sums)

    zero = jnp.zeros((8, LANES), F32)
    sums = lax.fori_loop(0, 256 // STEP, at, (zero,) * 9)
    return jnp.concatenate([col_sum(s) for s in sums], axis=0)


def attend_kernel(
    sc, p0, p1, p2, p3, mod, wq, wk, wv, kq, kk, kv,
    base_out, normed_out, qkv_out, conv_out, prob_out, mixed_out,
    held,
):
    step = pl.program_id(0)
    height, breadth = sc[0], sc[1]

    @pl.when(step == 0)
    def _():
        clear_margins(held)
        shift, scale = mod[0:1, :], 1.0 + mod[1:2, :]
        matrix = to_phase_matrix()
        for k, piece in enumerate((p0, p1, p2, p3)):
            at = sc[2 + k]
            moved = dot(matrix, piece[...])
            for g in range(GROUPS):
                start = pl.multiple_of(g * 256 + at * 64, 64)
                values = moved[g * 64 : g * 64 + 64, :] * live_rows(phase_rows(64, start), height, breadth)
                base_out[pl.ds(start, 64), :] = values.astype(BF)
                normed_out[pl.ds(start, 64), :] = (normal(values)[0] * scale + shift).astype(BF)

    weight = jnp.concatenate([wq[...], wk[...], wv[...]], axis=1)
    for r in range(0, 1024, 512):
        qkv_out[0, r : r + 512, :] = dot(normed_out[r : r + 512, :], weight).astype(BF)
    for s, kernel in enumerate((kq, kk, kv)):
        cols = slice(s * LANES, (s + 1) * LANES)
        hold(held, lambda g: qkv_out[0, g * 256 : g * 256 + 256, cols].astype(F32))

        def write(g, start, total):
            conv_out[0, pl.ds(g * 256 + start, STEP), cols] = total.astype(BF)

        convolve(held, kernel[...].astype(F32), write)

    token = iota((1, 256), 1)
    lane = iota((256, LANES), 1)

    def group(g, carry):
        start = pl.multiple_of(g * 256, 256)
        rows = pl.ds(start, 256)
        live = live_rows(token + start, height, breadth) > 0.5
        query = conv_out[0, rows, 0:LANES] * BF(HEAD_DIM**-0.5)
        key = conv_out[0, rows, LANES : 2 * LANES]
        value = conv_out[0, rows, 2 * LANES : 3 * LANES]
        parts = []
        for h in range(2):
            mine = (lane < HEAD_DIM) if h == 0 else (lane >= HEAD_DIM)
            score = dot(jnp.where(mine, query, BF(0)), key, 1, 1)
            score = jnp.where(live, score, masked_score)
            top = jnp.max(score, axis=-1, keepdims=True)
            raised = jnp.exp(score - top)
            prob = (raised * (1.0 / jnp.sum(raised, axis=-1, keepdims=True))).astype(BF)
            prob_out[0, g, h] = prob
            parts.append(dot(prob, value))
        mixed_out[rows, :] = jnp.where(lane < HEAD_DIM, parts[0], parts[1]).astype(BF)
        return carry

    lax.fori_loop(0, GROUPS, group, 0)


def attend(sc, pieces, mod, qkv_weight, attn_kernel):
    def piece_spec():
        return pl.BlockSpec((256, 768), lambda i, s: (0, 0))

    def weight_spec(k):
        return pl.BlockSpec((768, LANES), lambda i, s: (0, 6 * k + 3 * s[6] + i))

    def kernel_spec(k):
        return pl.BlockSpec((9, LANES), lambda i, s: (0, 6 * k + 3 * s[6] + i))

    whole = pl.BlockSpec((1024, 768), lambda i, s: (0, 0))
    return pl.pallas_call(
        attend_kernel,
        grid_spec=pltpu.PrefetchScalarGridSpec(
            num_scalar_prefetch=1,
            grid=(3,),
            in_specs=[piece_spec() for _ in range(4)]
            + [pl.BlockSpec((8, 768), lambda i, s: (0, 0))]
            + [weight_spec(k) for k in range(3)]
            + [kernel_spec(k) for k in range(3)],
            out_specs=[
                whole,
                whole,
                pl.BlockSpec((1, 1024, 384), lambda i, s: (i, 0, 0)),
                pl.BlockSpec((1, 1024, 384), lambda i, s: (i, 0, 0)),
                pl.BlockSpec((1, GROUPS, 2, 256, 256), lambda i, s: (i, 0, 0, 0, 0)),
                pl.BlockSpec((1024, LANES), lambda i, s: (0, i)),
            ],
            scratch_shapes=[pltpu.VMEM((2 * GROUPS, 2 * MARGIN + 256, LANES), F32)],
        ),
        out_shape=[
            jax.ShapeDtypeStruct((1024, 768), BF),
            jax.ShapeDtypeStruct((1024, 768), BF),
            jax.ShapeDtypeStruct((3, 1024, 384), BF),
            jax.ShapeDtypeStruct((3, 1024, 384), BF),
            jax.ShapeDtypeStruct((3, GROUPS, 2, 256, 256), BF),
            jax.ShapeDtypeStruct((1024, 384), BF),
        ],
        compiler_params=pltpu.CompilerParams(vmem_limit_bytes=VMEM_LIMIT),
        cost_estimate=pl.CostEstimate(flops=3_000_000_000, bytes_accessed=20_000_000, transcendentals=1600000),
        name="attend",
    )(sc, *pieces, mod, qkv_weight, qkv_weight, qkv_weight, attn_kernel, attn_kernel, attn_kernel)


def middle_kernel(
    sc, mixed_own, mixed_other, base, out_weight, mod, c0, c1, c2, c3,
    attended_out, middle_out, normed_out, branch_grad_out, seed_out,
    mixed, attended,
):
    height, breadth, core = sc[0], sc[1], sc[6]
    mixed[:, pl.ds(pl.multiple_of(core * 384, LANES), 384)] = mixed_own[...]
    mixed[:, pl.ds(pl.multiple_of((1 - core) * 384, LANES), 384)] = mixed_other[...]
    for r in range(0, 1024, 512):
        attended[r : r + 512, :] = dot(mixed[r : r + 512, :], out_weight[...])
    gate = mod[2:3, :]
    shift, scale = mod[3:4, :], 1.0 + mod[4:5, :]

    def at(i, carry):
        rows = pl.ds(pl.multiple_of(i * 64, 64), 64)
        got = attended[rows, :]
        attended_out[rows, :] = got.astype(BF)
        middle = base[rows, :].astype(F32) + gate * got
        middle_out[rows, :] = middle
        normed_out[rows, :] = (normal(middle)[0] * scale + shift).astype(BF)
        return carry

    lax.fori_loop(0, 16, at, 0)
    matrix = to_phase_matrix()
    gate_two, factor = mod[5:6, :], mod[6:7, :]
    for k, piece in enumerate((c0, c1, c2, c3)):
        at = sc[2 + k]
        moved = dot(matrix, piece[...])
        for g in range(GROUPS):
            start = pl.multiple_of(g * 256 + at * 64, 64)
            values = moved[g * 64 : g * 64 + 64, :] * live_rows(phase_rows(64, start), height, breadth)
            seed_out[pl.ds(start, 64), :] = values.astype(BF)
            branch_grad_out[pl.ds(start, 64), :] = (values * factor * gate_two).astype(BF)


def project_out(sc, mixed_own, mixed_other, base, out_weight, mod, pieces):
    full = lambda *shape: pl.BlockSpec(shape, lambda i, s: (0,) * len(shape))
    tokens = full(1024, 768)
    return pl.pallas_call(
        middle_kernel,
        grid_spec=pltpu.PrefetchScalarGridSpec(
            num_scalar_prefetch=1,
            grid=(1,),
            in_specs=[full(1024, 384), full(1024, 384), tokens, full(768, 768), full(8, 768)]
            + [full(256, 768)] * 4,
            out_specs=[tokens] * 5,
            scratch_shapes=[pltpu.VMEM((1024, 768), BF), pltpu.VMEM((1024, 768), F32)],
        ),
        out_shape=[
            jax.ShapeDtypeStruct((1024, 768), BF),
            jax.ShapeDtypeStruct((1024, 768), F32),
            jax.ShapeDtypeStruct((1024, 768), BF),
            jax.ShapeDtypeStruct((1024, 768), BF),
            jax.ShapeDtypeStruct((1024, 768), BF),
        ],
        compiler_params=pltpu.CompilerParams(vmem_limit_bytes=VMEM_LIMIT),
        cost_estimate=pl.CostEstimate(flops=2_000_000_000, bytes_accessed=20_000_000, transcendentals=0),
        name="project_out",
    )(sc, mixed_own, mixed_other, base, out_weight, mod, *pieces)


BLOCK = 256


def feed_kernel(
    first, sc, normed, branch_grad, up, down, kernel, *rest,
):
    if first:
        (down_grad, up_grad, kernel_grad, branch_out, normed_grad_out,
         held, normed_t, hid, d_act, acts, d_conv, d_hids) = rest
    else:
        (branch_in, normed_grad_in, down_grad, up_grad, kernel_grad, branch_out, normed_grad_out,
         held, normed_t, hid, d_act, acts, d_conv, d_hids) = rest
    step = pl.program_id(0)

    @pl.when(step == 0)
    def _():
        clear_margins(held)
        for r in range(0, 1024, 256):
            normed_t[:, r : r + 256] = normed[r : r + 256, :].T

    block = pl.ds(pl.multiple_of(step * BLOCK, BLOCK), BLOCK)
    for r in range(0, 1024, 512):
        hid[r : r + 512, :] = dot(normed[r : r + 512, :], up[:, block]).astype(BF)
        d_act[r : r + 512, :] = dot(branch_grad[r : r + 512, :], down[block, :], 1, 1)
    for lane_block in range(BLOCK // LANES):
        cols = slice(lane_block * LANES, (lane_block + 1) * LANES)
        dest = pl.ds(pl.multiple_of(step * BLOCK + lane_block * LANES, LANES), LANES)
        weights = kernel[:, cols].astype(F32)
        hold(held, lambda g: hid[g * 256 : g * 256 + 256, cols].astype(F32))

        def activate(g, start, v):
            rows = pl.ds(g * 256 + start, STEP)
            square = v * v
            bent = jnp.tanh(gelu_root * v * (1.0 + gelu_cube * square))
            half = 0.5 + 0.5 * bent
            acts[rows, dest] = (v * half).astype(BF)
            slope = half + 0.5 * v * (1.0 - bent * bent) * (gelu_root + 3.0 * gelu_root * gelu_cube * square)
            d_conv[rows, :] = (d_act[rows, cols] * slope).astype(BF)

        convolve(held, weights, activate)
        hold(held, lambda g: d_conv[g * 256 : g * 256 + 256, :].astype(F32))

        def source(g, start):
            return hid[pl.ds(g * 256 + start, STEP), cols].astype(F32)

        def write(g, start, total):
            d_hids[pl.ds(g * 256 + start, STEP), dest] = total.astype(BF)

        kernel_grad[:, cols] = convolve_back(held, weights, source, write)
    down_grad[block, :] = dot(acts[:, block].T, branch_grad[...]).astype(BF)
    up_grad[:, block] = dot(normed_t[...], d_hids[:, block]).astype(BF)

    @pl.when(step == pl.num_programs(0) - 1)
    def _():
        for r in range(0, 1024, 512):
            rows = slice(r, r + 512)
            branch = dot(acts[rows, :], down[...])
            normed_grad = dot(d_hids[rows, :], up[...], 1, 1)
            if not first:
                branch = branch + branch_in[rows, :]
                normed_grad = normed_grad + normed_grad_in[rows, :]
            branch_out[rows, :] = branch
            normed_grad_out[rows, :] = normed_grad


def feed(sc, normed, branch_grad, up_weight, down_weight, ffn_kernel, half, before):
    full = lambda *shape: pl.BlockSpec(shape, lambda i, s: (0,) * len(shape))
    tokens = full(1024, 768)
    first = before is None
    return pl.pallas_call(
        functools.partial(feed_kernel, first),
        grid_spec=pltpu.PrefetchScalarGridSpec(
            num_scalar_prefetch=1,
            grid=(3,),
            in_specs=[
                tokens,
                tokens,
                pl.BlockSpec((768, 768), lambda i, s: (0, 2 * s[6] + half)),
                pl.BlockSpec((768, 768), lambda i, s: (2 * s[6] + half, 0)),
                pl.BlockSpec((9, BLOCK), lambda i, s: (0, 6 * s[6] + 3 * half + i)),
            ]
            + ([] if first else [tokens, tokens]),
            out_specs=[
                full(768, 768),
                full(768, 768),
                pl.BlockSpec((9, BLOCK), lambda i, s: (0, i)),
                tokens,
                tokens,
            ],
            scratch_shapes=[
                pltpu.VMEM((2 * GROUPS, 2 * MARGIN + 256, LANES), F32),
                pltpu.VMEM((768, 1024), BF),
                pltpu.VMEM((1024, BLOCK), BF),
                pltpu.VMEM((1024, BLOCK), F32),
                pltpu.VMEM((1024, 768), BF),
                pltpu.VMEM((1024, LANES), BF),
                pltpu.VMEM((1024, 768), BF),
            ],
        ),
        out_shape=[
            jax.ShapeDtypeStruct((768, 768), BF),
            jax.ShapeDtypeStruct((768, 768), BF),
            jax.ShapeDtypeStruct((9, 768), F32),
            jax.ShapeDtypeStruct((1024, 768), F32),
            jax.ShapeDtypeStruct((1024, 768), F32),
        ],
        compiler_params=pltpu.CompilerParams(vmem_limit_bytes=VMEM_LIMIT),
        cost_estimate=pl.CostEstimate(flops=7_500_000_000, bytes_accessed=20_000_000, transcendentals=800000),
        name="feed",
    )(sc, normed, branch_grad, up_weight, down_weight, ffn_kernel, *([] if first else before))


def finish_kernel(sc, middle, branch, branch_other, seed, mod, near_out, far_out, sums_out):
    height, breadth, core = sc[0], sc[1], sc[6]
    gate, factor = mod[5:6, :], mod[6:7, :]
    matrix = to_phase_matrix()
    total = jnp.zeros((1, 768), F32)
    for local in range(2):
        parts = []
        for g in range(GROUPS):
            token = phase_rows(64, g * 256 + (2 * local + core) * 64)
            whole = branch[2 * g + local, 0] + branch_other[2 * g + local].astype(F32)
            total = total + col_sum(seed[2 * g + local, 0].astype(F32) * whole)
            result = middle[2 * g + local, 0] + gate * whole
            parts.append((result * live_rows(token, height, breadth)).astype(BF))
        done = dot(matrix, jnp.concatenate(parts, axis=0), 0, 0).astype(BF)

        @pl.when(sc[7] == local)
        def _():
            near_out[...] = done

        @pl.when(sc[7] != local)
        def _():
            far_out[...] = done

    sums_out[...] = total * factor


def half_spec():
    return pl.BlockSpec((8, 1, 64, 768), lambda i, s: (0, s[6], 0, 0))


def finish(sc, middle, branch, branch_other, seed, mod):
    full = lambda *shape: pl.BlockSpec(shape, lambda i, s: (0,) * len(shape))
    halves = lambda v: v.reshape(8, 2, 64, 768)
    return pl.pallas_call(
        finish_kernel,
        grid_spec=pltpu.PrefetchScalarGridSpec(
            num_scalar_prefetch=1,
            grid=(1,),
            in_specs=[half_spec(), half_spec(), full(8, 64, 768), half_spec(), full(8, 768)],
            out_specs=[full(256, 768), full(256, 768), full(1, 768)],
        ),
        out_shape=[
            jax.ShapeDtypeStruct((256, 768), BF),
            jax.ShapeDtypeStruct((256, 768), BF),
            jax.ShapeDtypeStruct((1, 768), F32),
        ],
        compiler_params=pltpu.CompilerParams(vmem_limit_bytes=VMEM_LIMIT),
        cost_estimate=pl.CostEstimate(flops=300_000_000, bytes_accessed=6_000_000, transcendentals=0),
        name="finish",
    )(sc, halves(middle), halves(branch), branch_other, halves(seed), mod)


def attend_back_kernel(
    sc, normed_grad, normed_grad_other, middle, attended, seed, mod,
    mixed, out_weight, normed, qkv, conv, prob, wq, wk, wv, kq, kk, kv,
    middle_grad, sums_out, weight_grad, kernel_grad, normed_grad_out,
    held, normed_t, d_att, d_mixed, d_conv, d_qkv,
):
    step = pl.program_id(0)

    @pl.when(step == 0)
    def _():
        clear_margins(held)
        for r in range(0, 1024, 256):
            normed_t[:, r : r + 256] = normed[r : r + 256, :].T
        gate, scale, factor = mod[2:3, :], 1.0 + mod[4:5, :], mod[6:7, :]

        def at(i, sums):
            d_shift, d_scale, d_gate = sums
            rows = pl.ds(pl.multiple_of(i * 64, 64), 64)
            grad = normed_grad[rows, :] + normed_grad_other[rows, :].astype(F32)
            unit, inverse = normal(middle[rows, :])
            both = grad * unit
            d_shift = d_shift + col_sum(grad)
            d_scale = d_scale + col_sum(both)
            grad = grad * scale
            mean = jnp.mean(grad, axis=-1, keepdims=True)
            along = jnp.mean(both * scale, axis=-1, keepdims=True)
            total = seed[rows, :].astype(F32) * factor + inverse * (grad - mean - unit * along)
            middle_grad[rows, :] = total
            d_gate = d_gate + col_sum(total * attended[rows, :].astype(F32))
            d_att[rows, :] = (total * gate).astype(BF)
            return d_shift, d_scale, d_gate

        zero = jnp.zeros((1, 768), F32)
        sums = lax.fori_loop(0, 16, at, (zero, zero, zero))
        for k in range(3):
            sums_out[k : k + 1, :] = 0.5 * sums[k]
        mixed_t = mixed[...].T
        grad = dot(mixed_t, d_att[...]).astype(BF)
        weight_grad[0:384, 1152:1536] = grad[:, 0:384]
        weight_grad[384:768, 1152:1536] = grad[:, 384:768]

    for r in range(0, 1024, 512):
        d_mixed[r : r + 512, :] = dot(d_att[r : r + 512, :], out_weight[...], 1, 1).astype(BF)

    lane = iota((256, LANES), 1)

    def group(g, carry):
        rows = pl.ds(pl.multiple_of(g * 256, 256), 256)
        grad = d_mixed[rows, :]
        query = conv[0, rows, 0:LANES]
        key = conv[0, rows, LANES : 2 * LANES]
        value = conv[0, rows, 2 * LANES : 3 * LANES]
        parts = []
        for h in range(2):
            mine = (lane < HEAD_DIM) if h == 0 else (lane >= HEAD_DIM)
            p = prob[0, g, h]
            d_value = dot(p.T, grad)
            d_prob = dot(jnp.where(mine, grad, BF(0)), value, 1, 1)
            wide_p = p.astype(F32)
            inner = jnp.sum(d_prob * wide_p, axis=-1, keepdims=True)
            d_score = (wide_p * (d_prob - inner)).astype(BF)
            parts.append((dot(d_score, key), dot(d_score.T, query), d_value))
        low = lane < HEAD_DIM
        for k in range(3):
            picked = jnp.where(low, parts[0][k], parts[1][k])
            if k < 2:
                picked = picked * HEAD_DIM**-0.5
            d_conv[rows, k * LANES : (k + 1) * LANES] = picked.astype(BF)
        return carry

    lax.fori_loop(0, GROUPS, group, 0)
    for s, kernel in enumerate((kq, kk, kv)):
        cols = slice(s * LANES, (s + 1) * LANES)
        hold(held, lambda g: d_conv[g * 256 : g * 256 + 256, cols].astype(F32))

        def source(g, start):
            return qkv[0, pl.ds(g * 256 + start, STEP), cols].astype(F32)

        def write(g, start, total):
            d_qkv[pl.ds(g * 256 + start, STEP), cols] = total.astype(BF)

        kernel_grad[0, :, cols] = convolve_back(held, kernel[...].astype(F32), source, write)
    grad = dot(normed_t[...], d_qkv[...]).astype(BF)
    for s in range(3):
        dest = pl.ds(pl.multiple_of(s * 384 + step * LANES, LANES), LANES)
        weight_grad[:, dest] = grad[:, s * LANES : (s + 1) * LANES]
    weight = jnp.concatenate([wq[...], wk[...], wv[...]], axis=1)
    for r in range(0, 1024, 512):
        part = dot(d_qkv[r : r + 512, :], weight, 1, 1)

        @pl.when(step == 0)
        def _():
            normed_grad_out[r : r + 512, :] = part

        @pl.when(step != 0)
        def _():
            normed_grad_out[r : r + 512, :] += part


def attend_back(sc, normed_grad, normed_grad_other, middle, attended, seed, mod, mixed, out_weight,
                normed, qkv, conv, prob, qkv_weight, attn_kernel):
    full = lambda *shape: pl.BlockSpec(shape, lambda i, s: (0,) * len(shape))
    tokens = full(1024, 768)

    def weight_spec(k):
        return pl.BlockSpec((768, LANES), lambda i, s: (0, 6 * k + 3 * s[6] + i))

    def kernel_spec(k):
        return pl.BlockSpec((9, LANES), lambda i, s: (0, 6 * k + 3 * s[6] + i))

    saved = pl.BlockSpec((1, 1024, 384), lambda i, s: (i, 0, 0))
    return pl.pallas_call(
        attend_back_kernel,
        grid_spec=pltpu.PrefetchScalarGridSpec(
            num_scalar_prefetch=1,
            grid=(3,),
            in_specs=[tokens, tokens, tokens, tokens, tokens, full(8, 768), full(1024, 384),
                      pl.BlockSpec((LANES, 768), lambda i, s: (3 * s[6] + i, 0)),
                      tokens, saved, saved,
                      pl.BlockSpec((1, GROUPS, 2, 256, 256), lambda i, s: (i, 0, 0, 0, 0))]
            + [weight_spec(k) for k in range(3)]
            + [kernel_spec(k) for k in range(3)],
            out_specs=[
                tokens,
                full(3, 768),
                full(768, 1536),
                pl.BlockSpec((1, 9, 384), lambda i, s: (i, 0, 0)),
                tokens,
            ],
            scratch_shapes=[
                pltpu.VMEM((2 * GROUPS, 2 * MARGIN + 256, LANES), F32),
                pltpu.VMEM((768, 1024), BF),
                pltpu.VMEM((1024, 768), BF),
                pltpu.VMEM((1024, LANES), BF),
                pltpu.VMEM((1024, 384), BF),
                pltpu.VMEM((1024, 384), BF),
            ],
        ),
        out_shape=[
            jax.ShapeDtypeStruct((1024, 768), F32),
            jax.ShapeDtypeStruct((3, 768), F32),
            jax.ShapeDtypeStruct((768, 1536), BF),
            jax.ShapeDtypeStruct((3, 9, 384), F32),
            jax.ShapeDtypeStruct((1024, 768), F32),
        ],
        compiler_params=pltpu.CompilerParams(vmem_limit_bytes=VMEM_LIMIT),
        cost_estimate=pl.CostEstimate(flops=8_000_000_000, bytes_accessed=30_000_000, transcendentals=0),
        name="attend_back",
    )(sc, normed_grad, normed_grad_other, middle, attended, seed, mod, mixed, out_weight,
      normed, qkv, conv, prob, qkv_weight, qkv_weight, qkv_weight, attn_kernel, attn_kernel, attn_kernel)


def input_kernel(sc, grad, grad_other, middle_grad, base, mod, near_out, far_out, sums_out):
    height, breadth, core = sc[0], sc[1], sc[6]
    scale = 1.0 + mod[1:2, :]
    matrix = to_phase_matrix()
    d_shift = jnp.zeros((1, 768), F32)
    d_scale = jnp.zeros((1, 768), F32)
    for local in range(2):
        parts = []
        for g in range(GROUPS):
            at = 2 * g + local
            token = phase_rows(64, g * 256 + (2 * local + core) * 64)
            total = grad[at, 0] + grad_other[at].astype(F32)
            unit, inverse = normal(base[at, 0].astype(F32))
            both = total * unit
            d_shift = d_shift + col_sum(total)
            d_scale = d_scale + col_sum(both)
            total = total * scale
            mean = jnp.mean(total, axis=-1, keepdims=True)
            along = jnp.mean(both * scale, axis=-1, keepdims=True)
            total = middle_grad[at, 0] + inverse * (total - mean - unit * along)
            parts.append((total * live_rows(token, height, breadth)).astype(BF))
        done = dot(matrix, jnp.concatenate(parts, axis=0), 0, 0).astype(BF)

        @pl.when(sc[7] == local)
        def _():
            near_out[...] = done

        @pl.when(sc[7] != local)
        def _():
            far_out[...] = done

    sums_out[0:1, :] = d_shift
    sums_out[1:2, :] = d_scale


def input_grad(sc, grad, grad_other, middle_grad, base, mod):
    full = lambda *shape: pl.BlockSpec(shape, lambda i, s: (0,) * len(shape))
    halves = lambda v: v.reshape(8, 2, 64, 768)
    return pl.pallas_call(
        input_kernel,
        grid_spec=pltpu.PrefetchScalarGridSpec(
            num_scalar_prefetch=1,
            grid=(1,),
            in_specs=[half_spec(), full(8, 64, 768), half_spec(), half_spec(), full(8, 768)],
            out_specs=[full(256, 768), full(256, 768), full(2, 768)],
        ),
        out_shape=[
            jax.ShapeDtypeStruct((256, 768), BF),
            jax.ShapeDtypeStruct((256, 768), BF),
            jax.ShapeDtypeStruct((2, 768), F32),
        ],
        compiler_params=pltpu.CompilerParams(vmem_limit_bytes=VMEM_LIMIT),
        cost_estimate=pl.CostEstimate(flops=300_000_000, bytes_accessed=6_000_000, transcendentals=0),
        name="input_grad",
    )(sc, halves(grad), grad_other, halves(middle_grad), halves(base), mod)


def swap(values, axis, bit):
    count = lax.axis_size(axis)
    return lax.ppermute(values, axis, [(i, i ^ bit) for i in range(count)])


def bits_of(count):
    return [1 << k for k in range(count.bit_length() - 1)]


def halving_order():
    wide = [("wide", bit) for bit in bits_of(lax.axis_size("wide"))]
    return wide


def has_bit(axis, bit):
    return (lax.axis_index(axis) & bit) != 0


def scatter_sum(block, order):
    for axis, bit in order:
        high = has_bit(axis, bit)
        half = block.shape[0] // 2
        lower, upper = block[:half], block[half:]
        send = jnp.where(high, lower, upper)
        keep = jnp.where(high, upper, lower)
        got = swap(send, axis, bit)
        block = (keep.astype(F32) + got.astype(F32)).astype(BF)
    return block


def gather(block, order):
    for axis, bit in reversed(order):
        got = swap(block, axis, bit)
        high = has_bit(axis, bit)
        block = jnp.concatenate([jnp.where(high, got, block), jnp.where(high, block, got)], axis=0)
    return block


def sum_all(values, order):
    for axis, bit in order:
        values = values + swap(values, axis, bit)
    return values


def on_device(
    tokens, cotangent, conditioning, aspect, bucket,
    qkv_weight, attn_kernel, out_weight, up_weight, ffn_kernel, down_weight,
):
    wide_count = lax.axis_size("wide")
    wide_at = lax.axis_index("wide")
    narrow_at = lax.axis_index("narrow")
    pair, core = narrow_at // 2, narrow_at % 2
    item = 2 * wide_at + pair
    sides = lax.dynamic_index_in_dim(aspect, item, 0, keepdims=False)
    home = lax.dynamic_index_in_dim(bucket, item, 0, keepdims=False)
    stays = home == wide_at

    def pieces_of(block):
        flat = block.reshape(2, 256, 768)
        own = lax.dynamic_index_in_dim(flat, pair, 0, keepdims=False)
        far = lax.dynamic_index_in_dim(flat, 1 - pair, 0, keepdims=False)
        got = swap(far, "narrow", 2)
        return own, got, swap(own, "narrow", 1), swap(got, "narrow", 1)

    token_pieces = pieces_of(tokens)
    seed_pieces = pieces_of(cotangent)
    from_right = lax.ppermute(conditioning, "wide", [(i + 1, i) for i in range(wide_count - 1)])
    modul = jnp.where(stays, conditioning, from_right).astype(F32).reshape(6, 768)
    factor = 1024.0 / (sides[0] * sides[1]).astype(F32)
    mod = jnp.concatenate([modul, jnp.full((2, 768), factor, F32)], axis=0)
    sc = jnp.stack(
        [sides[0], sides[1], 2 * pair + core, 2 * (1 - pair) + core, 2 * pair + 1 - core,
         2 * (1 - pair) + 1 - core, core, pair]
    ).astype(jnp.int32)
    attn_k = attn_kernel.reshape(9, -1)
    ffn_k = ffn_kernel.reshape(9, -1)

    base, normed_one, qkv, conv, prob, mixed = attend(sc, token_pieces, mod, qkv_weight, attn_k)
    mixed_other = swap(mixed, "narrow", 1)
    attended, middle, normed_two, d_branch, seed = project_out(
        sc, mixed, mixed_other, base, out_weight, mod, seed_pieces
    )
    down_a, up_a, ffn_a, branch, d_normed = feed(
        sc, normed_two, d_branch, up_weight, down_weight, ffn_k, 0, None
    )
    down_b, up_b, ffn_b, branch, d_normed = feed(
        sc, normed_two, d_branch, up_weight, down_weight, ffn_k, 1, (branch, d_normed)
    )

    def other_half(values):
        cut = values.reshape(8, 2, 64, 768)
        return lax.dynamic_index_in_dim(cut, 1 - core, 1, keepdims=False).astype(BF)

    d_normed_other = swap(d_normed.astype(BF), "narrow", 1)
    branch_other = swap(other_half(branch), "narrow", 1)
    near, far, d_gate_two = finish(sc, middle, branch, branch_other, seed, mod)
    far = swap(far, "narrow", 2)

    def as_output(near, far):
        first = jnp.where(pair == 0, near, far)
        second = jnp.where(pair == 0, far, near)
        return jnp.stack([first, second]).reshape(tokens.shape)

    block_out = as_output(near, far)
    d_middle, sums_two, attn_bundle, attn_kg, d_first = attend_back(
        sc, d_normed, d_normed_other, middle, attended, seed, mod, mixed, out_weight,
        normed_one, qkv, conv, prob, qkv_weight, attn_k
    )
    d_first_other = swap(other_half(d_first), "narrow", 1)
    near, far, sums_one = input_grad(sc, d_first, d_first_other, d_middle, base, mod)
    tokens_grad = as_output(near, swap(far, "narrow", 2))

    cond = jnp.concatenate(
        [sums_one, sums_two[2:3], sums_two[1:2], d_gate_two, sums_two[0:1]], axis=0
    )
    moves = jnp.where(stays, 0.0, cond)
    cond = jnp.where(stays, cond, 0.0) + lax.ppermute(
        moves, "wide", [(i, i + 1) for i in range(wide_count - 1)]
    )
    cond = sum_all(cond, [("narrow", 1), ("narrow", 2)])

    chips = [("wide", bit) for bit in bits_of(wide_count)] + [("narrow", 2)]
    order = [("narrow", 2)] + [("wide", bit) for bit in bits_of(wide_count)]

    def reduce(block):
        half = gather(scatter_sum(block, order), order)
        other = swap(half, "narrow", 1)
        return jnp.where(core == 0, half, other), jnp.where(core == 0, other, half)

    down_a0, down_a1 = reduce(down_a)
    up_a0, up_a1 = reduce(up_a)
    down_b0, down_b1 = reduce(down_b)
    up_b0, up_b1 = reduce(up_b)
    attn0, attn1 = reduce(attn_bundle)
    down_grad = jnp.concatenate([down_a0, down_b0, down_a1, down_b1], axis=0).astype(F32)
    up_grad = jnp.concatenate([up_a0, up_b0, up_a1, up_b1], axis=1).astype(F32)
    qkv_grad = jnp.concatenate(
        [v[:, 384 * s : 384 * s + 384] for s in range(3) for v in (attn0, attn1)], axis=1
    ).astype(F32)
    out_grad = jnp.concatenate(
        [
            jnp.concatenate([v[0:384, 1152:], v[384:768, 1152:]], axis=1)
            for v in (attn0, attn1)
        ],
        axis=0,
    ).astype(F32)

    def kernel_grads(values):
        half = sum_all(values, chips)
        other = swap(half, "narrow", 1)
        return jnp.where(core == 0, half, other), jnp.where(core == 0, other, half)

    ffn0, ffn1 = kernel_grads(jnp.concatenate([ffn_a, ffn_b], axis=1))
    ffn_grad = jnp.concatenate([ffn0, ffn1], axis=1).reshape(ffn_kernel.shape)
    attn_kg = attn_kg.reshape(3, 9, 3, 128).transpose(1, 2, 0, 3).reshape(9, 3, 384)
    kg0, kg1 = kernel_grads(attn_kg)
    attn_grad = jnp.concatenate([kg0, kg1], axis=2).reshape(attn_kernel.shape)

    return (
        block_out, tokens_grad, cond[0:5].reshape(1, -1), cond[5:6],
        qkv_grad, attn_grad, out_grad, up_grad, ffn_grad, down_grad,
    )


def solution(mesh):
    rows = P("wide", "narrow", None, None)
    in_specs = (rows, rows, P("wide", None)) + (P(),) * 8
    out_specs = (rows, rows, P("wide", None), P("wide", None)) + (P(),) * 6
    return jax.shard_map(
        on_device, mesh=mesh, in_specs=in_specs, out_specs=out_specs, check_vma=False
    )
```

```python
import functools

import jax
import jax.numpy as jnp
from jax import lax
from jax.experimental import pallas as pl
from jax.experimental.pallas import tpu as pltpu
from jax.sharding import PartitionSpec as P

HEAD_DIM = 64
LANES = 128
GROUPS = 4
MARGIN = 16

masked_score = -1000000000.0
norm_epsilon = 1e-06
gelu_root = 0.7978845608028654
gelu_cube = 0.044715

BF = jnp.bfloat16
F32 = jnp.float32
VMEM_LIMIT = 60 * 1024 * 1024


def dot(left, right, left_dim=1, right_dim=0):
    return lax.dot_general(
        left, right, (((left_dim,), (right_dim,)), ((), ())), preferred_element_type=F32
    )


ANYWHERE = pl.BlockSpec(memory_space=pl.ANY)


def full(*shape):
    return pl.BlockSpec(shape, lambda i, s: (0,) * len(shape))


def iota(shape, dim):
    return lax.broadcasted_iota(jnp.int32, shape, dim)


def phase_rows(rows, start):
    return start + iota((rows, 1), 0)


def live_rows(token, height, breadth):
    row = 2 * ((token >> 4) & 15) + (token >> 9)
    col = 2 * (token & 15) + ((token >> 8) & 1)
    return ((row < height) & (col < breadth)).astype(F32)


def to_phase_matrix():
    row = iota((256, 256), 0)
    col = iota((256, 256), 1)
    grid_row = 2 * ((row >> 4) & 3) + (row >> 7)
    grid_col = 2 * (row & 15) + ((row >> 6) & 1)
    return (col == grid_row * 32 + grid_col).astype(F32).astype(BF)


def normal(values):
    center = values - jnp.mean(values, axis=-1, keepdims=True)
    scale = lax.rsqrt(jnp.mean(center * center, axis=-1, keepdims=True) + norm_epsilon)
    return center * scale, scale


def col_sum(values):
    return jnp.sum(values, axis=0, keepdims=True)


def clear_margins(held):
    zero = jnp.zeros((2 * GROUPS, MARGIN, LANES), F32)
    held[:, 0:MARGIN, :] = zero
    held[:, MARGIN + 256 : 2 * MARGIN + 256, :] = zero


def hold(held, group_of):
    place = iota((256, LANES), 0) & 15
    for g in range(GROUPS):
        values = group_of(g)
        held[2 * g, MARGIN : MARGIN + 256, :] = values
        if g % 2:
            moved = jnp.where(place == 0, 0.0, pltpu.roll(values, 1, 0))
        else:
            moved = jnp.where(place == 15, 0.0, pltpu.roll(values, 255, 0))
        held[2 * g + 1, MARGIN : MARGIN + 256, :] = moved


def taps(g):
    alpha, beta = g // 2, g % 2
    out = []
    for a in range(3):
        for b in range(3):
            row = alpha + a - 1
            col = beta + b - 1
            src = 2 * (row % 2) + col % 2
            out.append((a, b, 2 * src + (0 if 0 <= col <= 1 else 1), MARGIN * (row // 2)))
    return out


STEP = 64


def convolve(held, kernel, write, flip=False):
    weights = [[kernel[3 * a + b : 3 * a + b + 1, :] for b in range(3)] for a in range(3)]

    def at(i, carry):
        start = pl.multiple_of(i * STEP, STEP)
        for g in range(GROUPS):
            total = None
            for a, b, src, off in taps(g):
                weight = weights[2 - a][2 - b] if flip else weights[a][b]
                part = weight * held[src, pl.ds(MARGIN + off + start, STEP), :]
                total = part if total is None else total + part
            write(g, start, total)
        return carry

    lax.fori_loop(0, 256 // STEP, at, 0)


def convolve_back(held, kernel, source, write):
    weights = [[kernel[3 * a + b : 3 * a + b + 1, :] for b in range(3)] for a in range(3)]

    def at(i, sums):
        start = pl.multiple_of(i * STEP, STEP)
        sums = list(sums)
        for g in range(GROUPS):
            total = None
            given = source(g, start)
            for a, b, src, off in taps(g):
                window = held[src, pl.ds(MARGIN + off + start, STEP), :]
                part = weights[2 - a][2 - b] * window
                total = part if total is None else total + part
                at_tap = 3 * (2 - a) + 2 - b
                prod = given * window
                sums[at_tap] = sums[at_tap] + jnp.sum(prod.reshape(STEP // 8, 8, LANES), axis=0)
            write(g, start, total)
        return tuple(sums)

    zero = jnp.zeros((8, LANES), F32)
    sums = lax.fori_loop(0, 256 // STEP, at, (zero,) * 9)
    return jnp.concatenate([col_sum(s) for s in sums], axis=0)


def attend_kernel(
    sc, p0, p1, p2, p3, mod, wq, wk, wv, kq, kk, kv,
    base_out, normed_out, qkv_out, conv_out, prob_out, mixed_out,
    held,
):
    step = pl.program_id(0)
    height, breadth = sc[0], sc[1]

    @pl.when(step == 0)
    def _():
        clear_margins(held)
        shift, scale = mod[0:1, :], 1.0 + mod[1:2, :]
        matrix = to_phase_matrix()
        for k, piece in enumerate((p0, p1, p2, p3)):
            at = sc[2 + k]
            moved = dot(matrix, piece[...])
            for g in range(GROUPS):
                start = pl.multiple_of(g * 256 + at * 64, 64)
                values = moved[g * 64 : g * 64 + 64, :] * live_rows(phase_rows(64, start), height, breadth)
                base_out[pl.ds(start, 64), :] = values.astype(BF)
                normed_out[pl.ds(start, 64), :] = (normal(values)[0] * scale + shift).astype(BF)

    weight = jnp.concatenate([wq[...], wk[...], wv[...]], axis=1)
    for r in range(0, 1024, 512):
        qkv_out[0, r : r + 512, :] = dot(normed_out[r : r + 512, :], weight).astype(BF)
    for s, kernel in enumerate((kq, kk, kv)):
        cols = slice(s * LANES, (s + 1) * LANES)
        hold(held, lambda g: qkv_out[0, g * 256 : g * 256 + 256, cols].astype(F32))

        def write(g, start, total):
            conv_out[0, pl.ds(g * 256 + start, STEP), cols] = total.astype(BF)

        convolve(held, kernel[...].astype(F32), write)

    token = iota((1, 256), 1)
    lane = iota((256, LANES), 1)

    def group(g, carry):
        start = pl.multiple_of(g * 256, 256)
        rows = pl.ds(start, 256)
        live = live_rows(token + start, height, breadth) > 0.5
        query = conv_out[0, rows, 0:LANES] * BF(HEAD_DIM**-0.5)
        key = conv_out[0, rows, LANES : 2 * LANES]
        value = conv_out[0, rows, 2 * LANES : 3 * LANES]
        parts = []
        for h in range(2):
            mine = (lane < HEAD_DIM) if h == 0 else (lane >= HEAD_DIM)
            score = dot(jnp.where(mine, query, BF(0)), key, 1, 1)
            score = jnp.where(live, score, masked_score)
            top = jnp.max(score, axis=-1, keepdims=True)
            raised = jnp.exp(score - top)
            prob = (raised * (1.0 / jnp.sum(raised, axis=-1, keepdims=True))).astype(BF)
            prob_out[0, g, h] = prob
            parts.append(dot(prob, value))
        mixed_out[rows, :] = jnp.where(lane < HEAD_DIM, parts[0], parts[1]).astype(BF)
        return carry

    lax.fori_loop(0, GROUPS, group, 0)


def attend(sc, pieces, mod, qkv_weight, attn_kernel):
    def piece_spec():
        return pl.BlockSpec((256, 768), lambda i, s: (0, 0))

    def weight_spec(k):
        return pl.BlockSpec((768, LANES), lambda i, s: (0, 6 * k + 3 * s[6] + i))

    def kernel_spec(k):
        return pl.BlockSpec((9, LANES), lambda i, s: (0, 6 * k + 3 * s[6] + i))

    whole = pl.BlockSpec((1024, 768), lambda i, s: (0, 0))
    return pl.pallas_call(
        attend_kernel,
        grid_spec=pltpu.PrefetchScalarGridSpec(
            num_scalar_prefetch=1,
            grid=(3,),
            in_specs=[piece_spec() for _ in range(4)]
            + [pl.BlockSpec((8, 768), lambda i, s: (0, 0))]
            + [weight_spec(k) for k in range(3)]
            + [kernel_spec(k) for k in range(3)],
            out_specs=[
                whole,
                whole,
                pl.BlockSpec((1, 1024, 384), lambda i, s: (i, 0, 0)),
                pl.BlockSpec((1, 1024, 384), lambda i, s: (i, 0, 0)),
                pl.BlockSpec((1, GROUPS, 2, 256, 256), lambda i, s: (i, 0, 0, 0, 0)),
                pl.BlockSpec((1024, LANES), lambda i, s: (0, i)),
            ],
            scratch_shapes=[pltpu.VMEM((2 * GROUPS, 2 * MARGIN + 256, LANES), F32)],
        ),
        out_shape=[
            jax.ShapeDtypeStruct((1024, 768), BF),
            jax.ShapeDtypeStruct((1024, 768), BF),
            jax.ShapeDtypeStruct((3, 1024, 384), BF),
            jax.ShapeDtypeStruct((3, 1024, 384), BF),
            jax.ShapeDtypeStruct((3, GROUPS, 2, 256, 256), BF),
            jax.ShapeDtypeStruct((1024, 384), BF),
        ],
        compiler_params=pltpu.CompilerParams(vmem_limit_bytes=VMEM_LIMIT),
        cost_estimate=pl.CostEstimate(flops=3_000_000_000, bytes_accessed=20_000_000, transcendentals=1600000),
        name="attend",
    )(sc, *pieces, mod, qkv_weight, qkv_weight, qkv_weight, attn_kernel, attn_kernel, attn_kernel)


def middle_kernel(
    sc, mixed_own, mixed_other, base, out_weight, mod, c0, c1, c2, c3,
    attended_out, middle_out, normed_out, branch_grad_out, seed_out,
    mixed, attended,
):
    height, breadth, core = sc[0], sc[1], sc[6]
    mixed[:, pl.ds(pl.multiple_of(core * 384, LANES), 384)] = mixed_own[...]
    mixed[:, pl.ds(pl.multiple_of((1 - core) * 384, LANES), 384)] = mixed_other[...]
    for r in range(0, 1024, 512):
        attended[r : r + 512, :] = dot(mixed[r : r + 512, :], out_weight[...])
    gate = mod[2:3, :]
    shift, scale = mod[3:4, :], 1.0 + mod[4:5, :]

    def at(i, carry):
        rows = pl.ds(pl.multiple_of(i * 64, 64), 64)
        got = attended[rows, :]
        attended_out[rows, :] = got.astype(BF)
        middle = base[rows, :].astype(F32) + gate * got
        middle_out[rows, :] = middle
        normed_out[rows, :] = (normal(middle)[0] * scale + shift).astype(BF)
        return carry

    lax.fori_loop(0, 16, at, 0)
    matrix = to_phase_matrix()
    gate_two, factor = mod[5:6, :], mod[6:7, :]
    for k, piece in enumerate((c0, c1, c2, c3)):
        at = sc[2 + k]
        moved = dot(matrix, piece[...])
        for g in range(GROUPS):
            start = pl.multiple_of(g * 256 + at * 64, 64)
            values = moved[g * 64 : g * 64 + 64, :] * live_rows(phase_rows(64, start), height, breadth)
            seed_out[pl.ds(start, 64), :] = values.astype(BF)
            branch_grad_out[pl.ds(start, 64), :] = (values * factor * gate_two).astype(BF)


def project_out(sc, mixed_own, mixed_other, base, out_weight, mod, pieces):
    tokens = full(1024, 768)
    return pl.pallas_call(
        middle_kernel,
        grid_spec=pltpu.PrefetchScalarGridSpec(
            num_scalar_prefetch=1,
            grid=(1,),
            in_specs=[full(1024, 384), full(1024, 384), tokens, full(768, 768), full(8, 768)]
            + [full(256, 768)] * 4,
            out_specs=[tokens] * 5,
            scratch_shapes=[pltpu.VMEM((1024, 768), BF), pltpu.VMEM((1024, 768), F32)],
        ),
        out_shape=[
            jax.ShapeDtypeStruct((1024, 768), BF),
            jax.ShapeDtypeStruct((1024, 768), F32),
            jax.ShapeDtypeStruct((1024, 768), BF),
            jax.ShapeDtypeStruct((1024, 768), BF),
            jax.ShapeDtypeStruct((1024, 768), BF),
        ],
        compiler_params=pltpu.CompilerParams(vmem_limit_bytes=VMEM_LIMIT),
        cost_estimate=pl.CostEstimate(flops=2_000_000_000, bytes_accessed=20_000_000, transcendentals=0),
        name="project_out",
    )(sc, mixed_own, mixed_other, base, out_weight, mod, *pieces)


BLOCK = 384


def split_halves(core, g, values, keep, send):
    for local in range(2):
        low = values[128 * local : 128 * local + 64, :]
        high = values[128 * local + 64 : 128 * local + 128, :]
        keep[2 * g + local] = jnp.where(core == 0, low, high)
        send[2 * g + local] = jnp.where(core == 0, high, low).astype(BF)


def feed_kernel(count, first, sc, normed, branch_grad, up, down, kernel, *rest):
    rest = rest[count:]
    if first:
        (up_keep, up_send, down_keep, down_send, kernel_grad, branch_out, normed_grad_out,
         held, normed_t, hid, d_act, acts, d_conv, d_hids) = rest
    else:
        (branch_in, normed_grad_in, up_keep, up_send, down_keep, down_send, kernel_grad,
         branch_keep, branch_send, normed_grad_out, normed_grad_send,
         held, normed_t, hid, d_act, acts, d_conv, d_hids) = rest
    step = pl.program_id(0)

    @pl.when(step == 0)
    def _():
        clear_margins(held)
        for r in range(0, 1024, 256):
            normed_t[:, r : r + 256] = normed[r : r + 256, :].T

    block = pl.ds(pl.multiple_of(step * BLOCK, BLOCK), BLOCK)
    for r in range(0, 1024, 512):
        hid[r : r + 512, :] = dot(normed[r : r + 512, :], up[:, block]).astype(BF)
        d_act[r : r + 512, :] = dot(branch_grad[r : r + 512, :], down[block, :], 1, 1)
    for lane_block in range(BLOCK // LANES):
        cols = slice(lane_block * LANES, (lane_block + 1) * LANES)
        dest = pl.ds(pl.multiple_of(step * BLOCK + lane_block * LANES, LANES), LANES)
        weights = kernel[:, cols].astype(F32)
        hold(held, lambda g: hid[g * 256 : g * 256 + 256, cols].astype(F32))

        def activate(g, start, v):
            rows = pl.ds(g * 256 + start, STEP)
            square = v * v
            bent = jnp.tanh(gelu_root * v * (1.0 + gelu_cube * square))
            half = 0.5 + 0.5 * bent
            acts[rows, dest] = (v * half).astype(BF)
            slope = half + 0.5 * v * (1.0 - bent * bent) * (gelu_root + 3.0 * gelu_root * gelu_cube * square)
            d_conv[rows, :] = (d_act[rows, cols] * slope).astype(BF)

        convolve(held, weights, activate)
        hold(held, lambda g: d_conv[g * 256 : g * 256 + 256, :].astype(F32))

        def source(g, start):
            return hid[pl.ds(g * 256 + start, STEP), cols].astype(F32)

        def write(g, start, total):
            d_hids[pl.ds(g * 256 + start, STEP), dest] = total.astype(BF)

        kernel_grad[:, cols] = convolve_back(held, weights, source, write)
    grad = dot(acts[:, block].T, branch_grad[...]).astype(BF)

    @pl.when(step == sc[8])
    def _():
        down_keep[...] = grad

    @pl.when(step != sc[8])
    def _():
        down_send[...] = grad

    @pl.when(step == pl.num_programs(0) - 1)
    def _():
        for pair, out in ((sc[7], up_keep), (1 - sc[7], up_send)):
            rows = pl.ds(pl.multiple_of(pair * 384, 384), 384)
            out[...] = dot(normed_t[rows, :], d_hids[...]).astype(BF)
        for r in range(0, 1024, 256):
            rows = slice(r, r + 256)
            branch = dot(acts[rows, :], down[...])
            normed_grad = dot(d_hids[rows, :], up[...], 1, 1)
            if first:
                branch_out[rows, :] = branch
                normed_grad_out[rows, :] = normed_grad
            else:
                split_halves(sc[6], r // 256, branch + branch_in[rows, :], branch_keep, branch_send)
                normed_grad = normed_grad + normed_grad_in[rows, :]
                normed_grad_out[rows, :] = normed_grad
                normed_grad_send[rows, :] = normed_grad.astype(BF)


def feed(sc, normed, branch_grad, up_weight, down_weight, ffn_kernel, half, before, deps=()):
    tokens = full(1024, 768)
    first = before is None
    piece = jax.ShapeDtypeStruct((384, 768), BF)
    return pl.pallas_call(
        functools.partial(feed_kernel, len(deps), first),
        grid_spec=pltpu.PrefetchScalarGridSpec(
            num_scalar_prefetch=1,
            grid=(2,),
            in_specs=[
                tokens,
                tokens,
                pl.BlockSpec((768, 768), lambda i, s: (0, 2 * s[6] + half)),
                pl.BlockSpec((768, 768), lambda i, s: (2 * s[6] + half, 0)),
                pl.BlockSpec((9, BLOCK), lambda i, s: (0, 4 * s[6] + 2 * half + i)),
            ]
            + [ANYWHERE] * len(deps)
            + ([] if first else [tokens, tokens]),
            out_specs=[full(384, 768)] * 4
            + [pl.BlockSpec((9, BLOCK), lambda i, s: (0, i))]
            + ([tokens, tokens] if first else [full(8, 64, 768), full(8, 64, 768), tokens, tokens]),
            scratch_shapes=[
                pltpu.VMEM((2 * GROUPS, 2 * MARGIN + 256, LANES), F32),
                pltpu.VMEM((768, 1024), BF),
                pltpu.VMEM((1024, BLOCK), BF),
                pltpu.VMEM((1024, BLOCK), F32),
                pltpu.VMEM((1024, 768), BF),
                pltpu.VMEM((1024, LANES), BF),
                pltpu.VMEM((1024, 768), BF),
            ],
        ),
        out_shape=[piece] * 4
        + [jax.ShapeDtypeStruct((9, 768), F32)]
        + (
            []
            if first
            else [jax.ShapeDtypeStruct((8, 64, 768), F32), jax.ShapeDtypeStruct((8, 64, 768), BF)]
        )
        + [
            jax.ShapeDtypeStruct((1024, 768), F32),
            jax.ShapeDtypeStruct((1024, 768), F32 if first else BF),
        ],
        compiler_params=pltpu.CompilerParams(vmem_limit_bytes=VMEM_LIMIT),
        cost_estimate=pl.CostEstimate(flops=15_000_000_000, bytes_accessed=60_000_000, transcendentals=800000),
        name="feed",
    )(sc, normed, branch_grad, up_weight, down_weight, ffn_kernel, *deps, *([] if first else before))


def finish_kernel(count, sc, middle, branch, branch_other, seed, mod, *rest):
    near_out, far_out, sums_out = rest[count:]
    height, breadth, core = sc[0], sc[1], sc[6]
    gate, factor = mod[5:6, :], mod[6:7, :]
    matrix = to_phase_matrix()
    total = jnp.zeros((1, 768), F32)
    for local in range(2):
        parts = []
        for g in range(GROUPS):
            token = phase_rows(64, g * 256 + (2 * local + core) * 64)
            whole = branch[2 * g + local] + branch_other[2 * g + local].astype(F32)
            total = total + col_sum(seed[2 * g + local, 0].astype(F32) * whole)
            result = middle[2 * g + local, 0] + gate * whole
            parts.append((result * live_rows(token, height, breadth)).astype(BF))
        done = dot(matrix, jnp.concatenate(parts, axis=0), 0, 0).astype(BF)

        @pl.when(sc[7] == local)
        def _():
            near_out[...] = done

        @pl.when(sc[7] != local)
        def _():
            far_out[...] = done

    sums_out[...] = total * factor


def half_spec():
    return pl.BlockSpec((8, 1, 64, 768), lambda i, s: (0, s[6], 0, 0))


def finish(sc, middle, branch, branch_other, seed, mod, deps=()):
    halves = lambda v: v.reshape(8, 2, 64, 768)
    return pl.pallas_call(
        functools.partial(finish_kernel, len(deps)),
        grid_spec=pltpu.PrefetchScalarGridSpec(
            num_scalar_prefetch=1,
            grid=(1,),
            in_specs=[half_spec(), full(8, 64, 768), full(8, 64, 768), half_spec(), full(8, 768)]
            + [ANYWHERE] * len(deps),
            out_specs=[full(256, 768), full(256, 768), full(1, 768)],
        ),
        out_shape=[
            jax.ShapeDtypeStruct((256, 768), BF),
            jax.ShapeDtypeStruct((256, 768), BF),
            jax.ShapeDtypeStruct((1, 768), F32),
        ],
        compiler_params=pltpu.CompilerParams(vmem_limit_bytes=VMEM_LIMIT),
        cost_estimate=pl.CostEstimate(flops=300_000_000, bytes_accessed=6_000_000, transcendentals=0),
        name="finish",
    )(sc, halves(middle), branch, branch_other, halves(seed), mod, *deps)


def norm_back_kernel(
    count, sc, normed_grad, normed_grad_other, middle, attended, seed, mod, mixed, *rest,
):
    middle_grad, att_grad, sums_out, out_keep, out_send = rest[count:]
    gate, scale, factor = mod[2:3, :], 1.0 + mod[4:5, :], mod[6:7, :]

    def at(i, sums):
        d_shift, d_scale, d_gate = sums
        rows = pl.ds(pl.multiple_of(i * 64, 64), 64)
        grad = normed_grad[rows, :] + normed_grad_other[rows, :].astype(F32)
        unit, inverse = normal(middle[rows, :])
        both = grad * unit
        d_shift = d_shift + col_sum(grad)
        d_scale = d_scale + col_sum(both)
        grad = grad * scale
        mean = jnp.mean(grad, axis=-1, keepdims=True)
        along = jnp.mean(both * scale, axis=-1, keepdims=True)
        total = seed[rows, :].astype(F32) * factor + inverse * (grad - mean - unit * along)
        middle_grad[rows, :] = total
        d_gate = d_gate + col_sum(total * attended[rows, :].astype(F32))
        att_grad[rows, :] = (total * gate).astype(BF)
        return d_shift, d_scale, d_gate

    zero = jnp.zeros((1, 768), F32)
    sums = lax.fori_loop(0, 16, at, (zero, zero, zero))
    for k in range(3):
        sums_out[k : k + 1, :] = 0.5 * sums[k]
    mixed_t = mixed[...].T
    for at_y, out in ((sc[8], out_keep), (1 - sc[8], out_send)):
        cols = pl.ds(pl.multiple_of(at_y * 384, 384), 384)
        out[...] = dot(mixed_t, att_grad[:, cols]).astype(BF)


def norm_back(sc, normed_grad, normed_grad_other, middle, attended, seed, mod, mixed, deps=()):
    tokens = full(1024, 768)
    return pl.pallas_call(
        functools.partial(norm_back_kernel, len(deps)),
        grid_spec=pltpu.PrefetchScalarGridSpec(
            num_scalar_prefetch=1,
            grid=(1,),
            in_specs=[tokens] * 5 + [full(8, 768), full(1024, 384)] + [ANYWHERE] * len(deps),
            out_specs=[tokens, tokens, full(3, 768), full(384, 384), full(384, 384)],
        ),
        out_shape=[
            jax.ShapeDtypeStruct((1024, 768), F32),
            jax.ShapeDtypeStruct((1024, 768), BF),
            jax.ShapeDtypeStruct((3, 768), F32),
            jax.ShapeDtypeStruct((384, 384), BF),
            jax.ShapeDtypeStruct((384, 384), BF),
        ],
        compiler_params=pltpu.CompilerParams(vmem_limit_bytes=VMEM_LIMIT),
        cost_estimate=pl.CostEstimate(flops=4_000_000_000, bytes_accessed=30_000_000, transcendentals=0),
        name="norm_back",
    )(sc, normed_grad, normed_grad_other, middle, attended, seed, mod, mixed, *deps)


def attend_back_kernel(
    count, axis, sc, att_grad, out_weight, normed, qkv, conv, prob, kq, kk, kv, *rest,
):
    (qkv_grad, kernel_grad, weight_keep, weight_send, held, normed_t, d_mixed, d_conv) = rest[count:]
    clear_margins(held)
    for r in range(0, 1024, 256):
        normed_t[:, r : r + 256] = normed[r : r + 256, :].T
    for r in range(0, 1024, 512):
        d_mixed[r : r + 512, :] = dot(att_grad[r : r + 512, :], out_weight[...], 1, 1).astype(BF)

    lane = iota((256, LANES), 1)

    def group(g, carry):
        rows = pl.ds(pl.multiple_of(g * 256, 256), 256)
        grad = d_mixed[rows, :]
        query = conv[0, rows, 0:LANES]
        key = conv[0, rows, LANES : 2 * LANES]
        value = conv[0, rows, 2 * LANES : 3 * LANES]
        parts = []
        for h in range(2):
            mine = (lane < HEAD_DIM) if h == 0 else (lane >= HEAD_DIM)
            p = prob[0, g, h]
            d_value = dot(p.T, grad)
            d_prob = dot(jnp.where(mine, grad, BF(0)), value, 1, 1)
            wide_p = p.astype(F32)
            inner = jnp.sum(d_prob * wide_p, axis=-1, keepdims=True)
            d_score = (wide_p * (d_prob - inner)).astype(BF)
            parts.append((dot(d_score, key), dot(d_score.T, query), d_value))
        low = lane < HEAD_DIM
        for k in range(3):
            picked = jnp.where(low, parts[0][k], parts[1][k])
            if k < 2:
                picked = picked * HEAD_DIM**-0.5
            d_conv[rows, k * LANES : (k + 1) * LANES] = picked.astype(BF)
        return carry

    lax.fori_loop(0, GROUPS, group, 0)
    for s, kernel in enumerate((kq, kk, kv)):
        cols = slice(s * LANES, (s + 1) * LANES)
        hold(held, lambda g: d_conv[g * 256 : g * 256 + 256, cols].astype(F32))

        def source(g, start):
            return qkv[0, pl.ds(g * 256 + start, STEP), cols].astype(F32)

        def write(g, start, total):
            qkv_grad[pl.ds(g * 256 + start, STEP), cols] = total.astype(BF)

        kernel_grad[:, cols] = convolve_back(held, kernel[...].astype(F32), source, write)
    for place, out in ((sc[axis], weight_keep), (1 - sc[axis], weight_send)):
        rows = pl.ds(pl.multiple_of(place * 384, 384), 384)
        out[...] = dot(normed_t[rows, :], qkv_grad[...]).astype(BF)


def attend_back(sc, heads, axis, att_grad, out_weight, normed, qkv, conv, prob, attn_kernel, deps=()):
    tokens = full(1024, 768)

    def kernel_spec(k):
        return pl.BlockSpec((9, LANES), lambda i, s: (0, 6 * k + 3 * s[6] + heads))

    saved = pl.BlockSpec((1, 1024, 384), lambda i, s: (heads, 0, 0))
    return pl.pallas_call(
        functools.partial(attend_back_kernel, len(deps), axis),
        grid_spec=pltpu.PrefetchScalarGridSpec(
            num_scalar_prefetch=1,
            grid=(1,),
            in_specs=[tokens, pl.BlockSpec((LANES, 768), lambda i, s: (3 * s[6] + heads, 0)),
                      tokens, saved, saved,
                      pl.BlockSpec((1, GROUPS, 2, 256, 256), lambda i, s: (heads, 0, 0, 0, 0))]
            + [kernel_spec(k) for k in range(3)]
            + [ANYWHERE] * len(deps),
            out_specs=[full(1024, 384), full(9, 384), full(384, 384), full(384, 384)],
            scratch_shapes=[
                pltpu.VMEM((2 * GROUPS, 2 * MARGIN + 256, LANES), F32),
                pltpu.VMEM((768, 1024), BF),
                pltpu.VMEM((1024, LANES), BF),
                pltpu.VMEM((1024, 384), BF),
            ],
        ),
        out_shape=[
            jax.ShapeDtypeStruct((1024, 384), BF),
            jax.ShapeDtypeStruct((9, 384), F32),
            jax.ShapeDtypeStruct((384, 384), BF),
            jax.ShapeDtypeStruct((384, 384), BF),
        ],
        compiler_params=pltpu.CompilerParams(vmem_limit_bytes=VMEM_LIMIT),
        cost_estimate=pl.CostEstimate(flops=6_000_000_000, bytes_accessed=30_000_000, transcendentals=0),
        name="attend_back",
    )(sc, att_grad, out_weight, normed, qkv, conv, prob, attn_kernel, attn_kernel, attn_kernel, *deps)


def first_back_kernel(count, sc, g0, g1, g2, *rest):
    weights = rest[0:9]
    keep, send, grads, weight = rest[9 + count :]
    core = sc[6]
    for k, grad in enumerate((g0, g1, g2)):
        grads[:, 384 * k : 384 * k + 384] = grad[...]
        for s in range(3):
            at = 384 * k + LANES * s
            weight[:, at : at + LANES] = weights[3 * k + s][...]
    for r in range(0, 1024, 256):
        split_halves(core, r // 256, dot(grads[r : r + 256, :], weight[...], 1, 1), keep, send)


def first_back(sc, grads, qkv_weight, deps=()):
    def weight_spec(heads, k):
        return pl.BlockSpec((768, LANES), lambda i, s: (0, 6 * k + 3 * s[6] + heads))

    return pl.pallas_call(
        functools.partial(first_back_kernel, len(deps)),
        grid_spec=pltpu.PrefetchScalarGridSpec(
            num_scalar_prefetch=1,
            grid=(1,),
            in_specs=[full(1024, 384)] * 3
            + [weight_spec(heads, k) for heads in range(3) for k in range(3)]
            + [ANYWHERE] * len(deps),
            out_specs=[full(8, 64, 768)] * 2,
            scratch_shapes=[pltpu.VMEM((1024, 1152), BF), pltpu.VMEM((768, 1152), BF)],
        ),
        out_shape=[jax.ShapeDtypeStruct((8, 64, 768), F32), jax.ShapeDtypeStruct((8, 64, 768), BF)],
        compiler_params=pltpu.CompilerParams(vmem_limit_bytes=VMEM_LIMIT),
        cost_estimate=pl.CostEstimate(flops=2_000_000_000, bytes_accessed=10_000_000, transcendentals=0),
        name="first_back",
    )(sc, *grads, *([qkv_weight] * 9), *deps)


def input_kernel(count, sc, grad, grad_other, middle_grad, base, mod, *rest):
    near_out, far_out, sums_out = rest[count:]
    height, breadth, core = sc[0], sc[1], sc[6]
    scale = 1.0 + mod[1:2, :]
    matrix = to_phase_matrix()
    d_shift = jnp.zeros((1, 768), F32)
    d_scale = jnp.zeros((1, 768), F32)
    for local in range(2):
        parts = []
        for g in range(GROUPS):
            at = 2 * g + local
            token = phase_rows(64, g * 256 + (2 * local + core) * 64)
            total = grad[at] + grad_other[at].astype(F32)
            unit, inverse = normal(base[at, 0].astype(F32))
            both = total * unit
            d_shift = d_shift + col_sum(total)
            d_scale = d_scale + col_sum(both)
            total = total * scale
            mean = jnp.mean(total, axis=-1, keepdims=True)
            along = jnp.mean(both * scale, axis=-1, keepdims=True)
            total = middle_grad[at, 0] + inverse * (total - mean - unit * along)
            parts.append((total * live_rows(token, height, breadth)).astype(BF))
        done = dot(matrix, jnp.concatenate(parts, axis=0), 0, 0).astype(BF)

        @pl.when(sc[7] == local)
        def _():
            near_out[...] = done

        @pl.when(sc[7] != local)
        def _():
            far_out[...] = done

    sums_out[0:1, :] = d_shift
    sums_out[1:2, :] = d_scale


def input_grad(sc, grad, grad_other, middle_grad, base, mod, deps=()):
    halves = lambda v: v.reshape(8, 2, 64, 768)
    return pl.pallas_call(
        functools.partial(input_kernel, len(deps)),
        grid_spec=pltpu.PrefetchScalarGridSpec(
            num_scalar_prefetch=1,
            grid=(1,),
            in_specs=[full(8, 64, 768), full(8, 64, 768), half_spec(), half_spec(), full(8, 768)]
            + [ANYWHERE] * len(deps),
            out_specs=[full(256, 768), full(256, 768), full(2, 768)],
        ),
        out_shape=[
            jax.ShapeDtypeStruct((256, 768), BF),
            jax.ShapeDtypeStruct((256, 768), BF),
            jax.ShapeDtypeStruct((2, 768), F32),
        ],
        compiler_params=pltpu.CompilerParams(vmem_limit_bytes=VMEM_LIMIT),
        cost_estimate=pl.CostEstimate(flops=300_000_000, bytes_accessed=6_000_000, transcendentals=0),
        name="input_grad",
    )(sc, grad, grad_other, halves(middle_grad), halves(base), mod, *deps)


def swap(values, axis, bit):
    count = lax.axis_size(axis)
    return lax.ppermute(values, axis, [(i, i ^ bit) for i in range(count)])


def bits_of(count):
    return [1 << k for k in range(count.bit_length() - 1)]


def halve_kernel(parts, count, sc, *rest):
    inputs, (keep1, send1, keep2, send2) = rest[: 4 * parts], rest[4 * parts + count :]
    half = keep1.shape[0]
    for part in range(parts):
        k1, r1, k2, r2 = inputs[4 * part : 4 * part + 4]
        width = k1.shape[1]
        cols = slice(part * width, (part + 1) * width)
        for kept, got, keep, send, bit in ((k1, r1, keep1, send1, sc[8]), (k2, r2, keep2, send2, sc[7])):
            for place, out in ((bit, keep), (1 - bit, send)):
                rows = pl.ds(pl.multiple_of(place * half, 16), half)
                out[:, cols] = (kept[rows, :].astype(F32) + got[rows, :].astype(F32)).astype(BF)


def quarter_kernel(count, sc, k1, r1, k2, r2, *rest):
    outs = rest[count:]
    width = k1.shape[1]
    for d, out in enumerate(outs):
        rows = pl.ds(pl.multiple_of((sc[9] ^ d) * 48, 16), 48)
        out[:, 0:width] = (k1[rows, :].astype(F32) + r1[rows, :].astype(F32)).astype(BF)
        out[:, width : 2 * width] = (k2[rows, :].astype(F32) + r2[rows, :].astype(F32)).astype(BF)


def total_kernel(count, sc, a, b, c, d, *rest):
    rest[count][...] = (
        (a[...].astype(F32) + b[...].astype(F32)) + (c[...].astype(F32) + d[...].astype(F32))
    ).astype(BF)


def glue(kernel, name, sc, operands, shapes, deps):
    return pl.pallas_call(
        functools.partial(kernel, len(deps)),
        grid_spec=pltpu.PrefetchScalarGridSpec(
            num_scalar_prefetch=1,
            grid=(1,),
            in_specs=[full(*v.shape) for v in operands] + [ANYWHERE] * len(deps),
            out_specs=[full(*shape) for shape in shapes],
        ),
        out_shape=[jax.ShapeDtypeStruct(shape, BF) for shape in shapes],
        cost_estimate=pl.CostEstimate(flops=1_000_000, bytes_accessed=4_000_000, transcendentals=0),
        compiler_params=pltpu.CompilerParams(vmem_limit_bytes=VMEM_LIMIT),
        name=name,
    )(sc, *operands, *deps)


def begin(keep1, send1, keep2, send2):
    for bit in bits_of(lax.axis_size("wide"))[3:]:
        keep1, send1, keep2, send2 = [
            (v.astype(F32) + swap(v, "wide", bit).astype(F32)).astype(BF)
            for v in (keep1, send1, keep2, send2)
        ]
    return keep1, swap(send1, "narrow", 2), keep2, swap(send2, "wide", 1)


class Flow:
    def __init__(self, sc, *parts):
        self.sc = sc
        self.parts = parts
        self.width = len(parts) * parts[0][0].shape[1]

    def halve(self, deps=()):
        operands = [v for part in self.parts for v in part]
        k1, s1, k2, s2 = glue(
            functools.partial(halve_kernel, len(self.parts)), "halve", self.sc, operands,
            [(192, self.width)] * 4, deps,
        )
        self.kept = k1, k2
        self.got = swap(s1, "wide", 1), swap(s2, "narrow", 2)
        return s1, s2

    def quarter(self, deps=()):
        outs = glue(
            quarter_kernel, "quarter", self.sc, (self.kept[0], self.got[0], self.kept[1], self.got[1]),
            [(48, 2 * self.width)] * 4, deps,
        )
        self.kept = outs[0]
        self.got = [swap(outs[d], "wide", 2 * d) for d in (1, 2, 3)]
        return tuple(outs[1:])

    def total(self, deps=()):
        (self.own,) = glue(
            total_kernel, "total", self.sc, (self.kept, *self.got), [(48, 2 * self.width)], deps
        )
        return (self.own,)

    def gather_one(self):
        every = [self.own, *(swap(self.own, "wide", 2 * d) for d in (1, 2, 3))]
        self.kept = tuple(
            jnp.concatenate([v[:, at : at + self.width] for v in every], axis=0) for at in (0, self.width)
        )
        self.got = swap(self.kept[0], "wide", 1), swap(self.kept[1], "narrow", 2)

    def gather_two(self):
        self.kept = tuple(jnp.concatenate(pair, axis=0) for pair in zip(self.kept, self.got))
        self.got = swap(self.kept[0], "narrow", 2), swap(self.kept[1], "wide", 1)

    def gather_three(self):
        self.kept = jnp.concatenate(
            [jnp.concatenate(pair, axis=0) for pair in zip(self.kept, self.got)], axis=1
        )
        self.got = swap(self.kept, "narrow", 1)

    def gather_all(self):
        return lax.all_gather(self.own, ("wide", "narrow"), axis=0, tiled=False)


def feed_done_kernel(sc, *refs):
    up_out, down_out = refs[4:]
    for core in range(2):
        one, two = refs[2 * core : 2 * core + 2]
        up_out[:, 1536 * core : 1536 * core + 1536] = one[0].astype(F32)
        for half in range(2):
            down_out[2 * core + half] = two[0, :, 768 * half : 768 * half + 768].astype(F32)


def feed_done(sc, gathered):
    def device(x, y, z, core):
        return (2 * z + y) * 4 + 2 * x + core

    def one(core):
        return pl.BlockSpec(
            (1, 48, 1536), lambda i, s: (device(i // 8, (i // 4) % 2, i % 4, core), 0, 0)
        )

    def two(core):
        return pl.BlockSpec(
            (1, 48, 1536), lambda i, s: (device((i // 4) % 2, i // 8, i % 4, core), 0, 1)
        )

    up, down = pl.pallas_call(
        feed_done_kernel,
        grid_spec=pltpu.PrefetchScalarGridSpec(
            num_scalar_prefetch=1,
            grid=(16,),
            in_specs=[one(0), two(0), one(1), two(1)],
            out_specs=[
                pl.BlockSpec((48, 3072), lambda i, s: (i, 0)),
                pl.BlockSpec((4, 48, 768), lambda i, s: (0, i, 0)),
            ],
        ),
        out_shape=[
            jax.ShapeDtypeStruct((768, 3072), F32),
            jax.ShapeDtypeStruct((4, 768, 768), F32),
        ],
        compiler_params=pltpu.CompilerParams(vmem_limit_bytes=VMEM_LIMIT),
        cost_estimate=pl.CostEstimate(flops=1_000_000, bytes_accessed=28_000_000, transcendentals=0),
        name="feed_done",
    )(sc, *([gathered] * 4))
    return up, down.reshape(3072, 768)


def attend_done_kernel(sc, one, two, other_one, other_two, qkv_grad, out_grad):
    def write(core, first, second):
        for at, part in enumerate((first[:, 0:384], first[:, 384:768], second[:, 384:768])):
            for k in range(3):
                dest = 768 * k + 384 * core + LANES * at
                qkv_grad[:, dest : dest + LANES] = part[:, LANES * k : LANES * k + LANES].astype(F32)
        out_grad[core] = second[:, 0:384].astype(F32)

    @pl.when(sc[6] == 0)
    def _():
        write(0, one[...], two[...])
        write(1, other_one[...], other_two[...])

    @pl.when(sc[6] != 0)
    def _():
        write(0, other_one[...], other_two[...])
        write(1, one[...], two[...])


def attend_done(sc, own, other):
    one = pl.BlockSpec((48, 768), lambda i, s: (i ^ s[10], 0))
    two = pl.BlockSpec((48, 768), lambda i, s: (i ^ s[11], 1))
    qkv_grad, out_grad = pl.pallas_call(
        attend_done_kernel,
        grid_spec=pltpu.PrefetchScalarGridSpec(
            num_scalar_prefetch=1,
            grid=(16,),
            in_specs=[one, two] * 2,
            out_specs=[
                pl.BlockSpec((48, 2304), lambda i, s: (i, 0)),
                pl.BlockSpec((2, 48, 384), lambda i, s: (0, i % 8, i // 8)),
            ],
        ),
        out_shape=[
            jax.ShapeDtypeStruct((768, 2304), F32),
            jax.ShapeDtypeStruct((2, 384, 768), F32),
        ],
        compiler_params=pltpu.CompilerParams(vmem_limit_bytes=VMEM_LIMIT),
        cost_estimate=pl.CostEstimate(flops=1_000_000, bytes_accessed=14_000_000, transcendentals=0),
        name="attend_done",
    )(sc, own, own, other, other)
    return qkv_grad, out_grad.reshape(768, 768)


def sum_all(values, order):
    for axis, bit in order:
        values = values + swap(values, axis, bit)
    return values


def on_device(
    tokens, cotangent, conditioning, aspect, bucket,
    qkv_weight, attn_kernel, out_weight, up_weight, ffn_kernel, down_weight,
):
    wide_count = lax.axis_size("wide")
    wide_at = lax.axis_index("wide")
    narrow_at = lax.axis_index("narrow")
    pair, core = narrow_at // 2, narrow_at % 2
    item = 2 * wide_at + pair
    sides = lax.dynamic_index_in_dim(aspect, item, 0, keepdims=False)
    home = lax.dynamic_index_in_dim(bucket, item, 0, keepdims=False)
    stays = home == wide_at

    def pieces_of(block):
        flat = block.reshape(2, 256, 768)
        own = lax.dynamic_index_in_dim(flat, pair, 0, keepdims=False)
        far = lax.dynamic_index_in_dim(flat, 1 - pair, 0, keepdims=False)
        got = swap(far, "narrow", 2)
        return own, got, swap(own, "narrow", 1), swap(got, "narrow", 1)

    token_pieces = pieces_of(tokens)
    seed_pieces = pieces_of(cotangent)
    from_right = lax.ppermute(conditioning, "wide", [(i + 1, i) for i in range(wide_count - 1)])
    modul = jnp.where(stays, conditioning, from_right).astype(F32).reshape(6, 768)
    factor = 1024.0 / (sides[0] * sides[1]).astype(F32)
    mod = jnp.concatenate([modul, jnp.full((2, 768), factor, F32)], axis=0)
    at_y, at_z = wide_at % 2, (wide_at // 2) % 4
    sc = jnp.stack(
        [sides[0], sides[1], 2 * pair + core, 2 * (1 - pair) + core, 2 * pair + 1 - core,
         2 * (1 - pair) + 1 - core, core, pair, at_y, at_z,
         8 * pair + 4 * at_y + at_z, 8 * at_y + 4 * pair + at_z]
    ).astype(jnp.int32)
    attn_k = attn_kernel.reshape(9, -1)
    ffn_k = ffn_kernel.reshape(9, -1)

    base, normed_one, qkv, conv, prob, mixed = attend(sc, token_pieces, mod, qkv_weight, attn_k)
    mixed_other = swap(mixed, "narrow", 1)
    attended, middle, normed_two, d_branch, seed = project_out(
        sc, mixed, mixed_other, base, out_weight, mod, seed_pieces
    )
    *streams, ffn_a, branch, d_normed = feed(
        sc, normed_two, d_branch, up_weight, down_weight, ffn_k, 0, None
    )
    part_a = begin(*streams)
    *streams, ffn_b, branch, branch_send, d_normed, d_normed_send = feed(
        sc, normed_two, d_branch, up_weight, down_weight, ffn_k, 1, (branch, d_normed)
    )
    d_normed_other = swap(d_normed_send, "narrow", 1)
    part_b = begin(*streams)
    branch_other = swap(branch_send, "narrow", 1)
    d_middle, d_att, sums_two, *out_parts = norm_back(
        sc, d_normed, d_normed_other, middle, attended, seed, mod, mixed
    )

    def back(heads, axis, deps):
        return attend_back(
            sc, heads, axis, d_att, out_weight, normed_one, qkv, conv, prob, attn_k, deps
        )

    feeds = Flow(sc, part_a, part_b)
    made = feeds.halve((d_att,))
    g0, kg0, *parts = back(0, 7, made)
    part_c = begin(*parts, *out_parts)
    made = feeds.quarter((g0,))
    g1, kg1, *parts_one = back(1, 7, made)
    g2, kg2, *parts_two = back(2, 8, (g1,))
    part_d = begin(*parts_one, *parts_two)
    made = feeds.total((g2,))
    gathered = feeds.gather_all()
    d_first, d_first_send = first_back(sc, (g0, g1, g2), qkv_weight, made)
    d_first_other = swap(d_first_send, "narrow", 1)
    attends = Flow(sc, part_c, part_d)
    made = attends.halve((d_first,))

    near, far, d_gate_two = finish(sc, middle, branch, branch_other, seed, mod, made)
    made = attends.quarter((near,))
    far = swap(far, "narrow", 2)

    def as_output(near, far):
        first = jnp.where(pair == 0, near, far)
        second = jnp.where(pair == 0, far, near)
        return jnp.stack([first, second]).reshape(tokens.shape)

    block_out = as_output(near, far)
    near, far, sums_one = input_grad(sc, d_first, d_first_other, d_middle, base, mod, made)
    attends.total((near,))
    tokens_grad = as_output(near, swap(far, "narrow", 2))

    cond = jnp.concatenate(
        [sums_one, sums_two[2:3], sums_two[1:2], d_gate_two, sums_two[0:1]], axis=0
    )
    moves = jnp.where(stays, 0.0, cond)
    cond = jnp.where(stays, cond, 0.0) + lax.ppermute(
        moves, "wide", [(i, i + 1) for i in range(wide_count - 1)]
    )
    cond = sum_all(cond, [("narrow", 1), ("narrow", 2)])

    chips = [("wide", bit) for bit in bits_of(wide_count)] + [("narrow", 2)]
    small = sum_all(jnp.concatenate([ffn_a, ffn_b, kg0, kg1, kg2], axis=1), chips)
    small_other = swap(small, "narrow", 1)
    first, second = jnp.where(core == 0, small, small_other), jnp.where(core == 0, small_other, small)
    ffn_grad = jnp.concatenate([first[:, :1536], second[:, :1536]], axis=1).reshape(ffn_kernel.shape)
    attn_grad = jnp.stack([first[:, 1536:], second[:, 1536:]], axis=1).reshape(9, 2, 3, 3, LANES)
    attn_grad = attn_grad.transpose(0, 3, 1, 2, 4).reshape(attn_kernel.shape)

    attends.gather_one()
    attends.gather_two()
    attends.gather_three()
    qkv_grad, out_grad = attend_done(sc, attends.kept, attends.got)
    up_grad, down_grad = feed_done(sc, gathered)

    return (
        block_out, tokens_grad, cond[0:5].reshape(1, -1), cond[5:6],
        qkv_grad, attn_grad, out_grad, up_grad, ffn_grad, down_grad,
    )


def solution(mesh):
    rows = P("wide", "narrow", None, None)
    in_specs = (rows, rows, P("wide", None)) + (P(),) * 8
    out_specs = (rows, rows, P("wide", None), P("wide", None)) + (P(),) * 6
    return jax.shard_map(
        on_device, mesh=mesh, in_specs=in_specs, out_specs=out_specs, check_vma=False
    )
```

```python
import functools

import jax
import jax.numpy as jnp
from jax import lax
from jax.experimental import pallas as pl
from jax.experimental.pallas import tpu as pltpu
from jax.sharding import PartitionSpec as P

HEAD_DIM = 64
LANES = 128
GROUPS = 4
MARGIN = 16

masked_score = -1000000000.0
norm_epsilon = 1e-06
gelu_root = 0.7978845608028654
gelu_cube = 0.044715

BF = jnp.bfloat16
F32 = jnp.float32
SCRATCH = 16 * 1024 * 1024


def dot(left, right, left_dim=1, right_dim=0):
    return lax.dot_general(
        left, right, (((left_dim,), (right_dim,)), ((), ())), preferred_element_type=F32
    )


ANYWHERE = pl.BlockSpec(memory_space=pl.ANY)
SCALARS = pl.BlockSpec(memory_space=pltpu.SMEM)
HERE = pl.BlockSpec(memory_space=pltpu.VMEM)


def shaped(*shape, dtype=BF):
    return jax.ShapeDtypeStruct(shape, dtype)


class Line:
    def __init__(self, scalars):
        self.scalars = scalars
        self.token = None


def run(kernel, name, line, operands, outs, scratch=(), limit=SCRATCH):
    count = len(operands)
    tokens = [] if line.token is None else [line.token]

    def body(sc_ref, *refs):
        refs = refs[:count] + refs[count + len(tokens) :]
        refs[count + len(outs)][...] = jnp.zeros((8, LANES), F32)
        kernel(sc_ref, *refs[: count + len(outs)], *refs[count + len(outs) + 1 :])

    *made, line.token = pl.pallas_call(
        body,
        in_specs=[SCALARS] + [HERE] * count + [ANYWHERE] * len(tokens),
        out_specs=[HERE] * (len(outs) + 1),
        out_shape=[*outs, shaped(8, LANES, dtype=F32)],
        scratch_shapes=list(scratch),
        compiler_params=pltpu.CompilerParams(vmem_limit_bytes=limit),
        cost_estimate=pl.CostEstimate(flops=1, bytes_accessed=1, transcendentals=0),
        name=name,
    )(line.scalars, *operands, *tokens)
    return made


def step(f, *given):
    return functools.partial(f, *given)


def weave(*lists):
    order = sorted(
        ((at + 0.5) / len(steps), which, at)
        for which, steps in enumerate(lists)
        for at in range(len(steps))
    )
    for _, which, at in order:
        lists[which][at]()


def iota(shape, dim):
    return lax.broadcasted_iota(jnp.int32, shape, dim)


def live_rows(token, height, breadth):
    row = 2 * ((token >> 4) & 15) + (token >> 9)
    col = 2 * (token & 15) + ((token >> 8) & 1)
    return ((row < height) & (col < breadth)).astype(F32)


def live_run(start, height, breadth):
    return live_rows(start + iota((64, 1), 0), height, breadth)


def to_phase_matrix():
    row = iota((256, 256), 0)
    col = iota((256, 256), 1)
    grid_row = 2 * ((row >> 4) & 3) + (row >> 7)
    grid_col = 2 * (row & 15) + ((row >> 6) & 1)
    return (col == grid_row * 32 + grid_col).astype(F32).astype(BF)


def normal(values):
    center = values - jnp.mean(values, axis=-1, keepdims=True)
    scale = lax.rsqrt(jnp.mean(center * center, axis=-1, keepdims=True) + norm_epsilon)
    return center * scale, scale


def col_sum(values):
    return jnp.sum(values, axis=0, keepdims=True)


HELD = pltpu.VMEM((2 * GROUPS, 2 * MARGIN + 256, LANES), F32)
STEP = 64


def clear_margins(held):
    zero = jnp.zeros((2 * GROUPS, MARGIN, LANES), F32)
    held[:, 0:MARGIN, :] = zero
    held[:, MARGIN + 256 : 2 * MARGIN + 256, :] = zero


def hold_steps(held, read):
    place = iota((256, LANES), 0) & 15

    def one(g):
        values = read(g)
        held[2 * g, MARGIN : MARGIN + 256, :] = values
        if g % 2:
            moved = jnp.where(place == 0, 0.0, pltpu.roll(values, 1, 0))
        else:
            moved = jnp.where(place == 15, 0.0, pltpu.roll(values, 255, 0))
        held[2 * g + 1, MARGIN : MARGIN + 256, :] = moved

    return [step(one, g) for g in range(GROUPS)]


def taps(g):
    alpha, beta = g // 2, g % 2
    out = []
    for a in range(3):
        for b in range(3):
            row = alpha + a - 1
            col = beta + b - 1
            src = 2 * (row % 2) + col % 2
            out.append((a, b, 2 * src + (0 if 0 <= col <= 1 else 1), MARGIN * (row // 2)))
    return out


def tap_weights(kernel):
    return [[kernel[3 * a + b : 3 * a + b + 1, :] for b in range(3)] for a in range(3)]


def taps_at(kernel, start):
    cols = lanes_at(start)
    return jnp.concatenate([kernel[a, :, cols].astype(F32) for a in range(3)], axis=0)


def runs():
    return [(g, start) for g in range(GROUPS) for start in range(0, 256, STEP)]


def run_rows(g, start):
    return slice(g * 256 + start, g * 256 + start + STEP)


def conv_steps(held, kernel, write):
    weights = tap_weights(kernel)

    def one(g, start):
        total = None
        for a, b, src, off in taps(g):
            part = weights[a][b] * held[src, MARGIN + off + start : MARGIN + off + start + STEP, :]
            total = part if total is None else total + part
        write(run_rows(g, start), total)

    return [step(one, *at) for at in runs()]


def back_steps(held, kernel, read, write, write_sums):
    weights = tap_weights(kernel)
    sums = [None] * 9

    def one(g, start):
        given = read(run_rows(g, start))
        total = None
        for a, b, src, off in taps(g):
            window = held[src, MARGIN + off + start : MARGIN + off + start + STEP, :]
            part = weights[2 - a][2 - b] * window
            total = part if total is None else total + part
            at = 3 * (2 - a) + 2 - b
            prod = jnp.sum((given * window).reshape(STEP // 8, 8, LANES), axis=0)
            sums[at] = prod if sums[at] is None else sums[at] + prod
        write(run_rows(g, start), total)

    def last():
        write_sums(jnp.concatenate([col_sum(v) for v in sums], axis=0))

    return [step(one, *at) for at in runs()] + [last]


def lanes_at(start):
    return pl.ds(pl.multiple_of(start, LANES), LANES)


def attend_kernel(
    sc, p0, p1, p2, p3, mod, qkv_weight, kernel,
    base_out, normed_out, qkv_out, conv_out, prob_out, mixed_out,
    held, weight,
):
    height, breadth, core = sc[0], sc[1], sc[6]
    clear_margins(held)
    shift, scale = mod[0:1, :], 1.0 + mod[1:2, :]
    matrix = to_phase_matrix()

    def norm(k, piece, g):
        start = pl.multiple_of(g * 256 + sc[2 + k] * 64, 64)
        moved = dot(matrix[g * 64 : g * 64 + 64, :], piece[...])
        values = moved * live_run(start, height, breadth)
        base_out[pl.ds(start, 64), :] = values.astype(BF)
        normed_out[pl.ds(start, 64), :] = (normal(values)[0] * scale + shift).astype(BF)

    def pick(pair, s):
        at = (3 * pair + s) * LANES
        weight[:, at : at + LANES] = qkv_weight[:, lanes_at(768 * s + 384 * core + LANES * pair)]

    weave(
        [step(norm, k, piece, g) for k, piece in enumerate((p0, p1, p2, p3)) for g in range(GROUPS)],
        [step(pick, pair, s) for pair in range(3) for s in range(3)],
    )

    def project(col, r):
        cols = slice(col, min(col + 256, 1152))
        qkv_out[r : r + 256, cols] = dot(normed_out[r : r + 256, :], weight[:, cols]).astype(BF)

    def project_steps(cols):
        return [step(project, col, r) for col in cols for r in range(0, 1024, 256)]

    def conv_pair(pair):
        steps = []
        for s in range(3):
            at = (3 * pair + s) * LANES
            cols = slice(at, at + LANES)

            def read(g, cols=cols):
                return qkv_out[g * 256 : g * 256 + 256, cols].astype(F32)

            def write(rows, total, cols=cols):
                conv_out[rows, cols] = total.astype(BF)

            steps += hold_steps(held, read)
            weights = taps_at(kernel, 768 * s + 384 * core + LANES * pair)
            steps += conv_steps(held, weights, write)
        return steps

    token = iota((1, 256), 1)
    lane = iota((256, LANES), 1)

    def attend_pair(pair):
        at = 3 * pair * LANES
        parts = {}

        def one(g, h):
            rows = slice(g * 256, g * 256 + 256)
            live = live_rows(token + g * 256, height, breadth) > 0.5
            query = conv_out[rows, at : at + LANES] * BF(HEAD_DIM**-0.5)
            key = conv_out[rows, at + LANES : at + 2 * LANES]
            value = conv_out[rows, at + 2 * LANES : at + 3 * LANES]
            mine = (lane < HEAD_DIM) if h == 0 else (lane >= HEAD_DIM)
            score = dot(jnp.where(mine, query, BF(0)), key, 1, 1)
            score = jnp.where(live, score, masked_score)
            top = jnp.max(score, axis=-1, keepdims=True)
            raised = jnp.exp(score - top)
            prob = (raised * (1.0 / jnp.sum(raised, axis=-1, keepdims=True))).astype(BF)
            prob_out[pair, g, h] = prob
            parts[h] = dot(prob, value)
            if h == 1:
                both = jnp.where(lane < HEAD_DIM, parts[0], parts[1])
                mixed_out[rows, pair * LANES : pair * LANES + LANES] = both.astype(BF)

        return [step(one, g, h) for g in range(GROUPS) for h in range(2)]

    weave(project_steps((0, 256)))
    weave(conv_pair(0), project_steps((512, 768, 1024)))
    weave(attend_pair(0), conv_pair(1))
    weave(attend_pair(1), conv_pair(2))
    weave(attend_pair(2))


def attend(sc, pieces, mod, qkv_weight, attn_kernel):
    return run(
        attend_kernel, "attend", sc, (*pieces, mod, qkv_weight, attn_kernel),
        [shaped(1024, 768), shaped(1024, 768), shaped(1024, 1152), shaped(1024, 1152),
         shaped(3, GROUPS, 2, 256, 256), shaped(1024, 384)],
        [HELD, pltpu.VMEM((768, 1152), BF)],
    )


def middle_kernel(
    sc, mixed_own, mixed_other, base, out_weight, mod, c0, c1, c2, c3,
    attended_out, normed_out, branch_grad_out, seed_out,
    mixed, attended,
):
    height, breadth, core = sc[0], sc[1], sc[6]
    mixed[:, pl.ds(pl.multiple_of(core * 384, LANES), 384)] = mixed_own[...]
    mixed[:, pl.ds(pl.multiple_of((1 - core) * 384, LANES), 384)] = mixed_other[...]
    gate = mod[2:3, :]
    shift, scale = mod[3:4, :], 1.0 + mod[4:5, :]
    gate_two, factor = mod[5:6, :], mod[6:7, :]
    matrix = to_phase_matrix()

    def project(r):
        attended[r : r + 256, :] = dot(mixed[r : r + 256, :], out_weight[...])

    def norm(r):
        rows = slice(r, r + 64)
        got = attended[rows, :].astype(BF)
        attended_out[rows, :] = got
        middle = base[rows, :].astype(F32) + gate * got.astype(F32)
        normed_out[rows, :] = (normal(middle)[0] * scale + shift).astype(BF)

    def seed(k, piece, g):
        start = pl.multiple_of(g * 256 + sc[2 + k] * 64, 64)
        moved = dot(matrix[g * 64 : g * 64 + 64, :], piece[...])
        values = moved * live_run(start, height, breadth)
        seed_out[pl.ds(start, 64), :] = values.astype(BF)
        branch_grad_out[pl.ds(start, 64), :] = (values * factor * gate_two).astype(BF)

    project(0)
    weave([step(project, r) for r in (256, 512, 768)], [step(norm, r) for r in range(0, 768, 64)],
          [step(seed, k, piece, g) for k, piece in enumerate((c0, c1, c2, c3)) for g in range(GROUPS)])
    weave([step(norm, r) for r in range(768, 1024, 64)])


def project_out(sc, mixed_own, mixed_other, base, out_weight, mod, pieces):
    return run(
        middle_kernel, "project_out", sc, (mixed_own, mixed_other, base, out_weight, mod, *pieces),
        [shaped(1024, 768)] * 4,
        [pltpu.VMEM((1024, 768), BF), pltpu.VMEM((1024, 768), F32)],
    )


BLOCK = 256


def keep_half(core, values, local):
    low = values[128 * local : 128 * local + 64, :]
    high = values[128 * local + 64 : 128 * local + 128, :]
    return jnp.where(core == 0, low, high), jnp.where(core == 0, high, low)


def feed_kernel(first, half, sc, normed, branch_grad, up, down, kernel, *rest):
    if first:
        (up_keep, up_send, down_keep, down_send, kernel_grad, acts, d_hids,
         held, held_back, hid, d_act, d_conv) = rest
    else:
        (before_acts, before_hids,
         up_keep, up_send, down_keep, down_send, kernel_grad, branch_keep, branch_send, normed_grad_out,
         held, held_back, hid, d_act, d_conv, acts, d_hids, branch, normed_grad) = rest
    core = sc[6]
    origin = core * 1536 + half * 768
    clear_margins(held)
    clear_margins(held_back)

    def weight_block(k):
        return pl.ds(pl.multiple_of(origin + k * BLOCK, BLOCK), BLOCK)

    def project_steps(k):
        block = weight_block(k)
        place = k % 2

        def one(r):
            hid[place, r : r + 256, :] = dot(normed[r : r + 256, :], up[:, block]).astype(BF)

        def two(r):
            d_act[place, r : r + 256, :] = dot(branch_grad[r : r + 256, :], down[block, :], 1, 1)

        return [step(f, r) for r in range(0, 1024, 256) for f in (one, two)]

    def local_steps(k):
        steps = []
        place = k % 2
        for lane_block in range(BLOCK // LANES):
            cols = slice(lane_block * LANES, (lane_block + 1) * LANES)
            at = k * BLOCK + lane_block * LANES
            dest = slice(at, at + LANES)
            weights = taps_at(kernel, origin + at)

            def read(g, cols=cols):
                return hid[place, g * 256 : g * 256 + 256, cols].astype(F32)

            def activate(rows, v, cols=cols, dest=dest):
                square = v * v
                bent = jnp.tanh(v * (gelu_root + (gelu_root * gelu_cube) * square))
                rise = 0.5 + 0.5 * bent
                value = v * rise
                acts[rows, dest] = value.astype(BF)
                slope = rise + value * (1.0 - bent) * (gelu_root + (3.0 * gelu_root * gelu_cube) * square)
                d_conv[rows, :] = (d_act[place, rows, cols] * slope).astype(BF)

            def source(rows, cols=cols):
                return hid[place, rows, cols].astype(F32)

            def write(rows, total, dest=dest):
                d_hids[rows, dest] = total.astype(BF)

            def write_sums(values, dest=dest):
                kernel_grad[:, dest] = values

            steps += hold_steps(held, read)
            steps += conv_steps(held, weights, activate)
            steps += hold_steps(held_back, lambda g: d_conv[g * 256 : g * 256 + 256, :].astype(F32))
            steps += back_steps(held_back, weights, source, write, write_sums)
        return steps

    def up_steps(k):
        cols = slice(k * BLOCK, (k + 1) * BLOCK)

        def one(pair, out):
            at = pl.ds(pl.multiple_of(pair * 384, 384), 384)
            out[:, cols] = dot(normed[:, at], d_hids[:, cols], 0, 0).astype(BF)

        return [step(one, sc[7], up_keep), step(one, 1 - sc[7], up_send)]

    def down_steps():
        def one(place, out, c):
            rows = pl.ds(pl.multiple_of(place * 384, 384), 384)
            out[:, c : c + 256] = dot(acts[:, rows], branch_grad[:, c : c + 256], 0, 0).astype(BF)

        return [
            step(one, place, out, c)
            for place, out in ((sc[8], down_keep), (1 - sc[8], down_send))
            for c in range(0, 768, 256)
        ]

    def before_steps(part):
        where = pl.ds(pl.multiple_of(core * 1536, 768), 768)

        def one(r):
            branch[r : r + 256, :] = dot(before_acts[r : r + 256, :], down[where, :])

        def two(r):
            normed_grad[r : r + 256, :] = dot(before_hids[r : r + 256, :], up[:, where], 1, 1)

        return [] if first else [step((one, two)[part], r) for r in range(0, 1024, 256)]

    weave(project_steps(0))
    weave(local_steps(0), project_steps(1), before_steps(0))
    weave(local_steps(1), project_steps(2), up_steps(0), before_steps(1))
    weave(local_steps(2), up_steps(1))
    weave(down_steps(), up_steps(2))
    if not first:
        where = pl.ds(pl.multiple_of(origin, 768), 768)
        for g in range(GROUPS):
            rows = slice(g * 256, g * 256 + 256)
            total = branch[rows, :] + dot(acts[rows, :], down[where, :])
            for local in range(2):
                keep, send = keep_half(core, total, local)
                branch_keep[2 * g + local] = keep
                branch_send[2 * g + local] = send.astype(BF)
            total = normed_grad[rows, :] + dot(d_hids[rows, :], up[:, where], 1, 1)
            normed_grad_out[rows, :] = total.astype(BF)


def feed(sc, normed, branch_grad, up_weight, down_weight, ffn_kernel, half, before):
    first = before is None
    return run(
        functools.partial(feed_kernel, first, half), "feed", sc,
        (normed, branch_grad, up_weight, down_weight, ffn_kernel, *(() if first else before)),
        [shaped(384, 768)] * 4
        + [shaped(9, 768, dtype=F32)]
        + (
            [shaped(1024, 768)] * 2
            if first
            else [shaped(8, 64, 768, dtype=F32), shaped(8, 64, 768), shaped(1024, 768)]
        ),
        [HELD, HELD, pltpu.VMEM((2, 1024, BLOCK), BF), pltpu.VMEM((2, 1024, BLOCK), F32),
         pltpu.VMEM((1024, LANES), BF)]
        + ([] if first else [pltpu.VMEM((1024, 768), BF)] * 2 + [pltpu.VMEM((1024, 768), F32)] * 2),
        limit=24 * 1024 * 1024,
    )


def put_pieces(sc, done, near_out, far_out):
    @pl.when(sc[7] == 0)
    def _():
        near_out[...] = done[0]
        far_out[...] = done[1]

    @pl.when(sc[7] != 0)
    def _():
        near_out[...] = done[1]
        far_out[...] = done[0]


def finish_kernel(sc, base, attended, branch, branch_other, seed, mod, near_out, far_out, sums_out):
    height, breadth, core = sc[0], sc[1], sc[6]
    gate_one, gate, factor = mod[2:3, :], mod[5:6, :], mod[6:7, :]
    matrix = to_phase_matrix()
    total = jnp.zeros((1, 768), F32)
    done = []
    for local in range(2):
        parts = []
        for g in range(GROUPS):
            start = pl.multiple_of(g * 256 + (2 * local + core) * 64, 64)
            rows = pl.ds(start, 64)
            whole = branch[2 * g + local] + branch_other[2 * g + local].astype(F32)
            total = total + col_sum(seed[rows, :].astype(F32) * whole)
            middle = base[rows, :].astype(F32) + gate_one * attended[rows, :].astype(F32)
            result = middle + gate * whole
            parts.append((result * live_run(start, height, breadth)).astype(BF))
        done.append(dot(matrix, jnp.concatenate(parts, axis=0), 0, 0).astype(BF))
    put_pieces(sc, done, near_out, far_out)
    sums_out[...] = total * factor


def finish(sc, base, attended, branch, branch_other, seed, mod):
    return run(
        finish_kernel, "finish", sc, (base, attended, branch, branch_other, seed, mod),
        [shaped(256, 768), shaped(256, 768), shaped(1, 768, dtype=F32)],
    )


def norm_back_kernel(
    sc, normed_grad, normed_grad_other, base, attended, seed, mod, mixed,
    middle_grad, att_grad, sums_out, out_keep, out_send,
):
    gate, scale, factor = mod[2:3, :], 1.0 + mod[4:5, :], mod[6:7, :]
    sums = [jnp.zeros((1, 768), F32) for _ in range(3)]

    def norm(r):
        rows = slice(r, r + 64)
        grad = normed_grad[rows, :].astype(F32) + normed_grad_other[rows, :].astype(F32)
        got = attended[rows, :].astype(F32)
        unit, inverse = normal(base[rows, :].astype(F32) + gate * got)
        both = grad * unit
        sums[0] = sums[0] + col_sum(grad)
        sums[1] = sums[1] + col_sum(both)
        grad = grad * scale
        mean = jnp.mean(grad, axis=-1, keepdims=True)
        along = jnp.mean(both * scale, axis=-1, keepdims=True)
        total = seed[rows, :].astype(F32) * factor + inverse * (grad - mean - unit * along)
        middle_grad[rows, :] = total
        sums[2] = sums[2] + col_sum(total * got)
        att_grad[rows, :] = (total * gate).astype(BF)

    for r in range(0, 1024, 64):
        norm(r)
    for k in range(3):
        sums_out[k : k + 1, :] = 0.5 * sums[k]
    for at_y, out in ((sc[8], out_keep), (1 - sc[8], out_send)):
        cols = pl.ds(pl.multiple_of(at_y * 384, 384), 384)
        out[...] = dot(mixed[...], att_grad[:, cols], 0, 0).astype(BF)


def norm_back(sc, normed_grad, normed_grad_other, base, attended, seed, mod, mixed):
    return run(
        norm_back_kernel, "norm_back", sc,
        (normed_grad, normed_grad_other, base, attended, seed, mod, mixed),
        [shaped(1024, 768, dtype=F32), shaped(1024, 768), shaped(3, 768, dtype=F32),
         shaped(384, 384), shaped(384, 384)],
    )


def attend_back_kernel(
    heads, axis, sc, att_grad, out_weight, normed, qkv, conv, prob, kernel,
    qkv_grad, kernel_grad, weight_keep, weight_send, held, d_mixed, d_conv,
):
    core = sc[6]
    at = 3 * heads * LANES
    clear_margins(held)
    mine_rows = pl.ds(pl.multiple_of(core * 384 + heads * LANES, LANES), LANES)
    for r in range(0, 1024, 256):
        d_mixed[r : r + 256, :] = dot(att_grad[r : r + 256, :], out_weight[mine_rows, :], 1, 1).astype(BF)

    lane = iota((256, LANES), 1)
    low = lane < HEAD_DIM
    parts = {}

    def one(g, h):
        rows = slice(g * 256, g * 256 + 256)
        grad = d_mixed[rows, :]
        query = conv[rows, at : at + LANES]
        key = conv[rows, at + LANES : at + 2 * LANES]
        value = conv[rows, at + 2 * LANES : at + 3 * LANES]
        mine = low if h == 0 else jnp.logical_not(low)
        p = prob[heads, g, h]
        d_value = dot(p, grad, 0, 0)
        d_prob = dot(jnp.where(mine, grad, BF(0)), value, 1, 1)
        wide_p = p.astype(F32)
        inner = jnp.sum(d_prob * wide_p, axis=-1, keepdims=True)
        d_score = (wide_p * (d_prob - inner)).astype(BF)
        parts[h] = (dot(d_score, key), dot(d_score, query, 0, 0), d_value)
        if h == 1:
            for k in range(3):
                picked = jnp.where(low, parts[0][k], parts[1][k])
                if k < 2:
                    picked = picked * HEAD_DIM**-0.5
                d_conv[rows, k * LANES : (k + 1) * LANES] = picked.astype(BF)

    def local_steps(s):
        cols = slice(s * LANES, (s + 1) * LANES)
        source_cols = slice(at + s * LANES, at + (s + 1) * LANES)

        def write(rows, total):
            qkv_grad[rows, cols] = total.astype(BF)

        def write_sums(values):
            kernel_grad[:, cols] = values

        weights = taps_at(kernel, 768 * s + 384 * core + LANES * heads)
        return hold_steps(
            held, lambda g: d_conv[g * 256 : g * 256 + 256, cols].astype(F32)
        ) + back_steps(held, weights, lambda rows: qkv[rows, source_cols].astype(F32), write, write_sums)

    weave([step(one, g, h) for g in range(GROUPS) for h in range(2)])
    for s in range(3):
        weave(local_steps(s))
    for place, out in ((sc[axis], weight_keep), (1 - sc[axis], weight_send)):
        rows = pl.ds(pl.multiple_of(place * 384, 384), 384)
        out[...] = dot(normed[:, rows], qkv_grad[...], 0, 0).astype(BF)


def attend_back(sc, heads, axis, att_grad, out_weight, normed, qkv, conv, prob, attn_kernel):
    return run(
        functools.partial(attend_back_kernel, heads, axis), "attend_back", sc,
        (att_grad, out_weight, normed, qkv, conv, prob, attn_kernel),
        [shaped(1024, 384), shaped(9, 384, dtype=F32), shaped(384, 384), shaped(384, 384)],
        [HELD, pltpu.VMEM((1024, LANES), BF), pltpu.VMEM((1024, 384), BF)],
    )


def first_back_kernel(sc, g0, g1, g2, qkv_weight, keep, send, grads, weight):
    core = sc[6]
    for k, grad in enumerate((g0, g1, g2)):
        grads[:, 384 * k : 384 * k + 384] = grad[...]
        for s in range(3):
            at = 384 * k + LANES * s
            weight[:, at : at + LANES] = qkv_weight[:, lanes_at(768 * s + 384 * core + LANES * k)]
    for g in range(GROUPS):
        total = dot(grads[g * 256 : g * 256 + 256, :], weight[...], 1, 1)
        for local in range(2):
            kept, sent = keep_half(core, total, local)
            keep[2 * g + local] = kept
            send[2 * g + local] = sent.astype(BF)


def first_back(sc, grads, qkv_weight):
    return run(
        first_back_kernel, "first_back", sc, (*grads, qkv_weight),
        [shaped(8, 64, 768, dtype=F32), shaped(8, 64, 768)],
        [pltpu.VMEM((1024, 1152), BF), pltpu.VMEM((768, 1152), BF)],
    )


def input_kernel(sc, grad, grad_other, middle_grad, base, mod, near_out, far_out, sums_out):
    height, breadth, core = sc[0], sc[1], sc[6]
    scale = 1.0 + mod[1:2, :]
    matrix = to_phase_matrix()
    d_shift = jnp.zeros((1, 768), F32)
    d_scale = jnp.zeros((1, 768), F32)
    done = []
    for local in range(2):
        parts = []
        for g in range(GROUPS):
            at = 2 * g + local
            start = pl.multiple_of(g * 256 + (2 * local + core) * 64, 64)
            rows = pl.ds(start, 64)
            total = grad[at] + grad_other[at].astype(F32)
            unit, inverse = normal(base[rows, :].astype(F32))
            both = total * unit
            d_shift = d_shift + col_sum(total)
            d_scale = d_scale + col_sum(both)
            total = total * scale
            mean = jnp.mean(total, axis=-1, keepdims=True)
            along = jnp.mean(both * scale, axis=-1, keepdims=True)
            total = middle_grad[rows, :] + inverse * (total - mean - unit * along)
            parts.append((total * live_run(start, height, breadth)).astype(BF))
        done.append(dot(matrix, jnp.concatenate(parts, axis=0), 0, 0).astype(BF))
    put_pieces(sc, done, near_out, far_out)
    sums_out[0:1, :] = d_shift
    sums_out[1:2, :] = d_scale


def input_grad(sc, grad, grad_other, middle_grad, base, mod):
    return run(
        input_kernel, "input_grad", sc, (grad, grad_other, middle_grad, base, mod),
        [shaped(256, 768), shaped(256, 768), shaped(2, 768, dtype=F32)],
    )


def swap(values, axis, bit):
    count = lax.axis_size(axis)
    return lax.ppermute(values, axis, [(i, i ^ bit) for i in range(count)])


def bits_of(count):
    return [1 << k for k in range(count.bit_length() - 1)]


def halve_kernel(parts, sc, *rest):
    inputs, (keep1, send1, keep2, send2) = rest[: 4 * parts], rest[4 * parts :]
    half = keep1.shape[0]
    for part in range(parts):
        k1, r1, k2, r2 = inputs[4 * part : 4 * part + 4]
        width = k1.shape[1]
        cols = slice(part * width, (part + 1) * width)
        for kept, got, keep, send, bit in ((k1, r1, keep1, send1, sc[8]), (k2, r2, keep2, send2, sc[7])):
            for place, out in ((bit, keep), (1 - bit, send)):
                rows = pl.ds(pl.multiple_of(place * half, 16), half)
                out[:, cols] = (kept[rows, :].astype(F32) + got[rows, :].astype(F32)).astype(BF)


def quarter_kernel(sc, k1, r1, k2, r2, *outs):
    width = k1.shape[1]
    for d, out in enumerate(outs):
        rows = pl.ds(pl.multiple_of((sc[9] ^ d) * 48, 16), 48)
        out[:, 0:width] = (k1[rows, :].astype(F32) + r1[rows, :].astype(F32)).astype(BF)
        out[:, width : 2 * width] = (k2[rows, :].astype(F32) + r2[rows, :].astype(F32)).astype(BF)


def total_kernel(sc, a, b, c, d, out):
    out[...] = (
        (a[...].astype(F32) + b[...].astype(F32)) + (c[...].astype(F32) + d[...].astype(F32))
    ).astype(BF)


def gather_one_kernel(sc, a, b, c, d, one, two):
    width = one.shape[1]
    for at, part in enumerate((a, b, c, d)):
        rows = slice(48 * at, 48 * at + 48)
        one[rows, :] = part[:, 0:width]
        two[rows, :] = part[:, width : 2 * width]


def gather_two_kernel(sc, k1, r1, k2, r2, one, two):
    half = k1.shape[0]
    for kept, got, out in ((k1, r1, one), (k2, r2, two)):
        out[0:half, :] = kept[...]
        out[half : 2 * half, :] = got[...]


def gather_three_kernel(sc, k1, r1, k2, r2, out):
    half, width = k1.shape
    for at, (kept, got) in enumerate(((k1, r1), (k2, r2))):
        cols = slice(width * at, width * at + width)
        out[0:half, cols] = kept[...]
        out[half : 2 * half, cols] = got[...]


def begin(keep1, send1, keep2, send2):
    for bit in bits_of(lax.axis_size("wide"))[3:]:
        keep1, send1, keep2, send2 = [
            (v.astype(F32) + swap(v, "wide", bit).astype(F32)).astype(BF)
            for v in (keep1, send1, keep2, send2)
        ]
    return keep1, swap(send1, "narrow", 2), keep2, swap(send2, "wide", 1)


class Flow:
    def __init__(self, line, *parts):
        self.line = line
        self.parts = parts
        self.width = len(parts) * parts[0][0].shape[1]

    def both(self):
        return self.kept[0], self.got[0], self.kept[1], self.got[1]

    def halve(self):
        operands = [v for part in self.parts for v in part]
        k1, s1, k2, s2 = run(
            functools.partial(halve_kernel, len(self.parts)), "halve", self.line, operands,
            [shaped(192, self.width)] * 4,
        )
        self.kept = k1, k2
        self.got = swap(s1, "wide", 1), swap(s2, "narrow", 2)

    def quarter(self):
        outs = run(
            quarter_kernel, "quarter", self.line, self.both(), [shaped(48, 2 * self.width)] * 4
        )
        self.kept = outs[0]
        self.got = [swap(outs[d], "wide", 2 * d) for d in (1, 2, 3)]

    def total(self):
        (own,) = run(
            total_kernel, "total", self.line, (self.kept, *self.got), [shaped(48, 2 * self.width)]
        )
        self.kept = own, *(swap(own, "wide", 2 * d) for d in (1, 2, 3))

    def gather_one(self):
        self.kept = run(
            gather_one_kernel, "gather_one", self.line, self.kept, [shaped(192, self.width)] * 2
        )
        self.got = swap(self.kept[0], "wide", 1), swap(self.kept[1], "narrow", 2)

    def gather_two(self):
        self.kept = run(
            gather_two_kernel, "gather_two", self.line, self.both(), [shaped(384, self.width)] * 2
        )
        self.got = swap(self.kept[0], "narrow", 2), swap(self.kept[1], "wide", 1)

    def gather_three(self):
        (own,) = run(
            gather_three_kernel, "gather_three", self.line, self.both(), [shaped(768, 2 * self.width)]
        )
        self.kept = own, swap(own, "narrow", 1)


def by_core(core, write, own, other):
    @pl.when(core == 0)
    def _():
        write(own, other)

    @pl.when(core != 0)
    def _():
        write(other, own)


def row_runs(sc):
    for i in range(16):
        yield (
            slice(48 * i, 48 * i + 48),
            pl.ds(pl.multiple_of((i ^ sc[10]) * 48, 16), 48),
            pl.ds(pl.multiple_of((i ^ sc[11]) * 48, 16), 48),
        )


def feed_done_kernel(sc, a, b, other_a, other_b, up_out, down_out):
    def write(first, second):
        for at, part in enumerate((*first, *second)):
            for rows, one, two in row_runs(sc):
                up_out[one, 768 * at : 768 * at + 768] = part[rows, 0:768].astype(F32)
                down_out[at, two, :] = part[rows, 768:1536].astype(F32)

    by_core(sc[6], write, (a, b), (other_a, other_b))


def feed_done(line, a, b):
    up, down = run(
        feed_done_kernel, "feed_done", line, (a.kept[0], b.kept[0], a.kept[1], b.kept[1]),
        [shaped(768, 3072, dtype=F32), shaped(4, 768, 768, dtype=F32)], limit=40 * 1024 * 1024,
    )
    return up, down.reshape(3072, 768)


def attend_done_kernel(sc, own, other, qkv_grad, out_grad):
    def write(first, second):
        for core, part in enumerate((first, second)):
            for i, (rows, one, two) in enumerate(row_runs(sc)):
                for at, (dest, col) in enumerate(((one, 0), (one, 384), (two, 1152))):
                    for k in range(3):
                        to = 768 * k + 384 * core + LANES * at
                        qkv_grad[dest, to : to + LANES] = part[
                            rows, col + LANES * k : col + LANES * k + LANES
                        ].astype(F32)
                block = i ^ sc[11]
                place = pl.ds(pl.multiple_of((block & 7) * 48, 16), 48)
                cols = pl.ds(pl.multiple_of((block >> 3) * 384, LANES), 384)
                out_grad[core, place, cols] = part[rows, 768:1152].astype(F32)

    by_core(sc[6], write, own, other)


def attend_done(line, flow):
    qkv_grad, out_grad = run(
        attend_done_kernel, "attend_done", line, flow.kept,
        [shaped(768, 2304, dtype=F32), shaped(2, 384, 768, dtype=F32)], limit=24 * 1024 * 1024,
    )
    return qkv_grad, out_grad.reshape(768, 768)


def join_kernel(sc, near, far, out):
    out[sc[7]] = near[...]
    out[1 - sc[7]] = far[...]


def join(line, near, far):
    (out,) = run(join_kernel, "join", line, (near, far), [shaped(2, 256, 768)])
    return out.reshape(2, 8, 32, 768)


def cond_kernel(sc, sums_one, sums_two, d_gate_two, stay, move):
    rows = jnp.concatenate(
        [sums_one[...], sums_two[2:3, :], sums_two[1:2, :], d_gate_two[...], sums_two[0:1, :],
         jnp.zeros((2, 768), F32)], axis=0
    )
    stays = sc[12].astype(F32)
    stay[...] = rows * stays
    move[...] = rows * (1.0 - stays)


def small_kernel(sc, stay, moved, k0, k1, k2, k3, k4, cond, taps_out):
    cond[...] = stay[...] + moved[...]
    taps_out[...] = jnp.zeros(taps_out.shape, F32)
    at = 0
    for k in (k0, k1, k2, k3, k4):
        width = k.shape[1]
        taps_out[0:9, at : at + width] = k[...]
        at += width


def add_kernel(sc, *refs):
    count = len(refs) // 3
    for k in range(count):
        refs[2 * count + k][...] = refs[k][...] + refs[count + k][...]


def add(line, *pairs):
    firsts = [first for first, _ in pairs]
    return run(
        add_kernel, "add", line, firsts + [second for _, second in pairs],
        [shaped(*v.shape, dtype=F32) for v in firsts],
    )


def small_done_kernel(sc, cond, cond_other, own, other, cond_out, shift_out, ffn_out, attn_out):
    total = cond[...] + cond_other[...]
    for k in range(5):
        cond_out[:, 768 * k : 768 * k + 768] = total[k : k + 1, :]
    shift_out[...] = total[5:6, :]

    def write(first, second):
        for core, part in enumerate((first, second)):
            for a in range(3):
                ffn_out[a, :, 1536 * core : 1536 * core + 1536] = part[3 * a : 3 * a + 3, 0:1536]
                for pair in range(3):
                    for s in range(3):
                        to = 768 * s + 384 * core + LANES * pair
                        col = 1536 + (3 * pair + s) * LANES
                        attn_out[a, :, to : to + LANES] = part[3 * a : 3 * a + 3, col : col + LANES]

    by_core(sc[6], write, own, other)


def on_device(
    tokens, cotangent, conditioning, aspect, bucket,
    qkv_weight, attn_kernel, out_weight, up_weight, ffn_kernel, down_weight,
):
    wide_count = lax.axis_size("wide")
    wide_at = lax.axis_index("wide")
    narrow_at = lax.axis_index("narrow")
    pair, core = narrow_at // 2, narrow_at % 2
    item = 2 * wide_at + pair
    sides = lax.dynamic_index_in_dim(aspect, item, 0, keepdims=False)
    home = lax.dynamic_index_in_dim(bucket, item, 0, keepdims=False)
    stays = home == wide_at

    def pieces_of(block):
        flat = block.reshape(2, 256, 768)
        own = lax.dynamic_index_in_dim(flat, pair, 0, keepdims=False)
        far = lax.dynamic_index_in_dim(flat, 1 - pair, 0, keepdims=False)
        got = swap(far, "narrow", 2)
        return own, got, swap(own, "narrow", 1), swap(got, "narrow", 1)

    token_pieces = pieces_of(tokens)
    seed_pieces = pieces_of(cotangent)
    from_right = lax.ppermute(conditioning, "wide", [(i + 1, i) for i in range(wide_count - 1)])
    modul = jnp.where(stays, conditioning, from_right).astype(F32).reshape(6, 768)
    factor = 1024.0 / (sides[0] * sides[1]).astype(F32)
    mod = jnp.concatenate([modul, jnp.full((2, 768), factor, F32)], axis=0)
    at_y, at_z = wide_at % 2, (wide_at // 2) % 4
    scalars = (
        sides[0], sides[1], 2 * pair + core, 2 * (1 - pair) + core, 2 * pair + 1 - core,
        2 * (1 - pair) + 1 - core, core, pair, at_y, at_z,
        8 * pair + 4 * at_y + at_z, 8 * at_y + 4 * pair + at_z, stays,
    )
    place = lax.iota(jnp.int32, 16)
    sc = sum(jnp.where(place == k, value, 0) for k, value in enumerate(scalars)).astype(jnp.int32)
    line = Line(sc)

    base, normed_one, qkv, conv, prob, mixed = attend(line, token_pieces, mod, qkv_weight, attn_kernel)
    mixed_other = swap(mixed, "narrow", 1)
    attended, normed_two, d_branch, seed = project_out(
        line, mixed, mixed_other, base, out_weight, mod, seed_pieces
    )

    def feed_half(half, before):
        return feed(line, normed_two, d_branch, up_weight, down_weight, ffn_kernel, half, before)

    *streams, ffn_a, acts, d_hids = feed_half(0, None)
    flow_a = Flow(line, begin(*streams))
    *streams, ffn_b, branch, branch_send, d_normed = feed_half(1, (acts, d_hids))
    d_normed_other = swap(d_normed, "narrow", 1)
    flow_b = Flow(line, begin(*streams))
    branch_other = swap(branch_send, "narrow", 1)
    flow_a.halve()
    d_middle, d_att, sums_two, *out_parts = norm_back(
        line, d_normed, d_normed_other, base, attended, seed, mod, mixed
    )

    def back(heads, axis):
        return attend_back(line, heads, axis, d_att, out_weight, normed_one, qkv, conv, prob, attn_kernel)

    g0, kg0, *parts = back(0, 7)
    part_c = begin(*parts, *out_parts)
    flow_a.quarter()
    flow_b.halve()
    g1, kg1, *parts_one = back(1, 7)
    flow_a.total()
    flow_b.quarter()
    g2, kg2, *parts_two = back(2, 8)
    flow_c = Flow(line, part_c, begin(*parts_one, *parts_two))
    d_first, d_first_send = first_back(line, (g0, g1, g2), qkv_weight)
    d_first_other = swap(d_first_send, "narrow", 1)
    flow_a.gather_one()
    flow_c.halve()
    near, far, d_gate_two = finish(line, base, attended, branch, branch_other, seed, mod)
    far = swap(far, "narrow", 2)
    flow_b.total()
    flow_a.gather_two()
    flow_c.quarter()
    near_grad, far_grad, sums_one = input_grad(line, d_first, d_first_other, d_middle, base, mod)
    far_grad = swap(far_grad, "narrow", 2)
    cond, move = run(
        cond_kernel, "cond", line, (sums_one, sums_two, d_gate_two), [shaped(8, 768, dtype=F32)] * 2
    )
    moved = lax.ppermute(move, "wide", [(i, i + 1) for i in range(wide_count - 1)])
    flow_b.gather_one()
    flow_c.total()
    flow_a.gather_three()
    block_out = join(line, near, far)
    cond, small = run(
        small_kernel, "small", line, (cond, moved, ffn_a, ffn_b, kg0, kg1, kg2),
        [shaped(8, 768, dtype=F32), shaped(16, 2688, dtype=F32)],
    )
    cond_far, small_far = swap(cond, "narrow", 2), swap(small, "narrow", 2)
    flow_b.gather_two()
    cond, small = add(line, (cond, cond_far), (small, small_far))
    cond_far = swap(cond, "narrow", 1)
    tokens_grad = join(line, near_grad, far_grad)
    flow_c.gather_one()
    for bit in bits_of(wide_count):
        (small,) = add(line, (small, swap(small, "wide", bit)))
    flow_b.gather_three()
    flow_c.gather_two()
    cond_grad, shift_grad, ffn_grad, attn_grad = run(
        small_done_kernel, "small_done", line, (cond, cond_far, small, swap(small, "narrow", 1)),
        [shaped(1, 3840, dtype=F32), shaped(1, 768, dtype=F32), shaped(3, 3, 3072, dtype=F32),
         shaped(3, 3, 2304, dtype=F32)],
    )
    up_grad, down_grad = feed_done(line, flow_a, flow_b)
    flow_c.gather_three()
    qkv_grad, out_grad = attend_done(line, flow_c)

    return (
        block_out, tokens_grad, cond_grad, shift_grad,
        qkv_grad, attn_grad, out_grad, up_grad, ffn_grad, down_grad,
    )


def solution(mesh):
    rows = P("wide", "narrow", None, None)
    in_specs = (rows, rows, P("wide", None)) + (P(),) * 8
    out_specs = (rows, rows, P("wide", None), P("wide", None)) + (P(),) * 6
    return jax.shard_map(
        on_device, mesh=mesh, in_specs=in_specs, out_specs=out_specs, check_vma=False
    )
```

```python
import functools

import jax
import jax.numpy as jnp
from jax import lax
from jax.experimental import pallas as pl
from jax.experimental.pallas import tpu as pltpu
from jax.sharding import PartitionSpec as P

HEAD_DIM = 64
LANES = 128
GROUPS = 4
MARGIN = 16

masked_score = -1000000000.0
norm_epsilon = 1e-06
gelu_root = 0.7978845608028654
gelu_cube = 0.044715

BF = jnp.bfloat16
F32 = jnp.float32
SCRATCH = 16 * 1024 * 1024
ALL_VMEM = 61 * 1024 * 1024
COST = 1150000000


def dot(left, right, left_dim=1, right_dim=0):
    return lax.dot_general(
        left, right, (((left_dim,), (right_dim,)), ((), ())), preferred_element_type=F32
    )


ANYWHERE = pl.BlockSpec(memory_space=pl.ANY)
DISTANT = pl.BlockSpec(memory_space=pltpu.HBM)
SCALARS = pl.BlockSpec(memory_space=pltpu.SMEM)
HERE = pl.BlockSpec(memory_space=pltpu.VMEM)


def shaped(*shape, dtype=BF):
    return jax.ShapeDtypeStruct(shape, dtype)


HALVINGS = ("x", "y", "z", "w"), ("y", "z", "x", "w")


class Place:
    def __init__(self, aspect=None, bucket=None):
        wide, narrow = lax.axis_index("wide"), lax.axis_index("narrow")
        self.pair, self.core = narrow // 2, narrow % 2
        bits = {"x": self.pair, "y": wide % 2, "z": (wide // 2) % 2, "w": (wide // 4) % 2}
        self.bits = [
            jnp.where(self.core == 0, bits[first], bits[second]) for first, second in zip(*HALVINGS)
        ]
        self.chip = self.chip_of(self.bits)
        self.other_chip = self.chip_of(
            [jnp.where(self.core == 0, bits[second], bits[first]) for first, second in zip(*HALVINGS)]
        )
        self.pieces = (
            narrow, 2 * (1 - self.pair) + self.core, 2 * self.pair + 1 - self.core,
            2 * (1 - self.pair) + 1 - self.core,
        )
        if aspect is not None:
            item = 2 * wide + self.pair
            self.height, self.breadth = aspect[item, 0], aspect[item, 1]
            self.stays = bucket[item] == wide

    def chip_of(self, bits):
        return 8 * bits[0] + 4 * bits[1] + 2 * bits[2] + bits[3]


class Line:
    def __init__(self, aspect, bucket):
        self.items = aspect, bucket
        self.token = None


def run(kernel, name, line, operands, outs, scratch=(), limit=SCRATCH, items=False, far=(), far_outs=False, us=1.0):
    count = len(operands)
    tokens = [] if line.token is None else [line.token]
    scalars = list(line.items) if items else []

    def body(*refs):
        place = Place(*refs[: len(scalars)])
        refs = refs[len(scalars) :]
        refs = refs[:count] + refs[count + len(tokens) :]
        refs[count + len(outs)][...] = jnp.zeros((8, LANES), F32)
        kernel(place, *refs[: count + len(outs)], *refs[count + len(outs) + 1 :])

    *made, line.token = pl.pallas_call(
        body,
        in_specs=[SCALARS] * len(scalars)
        + [DISTANT if k in far else HERE for k in range(count)]
        + [ANYWHERE] * len(tokens),
        out_specs=[DISTANT if far_outs else HERE] * len(outs) + [HERE],
        out_shape=[*outs, shaped(8, LANES, dtype=F32)],
        scratch_shapes=list(scratch),
        compiler_params=pltpu.CompilerParams(vmem_limit_bytes=limit),
        cost_estimate=pl.CostEstimate(flops=int(us * COST), bytes_accessed=1, transcendentals=0),
        name=name,
    )(*scalars, *operands, *tokens)
    return made


def step(f, *given):
    return functools.partial(f, *given)


def weave(*lists):
    order = sorted(
        ((at + 0.5) / len(steps), which, at)
        for which, steps in enumerate(lists)
        for at in range(len(steps))
    )
    for _, which, at in order:
        lists[which][at]()


def iota(shape, dim):
    return lax.broadcasted_iota(jnp.int32, shape, dim)


def live_rows(token, height, breadth):
    row = 2 * ((token >> 4) & 15) + (token >> 9)
    col = 2 * (token & 15) + ((token >> 8) & 1)
    return ((row < height) & (col < breadth)).astype(F32)


def live_run(start, height, breadth):
    return live_rows(start + iota((64, 1), 0), height, breadth)


def to_phase_matrix():
    row = iota((256, 256), 0)
    col = iota((256, 256), 1)
    grid_row = 2 * ((row >> 4) & 3) + (row >> 7)
    grid_col = 2 * (row & 15) + ((row >> 6) & 1)
    return (col == grid_row * 32 + grid_col).astype(F32).astype(BF)


def normal(values):
    center = values - jnp.mean(values, axis=-1, keepdims=True)
    scale = lax.rsqrt(jnp.mean(center * center, axis=-1, keepdims=True) + norm_epsilon)
    return center * scale, scale


def col_sum(values):
    return jnp.sum(values, axis=0, keepdims=True)


HELD = pltpu.VMEM((2 * GROUPS, 2 * MARGIN + 256, LANES), F32)
STEP = 64


def clear_margins(held):
    zero = jnp.zeros((2 * GROUPS, MARGIN, LANES), F32)
    held[:, 0:MARGIN, :] = zero
    held[:, MARGIN + 256 : 2 * MARGIN + 256, :] = zero


def hold_steps(held, read):
    place = iota((256, LANES), 0) & 15

    def one(g):
        values = read(g)
        held[2 * g, MARGIN : MARGIN + 256, :] = values
        if g % 2:
            moved = jnp.where(place == 0, 0.0, pltpu.roll(values, 1, 0))
        else:
            moved = jnp.where(place == 15, 0.0, pltpu.roll(values, 255, 0))
        held[2 * g + 1, MARGIN : MARGIN + 256, :] = moved

    return [step(one, g) for g in range(GROUPS)]


def taps(g):
    alpha, beta = g // 2, g % 2
    out = []
    for a in range(3):
        for b in range(3):
            row = alpha + a - 1
            col = beta + b - 1
            src = 2 * (row % 2) + col % 2
            out.append((a, b, 2 * src + (0 if 0 <= col <= 1 else 1), MARGIN * (row // 2)))
    return out


def tap_weights(kernel):
    return [[kernel[3 * a + b : 3 * a + b + 1, :] for b in range(3)] for a in range(3)]


def taps_at(kernel, start):
    cols = lanes_at(start)
    return jnp.concatenate([kernel[a, :, cols].astype(F32) for a in range(3)], axis=0)


def runs():
    return [(g, start) for g in range(GROUPS) for start in range(0, 256, STEP)]


def run_rows(g, start):
    return slice(g * 256 + start, g * 256 + start + STEP)


def conv_steps(held, kernel, write):
    weights = tap_weights(kernel)

    def one(g, start):
        total = None
        for a, b, src, off in taps(g):
            part = weights[a][b] * held[src, MARGIN + off + start : MARGIN + off + start + STEP, :]
            total = part if total is None else total + part
        write(run_rows(g, start), total)

    return [step(one, *at) for at in runs()]


def back_steps(held, kernel, read, write, write_sums):
    weights = tap_weights(kernel)
    sums = [None] * 9

    def one(g, start):
        given = read(run_rows(g, start))
        total = None
        for a, b, src, off in taps(g):
            window = held[src, MARGIN + off + start : MARGIN + off + start + STEP, :]
            part = weights[2 - a][2 - b] * window
            total = part if total is None else total + part
            at = 3 * (2 - a) + 2 - b
            prod = jnp.sum((given * window).reshape(STEP // 8, 8, LANES), axis=0)
            sums[at] = prod if sums[at] is None else sums[at] + prod
        write(run_rows(g, start), total)

    def last():
        write_sums(jnp.concatenate([col_sum(v) for v in sums], axis=0))

    return [step(one, *at) for at in runs()] + [last]


def lanes_at(start):
    return pl.ds(pl.multiple_of(start, LANES), LANES)


def attend_kernel(
    sc, p0, p1, p2, p3, cond, cond_right, weight, kernel,
    base_out, normed_out, qkv_out, conv_out, prob_out, mixed_out, mod,
    held,
):
    height, breadth, core = sc.height, sc.breadth, sc.core
    clear_margins(held)
    for k in range(6):
        cols = slice(768 * k, 768 * k + 768)
        mod[k : k + 1, :] = jnp.where(sc.stays, cond[:, cols].astype(F32), cond_right[:, cols].astype(F32))
    tokens = (height * breadth).astype(F32)
    mod[6:8, :] = jnp.full((2, 768), 1024.0, F32) / tokens
    shift, scale = mod[0:1, :], 1.0 + mod[1:2, :]
    matrix = to_phase_matrix()

    def norm(k, piece, g):
        start = pl.multiple_of(g * 256 + sc.pieces[k] * 64, 64)
        moved = dot(matrix[g * 64 : g * 64 + 64, :], piece[...])
        values = moved * live_run(start, height, breadth)
        base_out[pl.ds(start, 64), :] = values.astype(BF)
        normed_out[pl.ds(start, 64), :] = (normal(values)[0] * scale + shift).astype(BF)

    weave([step(norm, k, piece, g) for k, piece in enumerate((p0, p1, p2, p3)) for g in range(GROUPS)])

    def project(col, r):
        cols = slice(col, min(col + 256, 1152))
        qkv_out[r : r + 256, cols] = dot(normed_out[r : r + 256, :], weight[:, cols]).astype(BF)

    def project_steps(cols):
        return [step(project, col, r) for col in cols for r in range(0, 1024, 256)]

    def conv_pair(pair):
        steps = []
        for s in range(3):
            at = (3 * pair + s) * LANES
            cols = slice(at, at + LANES)

            def read(g, cols=cols):
                return qkv_out[g * 256 : g * 256 + 256, cols].astype(F32)

            def write(rows, total, cols=cols):
                conv_out[rows, cols] = total.astype(BF)

            steps += hold_steps(held, read)
            weights = taps_at(kernel, 768 * s + 384 * core + LANES * pair)
            steps += conv_steps(held, weights, write)
        return steps

    token = iota((1, 256), 1)
    lane = iota((256, LANES), 1)

    def attend_pair(pair):
        at = 3 * pair * LANES
        parts = {}

        def one(g, h):
            rows = slice(g * 256, g * 256 + 256)
            live = live_rows(token + g * 256, height, breadth) > 0.5
            query = conv_out[rows, at : at + LANES] * BF(HEAD_DIM**-0.5)
            key = conv_out[rows, at + LANES : at + 2 * LANES]
            value = conv_out[rows, at + 2 * LANES : at + 3 * LANES]
            mine = (lane < HEAD_DIM) if h == 0 else (lane >= HEAD_DIM)
            score = dot(jnp.where(mine, query, BF(0)), key, 1, 1)
            score = jnp.where(live, score, masked_score)
            top = jnp.max(score, axis=-1, keepdims=True)
            raised = jnp.exp(score - top)
            prob = (raised * (1.0 / jnp.sum(raised, axis=-1, keepdims=True))).astype(BF)
            prob_out[pair, g, h] = prob
            parts[h] = dot(prob, value)
            if h == 1:
                both = jnp.where(lane < HEAD_DIM, parts[0], parts[1])
                mixed_out[rows, pair * LANES : pair * LANES + LANES] = both.astype(BF)

        return [step(one, g, h) for g in range(GROUPS) for h in range(2)]

    weave(project_steps((0, 256)))
    weave(conv_pair(0), project_steps((512, 768, 1024)))
    weave(attend_pair(0), conv_pair(1))
    weave(attend_pair(1), conv_pair(2))
    weave(attend_pair(2))


def attend(line, pieces, cond, cond_right, weight, attn_kernel):
    return run(
        attend_kernel, "attend", line, (*pieces, cond, cond_right, weight, attn_kernel),
        [shaped(1024, 768), shaped(1024, 768), shaped(1024, 1152), shaped(1024, 1152),
         shaped(3, GROUPS, 2, 256, 256), shaped(1024, 384), shaped(8, 768, dtype=F32)],
        [HELD], items=True, us=11.5
    )


def middle_kernel(
    sc, mixed_own, mixed_other, base, out_weight, mod, seeds, seeds_other,
    attended_out, normed_out, branch_grad_out, seed_out,
    mixed, attended,
):
    height, breadth, core = sc.height, sc.breadth, sc.core
    mixed[:, pl.ds(pl.multiple_of(core * 384, LANES), 384)] = mixed_own[...]
    mixed[:, pl.ds(pl.multiple_of((1 - core) * 384, LANES), 384)] = mixed_other[...]
    gate = mod[2:3, :]
    shift, scale = mod[3:4, :], 1.0 + mod[4:5, :]
    gate_two, factor = mod[5:6, :], mod[6:7, :]
    matrix = to_phase_matrix()

    def project(r):
        attended[r : r + 256, :] = dot(mixed[r : r + 256, :], out_weight[...])

    def norm(r):
        rows = slice(r, r + 64)
        got = attended[rows, :].astype(BF)
        attended_out[rows, :] = got
        middle = base[rows, :].astype(F32) + gate * got.astype(F32)
        normed_out[rows, :] = (normal(middle)[0] * scale + shift).astype(BF)

    def seed(k, piece, g):
        start = pl.multiple_of(g * 256 + sc.pieces[k] * 64, 64)
        moved = dot(matrix[g * 64 : g * 64 + 64, :], piece[256 * (k % 2) : 256 * (k % 2) + 256, :])
        values = moved * live_run(start, height, breadth)
        seed_out[pl.ds(start, 64), :] = values.astype(BF)
        branch_grad_out[pl.ds(start, 64), :] = (values * factor * gate_two).astype(BF)

    project(0)
    weave([step(project, r) for r in (256, 512, 768)], [step(norm, r) for r in range(0, 768, 64)],
          [step(seed, k, piece, g) for k, piece in enumerate((seeds, seeds, seeds_other, seeds_other))
           for g in range(GROUPS)])
    weave([step(norm, r) for r in range(768, 1024, 64)])


def project_out(sc, mixed_own, mixed_other, base, out_weight, mod, pieces):
    return run(
        middle_kernel, "project_out", sc, (mixed_own, mixed_other, base, out_weight, mod, *pieces),
        [shaped(1024, 768)] * 4,
        [pltpu.VMEM((1024, 768), BF), pltpu.VMEM((1024, 768), F32)], items=True, us=4.6
    )


BLOCK = 256


def keep_half(core, values, local):
    low = values[128 * local : 128 * local + 64, :]
    high = values[128 * local + 64 : 128 * local + 128, :]
    return jnp.where(core == 0, low, high), jnp.where(core == 0, high, low)


def gelu_parts(v):
    square = v * v
    bent = jnp.tanh(v * (gelu_root + (gelu_root * gelu_cube) * square))
    rise = 0.5 + 0.5 * bent
    value = v * rise
    slope = rise + value * (1.0 - bent) * (gelu_root + (3.0 * gelu_root * gelu_cube) * square)
    return value, slope


def feed_kernel(sc, normed, branch_grad, up, down, kernel, keep, send, acts, hid, d_conv, held, d_act):
    clear_margins(held)

    def project_steps(k):
        cols = slice(k * BLOCK, (k + 1) * BLOCK)
        place = k % 2

        def one(r):
            hid[r : r + 256, cols] = dot(normed[r : r + 256, :], up[:, cols]).astype(BF)

        def two(r):
            d_act[place, r : r + 256, :] = dot(branch_grad[r : r + 256, :], down[cols, :], 1, 1)

        return [step(f, r) for r in range(0, 1024, 256) for f in (one, two)]

    def local_steps(k):
        steps = []
        place = k % 2
        for lane_block in range(BLOCK // LANES):
            cols = slice(lane_block * LANES, (lane_block + 1) * LANES)
            at = k * BLOCK + lane_block * LANES
            dest = slice(at, at + LANES)

            def read(g, dest=dest):
                return hid[g * 256 : g * 256 + 256, dest].astype(F32)

            def activate(rows, v, cols=cols, dest=dest):
                value, slope = gelu_parts(v)
                acts[rows, dest] = value.astype(BF)
                d_conv[rows, dest] = (d_act[place, rows, cols] * slope).astype(BF)

            steps += hold_steps(held, read)
            steps += conv_steps(held, taps_at(kernel, sc.core * 1536 + at), activate)
        return steps

    def down_steps():
        def one(place, out, r, c):
            rows = pl.ds(pl.multiple_of(place * 768 + r, 256), 256)
            out[r : r + 256, c : c + 256] = dot(acts[:, rows], branch_grad[:, c : c + 256], 0, 0).astype(BF)

        return [
            step(one, place, out, r, c)
            for place, out in ((1 - sc.bits[0], send), (sc.bits[0], keep))
            for r in range(0, 768, 256)
            for c in range(0, 768, 256)
        ]

    weave(project_steps(0))
    for k in range(5):
        weave(local_steps(k), project_steps(k + 1))
    weave(local_steps(5))
    weave(down_steps())


def feed(line, normed, branch_grad, up, down, ffn_kernel):
    return run(
        feed_kernel, "feed", line, (normed, branch_grad, up, down, ffn_kernel),
        [shaped(768, 768), shaped(768, 768), shaped(1024, 1536), shaped(1024, 1536), shaped(1024, 1536)],
        [HELD, pltpu.VMEM((2, 1024, BLOCK), F32)], limit=18 * 1024 * 1024, us=13.0,
    )


def feed_back_kernel(
    sc, normed, up, down, kernel, acts, hid, d_conv,
    keep, send, kernel_grad, branch_keep, branch_send, normed_grad_out, held, d_hids,
):
    core = sc.core
    clear_margins(held)

    def local_steps(at):
        cols = slice(at, at + LANES)

        def write(rows, total):
            d_hids[rows, cols] = total.astype(BF)

        def write_sums(values):
            kernel_grad[:, cols] = values

        return hold_steps(held, lambda g: d_conv[g * 256 : g * 256 + 256, cols].astype(F32)) + back_steps(
            held, taps_at(kernel, core * 1536 + at), lambda rows: hid[rows, cols].astype(F32), write,
            write_sums,
        )

    def up_steps(k):
        cols = slice(k * BLOCK, (k + 1) * BLOCK)

        def one(pair, out):
            at = pl.ds(pl.multiple_of(pair * 384, 384), 384)
            out[:, cols] = dot(normed[:, at], d_hids[:, cols], 0, 0).astype(BF)

        return [step(one, 1 - sc.bits[0], send), step(one, sc.bits[0], keep)]

    def branch_steps():
        def one(g):
            total = dot(acts[g * 256 : g * 256 + 256, :], down[...])
            for local in range(2):
                kept, sent = keep_half(core, total, local)
                branch_keep[2 * g + local] = kept
                branch_send[2 * g + local] = sent.astype(BF)

        return [step(one, g) for g in range(GROUPS)]

    branch = branch_steps()
    for k in range(6):
        weave(
            local_steps(k * BLOCK) + local_steps(k * BLOCK + LANES),
            (up_steps(k - 1) if k else []) + branch[k : k + 1],
        )
    weave(up_steps(5))
    for r in range(0, 1024, 256):
        normed_grad_out[r : r + 256, :] = dot(d_hids[r : r + 256, :], up[...], 1, 1).astype(BF)


def feed_back(line, normed, up, down, ffn_kernel, acts, hid, d_conv):
    return run(
        feed_back_kernel, "feed_back", line, (normed, up, down, ffn_kernel, acts, hid, d_conv),
        [shaped(384, 1536), shaped(384, 1536), shaped(9, 1536, dtype=F32), shaped(8, 64, 768, dtype=F32),
         shaped(8, 64, 768), shaped(1024, 768)],
        [HELD, pltpu.VMEM((1024, 1536), BF)], limit=18 * 1024 * 1024, us=14.0,
    )


def put_pieces(sc, done, near_out, far_out):
    @pl.when(sc.pair == 0)
    def _():
        near_out[...] = done[0]
        far_out[...] = done[1]

    @pl.when(sc.pair != 0)
    def _():
        near_out[...] = done[1]
        far_out[...] = done[0]


def finish_kernel(sc, base, attended, branch, branch_other, seed, mod, near_out, far_out, sums_out):
    height, breadth, core = sc.height, sc.breadth, sc.core
    gate_one, gate, factor = mod[2:3, :], mod[5:6, :], mod[6:7, :]
    matrix = to_phase_matrix()
    total = jnp.zeros((1, 768), F32)
    done = []
    for local in range(2):
        parts = []
        for g in range(GROUPS):
            start = pl.multiple_of(g * 256 + (2 * local + core) * 64, 64)
            rows = pl.ds(start, 64)
            whole = branch[2 * g + local] + branch_other[8 + 2 * g + local].astype(F32)
            total = total + col_sum(seed[rows, :].astype(F32) * whole)
            middle = base[rows, :].astype(F32) + gate_one * attended[rows, :].astype(F32)
            result = middle + gate * whole
            parts.append((result * live_run(start, height, breadth)).astype(BF))
        done.append(dot(matrix, jnp.concatenate(parts, axis=0), 0, 0).astype(BF))
    put_pieces(sc, done, near_out, far_out)
    sums_out[...] = total * factor


def finish(sc, base, attended, branch, branch_other, seed, mod):
    return run(
        finish_kernel, "finish", sc, (base, attended, branch, branch_other, seed, mod),
        [shaped(256, 768), shaped(256, 768), shaped(1, 768, dtype=F32)], items=True, us=1.8
    )


def norm_back_kernel(
    sc, normed_grad, normed_grad_other, base, attended, seed, mod, mixed,
    middle_grad, att_grad, sums_out, out_keep, out_send,
):
    gate, scale, factor = mod[2:3, :], 1.0 + mod[4:5, :], mod[6:7, :]
    sums = [jnp.zeros((1, 768), F32) for _ in range(3)]

    def norm(r):
        rows = slice(r, r + 64)
        grad = normed_grad[rows, :].astype(F32) + normed_grad_other[rows, :].astype(F32)
        got = attended[rows, :].astype(F32)
        unit, inverse = normal(base[rows, :].astype(F32) + gate * got)
        both = grad * unit
        sums[0] = sums[0] + col_sum(grad)
        sums[1] = sums[1] + col_sum(both)
        grad = grad * scale
        mean = jnp.mean(grad, axis=-1, keepdims=True)
        along = jnp.mean(both * scale, axis=-1, keepdims=True)
        total = seed[rows, :].astype(F32) * factor + inverse * (grad - mean - unit * along)
        middle_grad[rows, :] = total
        sums[2] = sums[2] + col_sum(total * got)
        att_grad[rows, :] = (total * gate).astype(BF)

    for r in range(0, 1024, 64):
        norm(r)
    for k in range(3):
        sums_out[k : k + 1, :] = 0.5 * sums[k]
    for place, out in ((sc.bits[0], out_keep), (1 - sc.bits[0], out_send)):
        cols = pl.ds(pl.multiple_of(place * 384, 384), 384)
        out[...] = dot(mixed[...], att_grad[:, cols], 0, 0).astype(BF)


def norm_back(sc, normed_grad, normed_grad_other, base, attended, seed, mod, mixed):
    return run(
        norm_back_kernel, "norm_back", sc,
        (normed_grad, normed_grad_other, base, attended, seed, mod, mixed),
        [shaped(1024, 768, dtype=F32), shaped(1024, 768), shaped(3, 768, dtype=F32),
         shaped(384, 384), shaped(384, 384)], us=4.4
    )


def attend_back_kernel(
    heads, sc, att_grad, out_weight, normed, qkv, conv, prob, kernel, *rest,
):
    (*before, qkv_grad, kernel_grad, weight_keep, weight_send, held, d_mixed, d_conv) = rest
    for given, out in zip(before, (weight_keep, weight_send)):
        out[:, 384:768] = given[...]
    core = sc.core
    at = 3 * heads * LANES
    clear_margins(held)
    mine_rows = slice(heads * LANES, heads * LANES + LANES)
    for r in range(0, 1024, 256):
        d_mixed[r : r + 256, :] = dot(att_grad[r : r + 256, :], out_weight[mine_rows, :], 1, 1).astype(BF)

    lane = iota((256, LANES), 1)
    low = lane < HEAD_DIM
    parts = {}

    def one(g, h):
        rows = slice(g * 256, g * 256 + 256)
        grad = d_mixed[rows, :]
        query = conv[rows, at : at + LANES]
        key = conv[rows, at + LANES : at + 2 * LANES]
        value = conv[rows, at + 2 * LANES : at + 3 * LANES]
        mine = low if h == 0 else jnp.logical_not(low)
        p = prob[heads, g, h]
        d_value = dot(p, grad, 0, 0)
        d_prob = dot(jnp.where(mine, grad, BF(0)), value, 1, 1)
        wide_p = p.astype(F32)
        inner = jnp.sum(d_prob * wide_p, axis=-1, keepdims=True)
        d_score = (wide_p * (d_prob - inner)).astype(BF)
        parts[h] = (dot(d_score, key), dot(d_score, query, 0, 0), d_value)
        if h == 1:
            for k in range(3):
                picked = jnp.where(low, parts[0][k], parts[1][k])
                if k < 2:
                    picked = picked * HEAD_DIM**-0.5
                d_conv[rows, k * LANES : (k + 1) * LANES] = picked.astype(BF)

    def local_steps(s):
        cols = slice(s * LANES, (s + 1) * LANES)
        source_cols = slice(at + s * LANES, at + (s + 1) * LANES)

        def write(rows, total):
            qkv_grad[rows, cols] = total.astype(BF)

        def write_sums(values):
            kernel_grad[:, cols] = values

        weights = taps_at(kernel, 768 * s + 384 * core + LANES * heads)
        return hold_steps(
            held, lambda g: d_conv[g * 256 : g * 256 + 256, cols].astype(F32)
        ) + back_steps(held, weights, lambda rows: qkv[rows, source_cols].astype(F32), write, write_sums)

    weave([step(one, g, h) for g in range(GROUPS) for h in range(2)])
    for s in range(3):
        weave(local_steps(s))
    for place, out in ((sc.bits[0], weight_keep), (1 - sc.bits[0], weight_send)):
        rows = pl.ds(pl.multiple_of(place * 384, 384), 384)
        out[:, 0:384] = dot(normed[:, rows], qkv_grad[...], 0, 0).astype(BF)


def attend_back(sc, heads, att_grad, out_weight, normed, qkv, conv, prob, attn_kernel, before=()):
    return run(
        functools.partial(attend_back_kernel, heads), "attend_back", sc,
        (att_grad, out_weight, normed, qkv, conv, prob, attn_kernel, *before),
        [shaped(1024, 384), shaped(9, 384, dtype=F32)] + [shaped(384, 768 if before else 384)] * 2,
        [HELD, pltpu.VMEM((1024, LANES), BF), pltpu.VMEM((1024, 384), BF)], us=6.3
    )


def first_back_kernel(sc, g0, g1, g2, weight, branch, keep, send):
    core = sc.core
    send[8:16] = branch[...]
    for g in range(GROUPS):
        rows = slice(g * 256, g * 256 + 256)
        total = None
        for k, grad in enumerate((g0, g1, g2)):
            part = dot(grad[rows, :], weight[:, 384 * k : 384 * k + 384], 1, 1)
            total = part if total is None else total + part
        for local in range(2):
            kept, sent = keep_half(core, total, local)
            keep[2 * g + local] = kept
            send[2 * g + local] = sent.astype(BF)


def first_back(line, grads, weight, branch):
    return run(
        first_back_kernel, "first_back", line, (*grads, weight, branch),
        [shaped(8, 64, 768, dtype=F32), shaped(16, 64, 768)], us=2.7
    )


def input_kernel(sc, grad, grad_other, middle_grad, base, mod, near_out, far_out, sums_out):
    height, breadth, core = sc.height, sc.breadth, sc.core
    scale = 1.0 + mod[1:2, :]
    matrix = to_phase_matrix()
    d_shift = jnp.zeros((1, 768), F32)
    d_scale = jnp.zeros((1, 768), F32)
    done = []
    for local in range(2):
        parts = []
        for g in range(GROUPS):
            at = 2 * g + local
            start = pl.multiple_of(g * 256 + (2 * local + core) * 64, 64)
            rows = pl.ds(start, 64)
            total = grad[at] + grad_other[at].astype(F32)
            unit, inverse = normal(base[rows, :].astype(F32))
            both = total * unit
            d_shift = d_shift + col_sum(total)
            d_scale = d_scale + col_sum(both)
            total = total * scale
            mean = jnp.mean(total, axis=-1, keepdims=True)
            along = jnp.mean(both * scale, axis=-1, keepdims=True)
            total = middle_grad[rows, :] + inverse * (total - mean - unit * along)
            parts.append((total * live_run(start, height, breadth)).astype(BF))
        done.append(dot(matrix, jnp.concatenate(parts, axis=0), 0, 0).astype(BF))
    put_pieces(sc, done, near_out, far_out)
    sums_out[0:1, :] = d_shift
    sums_out[1:2, :] = d_scale


def input_grad(sc, grad, grad_other, middle_grad, base, mod):
    return run(
        input_kernel, "input_grad", sc, (grad, grad_other, middle_grad, base, mod),
        [shaped(256, 768), shaped(256, 768), shaped(2, 768, dtype=F32)], items=True, us=2.6
    )


def swap(values, axis, bit):
    count = lax.axis_size(axis)
    return lax.ppermute(values, axis, [(i, i ^ bit) for i in range(count)])


def swap_at(values, k):
    wide, narrow = lax.axis_size("wide"), lax.axis_size("narrow")
    steps = {"x": (0, 2), "y": (1, 0), "z": (2, 0), "w": (4, 0)}
    pairs = []
    for w in range(wide):
        for n in range(narrow):
            dw, dn = steps[HALVINGS[n % 2][k]]
            pairs.append((w * narrow + n, (w ^ dw) * narrow + (n ^ dn)))
    return lax.ppermute(values, ("wide", "narrow"), pairs)


def bits_of(count):
    return [1 << k for k in range(count.bit_length() - 1)]


def halve_kernel(k, sc, kept, got, *rest):
    if len(rest) > 2:
        given, *rest, passed = rest
        passed[...] = given[...]
    half = kept.shape[0] // 2
    for d, out in enumerate(rest):
        rows = pl.ds(pl.multiple_of((sc.bits[k] ^ d) * half, 16), half)
        out[...] = (kept[rows, :].astype(F32) + got[rows, :].astype(F32)).astype(BF)


def total_kernel(sc, kept, got, out):
    out[...] = (kept[...].astype(F32) + got[...].astype(F32)).astype(BF)


def stack_kernel(sc, kept, got, out):
    half = kept.shape[0]
    out[0:half, :] = kept[...]
    out[half : 2 * half, :] = got[...]


class Flow:
    def __init__(self, line, keep, send):
        self.line = line
        for bit in bits_of(lax.axis_size("wide"))[3:]:
            keep, send = [
                (v.astype(F32) + swap(v, "wide", bit).astype(F32)).astype(BF) for v in (keep, send)
            ]
        self.kept, self.got = keep, swap_at(send, 0)

    def halve(self, k, *given):
        rows, width = self.kept.shape
        self.kept, send, *passed = run(
            functools.partial(halve_kernel, k), "halve", self.line, (self.kept, self.got, *given),
            [shaped(rows // 2, width)] * 2 + [shaped(*v.shape) for v in given],
        )
        self.got = swap_at(send, k)
        return passed

    def total(self):
        (self.kept,) = run(
            total_kernel, "total", self.line, (self.kept, self.got), [shaped(*self.kept.shape)]
        )
        self.got = swap_at(self.kept, 3)

    def stack(self, k):
        rows, width = self.kept.shape
        (self.kept,) = run(
            stack_kernel, "stack", self.line, (self.kept, self.got), [shaped(2 * rows, width)]
        )
        self.got = swap_at(self.kept, k - 1) if k else swap(self.kept, "narrow", 1)


def by_core(core, write, own, other):
    @pl.when(core == 0)
    def _():
        write(own, other)

    @pl.when(core != 0)
    def _():
        write(other, own)


def row_runs(chip, rows):
    for i in range(16):
        yield slice(rows * i, rows * i + rows), (i ^ chip)


def leave(buffers, outs, sems):
    return [pltpu.make_async_copy(src, dst, sems.at[k]) for k, (src, dst) in enumerate(zip(buffers, outs))]


def down_done_kernel(sc, own, other, out, buffer, sems):
    copies = leave([buffer.at[k] for k in range(2)], [out.at[sc.core], out.at[1 - sc.core]], sems)
    for k, (part, chip) in enumerate(((own, sc.chip), (other, sc.other_chip))):
        for rows, place in row_runs(chip, 96):
            buffer[k, pl.ds(pl.multiple_of(place * 96, 32), 96), :] = part[rows, :].astype(F32)
        copies[k].start()
    for copy in copies:
        copy.wait()


def down_done(line, flow):
    (out,) = run(
        down_done_kernel, "down_done", line, (flow.kept, flow.got), [shaped(2, 1536, 768, dtype=F32)],
        [pltpu.VMEM((2, 1536, 768), F32), pltpu.SemaphoreType.DMA((2,))], far_outs=True,
        limit=12 * 1024 * 1024, us=4.0,
    )
    return out.reshape(3072, 768)


def up_done_kernel(sc, own, other, out, buffer, sems):
    def at(core):
        return out.at[:, pl.ds(pl.multiple_of(core * 1536, 1536), 1536)]

    copies = leave([buffer.at[k] for k in range(2)], [at(sc.core), at(1 - sc.core)], sems)
    for k, (part, chip) in enumerate(((own, sc.chip), (other, sc.other_chip))):
        for rows, place in row_runs(chip, 48):
            buffer[k, pl.ds(pl.multiple_of(place * 48, 16), 48), :] = part[rows, :].astype(F32)
        copies[k].start()
    for copy in copies:
        copy.wait()


def up_done(line, flow):
    (out,) = run(
        up_done_kernel, "up_done", line, (flow.kept, flow.got), [shaped(768, 3072, dtype=F32)],
        [pltpu.VMEM((2, 768, 1536), F32), pltpu.SemaphoreType.DMA((2,))], far_outs=True,
        limit=12 * 1024 * 1024, us=4.0,
    )
    return out


def attend_done_kernel(sc, c, d, c_other, d_other, qkv_grad, out_grad, qkv, out, sems):
    copies = leave(
        [qkv.at[k] for k in range(6)] + [out.at[k] for k in range(2)],
        [
            qkv_grad.at[:, pl.ds(pl.multiple_of(768 * s + 384 * core, LANES), 384)]
            for core in (sc.core, 1 - sc.core)
            for s in range(3)
        ]
        + [out_grad.at[core] for core in (sc.core, 1 - sc.core)],
        sems,
    )
    for k, (one, two, chip) in enumerate(((c, d, sc.chip), (c_other, d_other, sc.other_chip))):
        for rows, place in row_runs(chip, 48):
            dest = pl.ds(pl.multiple_of(place * 48, 16), 48)
            for s in range(3):
                for at, (part, col) in enumerate(((one, 0), (two, 384), (two, 0))):
                    col = col + LANES * s
                    qkv[3 * k + s, dest, LANES * at : LANES * at + LANES] = part[
                        rows, col : col + LANES
                    ].astype(F32)
            dest = pl.ds(pl.multiple_of((place & 7) * 48, 16), 48)
            cols = pl.ds(pl.multiple_of((place >> 3) * 384, LANES), 384)
            out[k, dest, cols] = one[rows, 384:768].astype(F32)
        for copy in (*copies[3 * k : 3 * k + 3], copies[6 + k]):
            copy.start()
    for copy in copies:
        copy.wait()


def attend_done(line, c, d):
    qkv_grad, out_grad = run(
        attend_done_kernel, "attend_done", line, (c.kept, d.kept, c.got, d.got),
        [shaped(768, 2304, dtype=F32), shaped(2, 384, 768, dtype=F32)],
        [pltpu.VMEM((6, 768, 384), F32), pltpu.VMEM((2, 384, 768), F32), pltpu.SemaphoreType.DMA((8,))],
        far_outs=True, limit=14 * 1024 * 1024, us=4.0,
    )
    return qkv_grad, out_grad.reshape(768, 768)


def join_kernel(sc, near, far, out):
    out[sc.pair] = near[...]
    out[1 - sc.pair] = far[...]


def join(line, near, far):
    (out,) = run(join_kernel, "join", line, (near, far), [shaped(2, 256, 768)])
    return out.reshape(2, 8, 32, 768)


def cond_kernel(sc, sums_one, sums_two, d_gate_two, stay, move):
    rows = jnp.concatenate(
        [sums_one[...], sums_two[2:3, :], sums_two[1:2, :], d_gate_two[...], sums_two[0:1, :],
         jnp.zeros((2, 768), F32)], axis=0
    )
    stays = sc.stays.astype(F32)
    stay[...] = rows * stays
    move[...] = rows * (1.0 - stays)


def small_kernel(sc, stay, moved, *refs):
    *parts, out = refs
    out[...] = jnp.zeros(out.shape, F32)
    out[16:24, 0:768] = stay[...] + moved[...]
    at = 0
    for part in parts:
        width = part.shape[1]
        out[0:9, at : at + width] = part[...]
        at += width


def add_first_kernel(sc, own, other, out, cond):
    total = own[...] + other[...]
    out[...] = total
    cond[...] = total[16:24, 0:768]


def add_kernel(sc, own, other, out):
    out[...] = own[...] + other[...]


def add_last_kernel(sc, own, other, cond, out):
    out[0:16, :] = own[0:16, :] + other[0:16, :]
    out[16:24, 0:768] = cond[...]
    out[16:24, 768:2688] = jnp.zeros((8, 1920), F32)


def small_done_kernel(sc, own, other, cond_out, shift_out, ffn_out, attn_out):
    total = own[16:24, 0:768] + other[16:24, 0:768]
    for k in range(5):
        cond_out[:, 768 * k : 768 * k + 768] = total[k : k + 1, :]
    shift_out[...] = total[5:6, :]

    def write(first, second):
        for core, part in enumerate((first, second)):
            for a in range(3):
                ffn_out[a, :, 1536 * core : 1536 * core + 1536] = part[3 * a : 3 * a + 3, 0:1536]
                for pair in range(3):
                    for s in range(3):
                        to = 768 * s + 384 * core + LANES * pair
                        col = 1536 + (3 * pair + s) * LANES
                        attn_out[a, :, to : to + LANES] = part[3 * a : 3 * a + 3, col : col + LANES]

    by_core(sc.core, write, own, other)


def copy_all(sems, pairs):
    copies = [pltpu.make_async_copy(src, dst, sems.at[k]) for k, (src, dst) in enumerate(pairs)]
    for copy in copies:
        copy.start()
    for copy in copies:
        copy.wait()


def cut_pieces_kernel(sc, block, far, own, sems):
    copy_all(sems, [(block.at[1 - sc.pair], far), (block.at[sc.pair], own)])


def cut_pieces(line, block):
    return run(
        cut_pieces_kernel, "cut_pieces", line, (block.reshape(2, 256, 768),), [shaped(256, 768)] * 2,
        [pltpu.SemaphoreType.DMA((2,))], far=(0,), limit=ALL_VMEM,
    )


def pass_kernel(sc, *refs):
    count = len(refs) // 2
    for k in range(count):
        refs[count + k][...] = refs[k][...]


def pass_on(line, *arrays):
    return run(pass_kernel, "pass_on", line, arrays, [shaped(*v.shape) for v in arrays])


def pack_kernel(sc, one, two, out):
    out[0:256, :] = one[...]
    out[256:512, :] = two[...]


def cut_weights_kernel(sc, qkv, out, up, down, qkv_part, out_part, up_part, down_part, sems):
    core = sc.core
    pairs = [
        (
            qkv.at[:, lanes_at(768 * s + 384 * core + LANES * pair)],
            qkv_part.at[:, pl.ds((3 * pair + s) * LANES, LANES)],
        )
        for pair in range(3)
        for s in range(3)
    ]
    pairs += [
        (out.at[pl.ds(pl.multiple_of(384 * core, 384), 384), :], out_part),
        (up.at[:, pl.ds(pl.multiple_of(1536 * core, 1536), 1536)], up_part),
        (down.at[pl.ds(pl.multiple_of(1536 * core, 1536), 1536), :], down_part),
    ]
    copy_all(sems, pairs)


def cut_weights(line, qkv_weight, out_weight, up_weight, down_weight):
    return run(
        cut_weights_kernel, "cut_weights", line, (qkv_weight, out_weight, up_weight, down_weight),
        [shaped(768, 1152), shaped(384, 768), shaped(768, 1536), shaped(1536, 768)],
        [pltpu.SemaphoreType.DMA((12,))], far=(0, 1, 2, 3), limit=ALL_VMEM, us=2.5
    )


ORDER = (
    "F_a", "F_b", "h2a", "N", "A0", "h3a", "A1", "h2b", "h4a", "A2",
    "h2c", "h3b", "fb", "tota", "h3c", "h4b", "h2d", "h4c", "s1a", "inp",
    "s2a", "h3d", "totc", "totb", "finish", "s1c", "s3a", "cond", "h4d", "s1b",
    "join2", "totd", "s2c", "small", "s2b", "add1", "s3b", "s1d", "s4a", "add2",
    "down_done", "s2d", "s3c", "add3", "s4b", "join1", "s3d", "up_done", "s4c", "add4",
    "s4d", "small_done", "attend_done",
)


def on_device(
    tokens, cotangent, conditioning, aspect, bucket,
    qkv_weight, attn_kernel, out_weight, up_weight, ffn_kernel, down_weight,
):
    wide_count = lax.axis_size("wide")
    line = Line(aspect, bucket)
    far, own = cut_pieces(line, tokens)
    got = swap(far, "narrow", 2)
    own_other = swap(own, "narrow", 1)
    cond_right = lax.ppermute(conditioning, "wide", [(i + 1, i) for i in range(wide_count - 1)])
    weights = cut_weights(line, qkv_weight, out_weight, up_weight, down_weight)
    qkv_part, out_part, up_part, down_part = weights
    seed_far, seed_own = cut_pieces(line, cotangent)
    got, cond_right = pass_on(line, got, cond_right)
    token_pieces = own, got, own_other, swap(got, "narrow", 1)
    base, normed_one, qkv, conv, prob, mixed, mod = attend(
        line, token_pieces, conditioning, cond_right, qkv_part, attn_kernel
    )
    (seeds,) = run(pack_kernel, "pack", line, (seed_own, swap(seed_far, "narrow", 2)), [shaped(512, 768)])
    mixed_other = swap(mixed, "narrow", 1)
    seed_pieces = seeds, swap(seeds, "narrow", 1)
    attended, normed_two, d_branch, seed = project_out(
        line, mixed, mixed_other, base, out_weight, mod, seed_pieces
    )

    made = {}
    flows = {}

    def do_feed():
        keep, send, *made["saved"] = feed(line, normed_two, d_branch, up_part, down_part, ffn_kernel)
        flows["a"] = Flow(line, keep, send)

    def do_feed_back():
        keep, send, made["ffn"], made["branch"], made["branch_send"], made["d_normed"] = feed_back(
            line, normed_two, up_part, down_part, ffn_kernel, *made["saved"]
        )
        flows["b"] = Flow(line, keep, send)

    def do_norm_back():
        (passed,) = made["passed_a"]
        made["d_middle"], made["d_att"], made["sums_two"], *made["out"] = norm_back(
            line, made["d_normed"], swap(passed, "narrow", 1), base, attended, seed, mod, mixed
        )

    def do_attend_back(heads, before, flow):
        grad, taps_grad, *parts = attend_back(
            line, heads, made["d_att"], out_part, normed_one, qkv, conv, prob, attn_kernel,
            made[before] if before else (),
        )
        made["g", heads], made["taps", heads], made["parts", heads] = grad, taps_grad, parts
        if flow:
            flows[flow] = Flow(line, *parts)

    def do_first_back():
        made["d_first"], made["first_send"] = first_back(
            line, [made["g", heads] for heads in range(3)], qkv_part, made["branch_send"]
        )

    def do_halve(name, k, given=None):
        made["passed_" + name] = flows[name].halve(k, *(() if given is None else (made[given],)))
        if given == "first_send":
            made["first_other"] = swap(made["passed_" + name][0], "narrow", 1)

    def do_finish():
        made["near"], far, made["d_gate_two"] = finish(
            line, base, attended, made["branch"], made["first_other"], seed, mod
        )
        made["far"] = swap(far, "narrow", 2)

    def do_input():
        made["near_grad"], far, made["sums_one"] = input_grad(
            line, made["d_first"], made["first_other"], made["d_middle"], base, mod
        )
        made["far_grad"] = swap(far, "narrow", 2)

    def do_join(name, near, far):
        made[name] = join(line, made[near], made[far])

    def do_cond():
        made["cond"], move = run(
            cond_kernel, "cond", line, (made["sums_one"], made["sums_two"], made["d_gate_two"]),
            [shaped(8, 768, dtype=F32)] * 2, items=True,
        )
        made["moved"] = lax.ppermute(move, "wide", [(i, i + 1) for i in range(wide_count - 1)])

    small_shape = shaped(24, 2688, dtype=F32)

    def do_small():
        parts = made["ffn"], *(made["taps", heads] for heads in range(3))
        (total,) = run(small_kernel, "small", line, (made["cond"], made["moved"], *parts), [small_shape])
        made["small"] = total, swap(total, "narrow", 2)

    def do_add_first():
        total, made["cond"] = run(
            add_first_kernel, "add_first", line, made["small"], [small_shape, shaped(8, 768, dtype=F32)]
        )
        made["small"] = total, swap(total, "wide", 1)

    def do_add(bit):
        (total,) = run(add_kernel, "add", line, made["small"], [small_shape])
        made["small"] = total, swap(total, "wide", bit)

    def do_add_last():
        for bit in bits_of(wide_count)[3:]:
            do_add(bit)
        (total,) = run(add_last_kernel, "add_last", line, (*made["small"], made["cond"]), [small_shape])
        made["small"] = total, swap(total, "narrow", 1)

    def do_small_done():
        made["small_out"] = run(
            small_done_kernel, "small_done", line, made["small"],
            [shaped(1, 3840, dtype=F32), shaped(1, 768, dtype=F32), shaped(3, 3, 3072, dtype=F32),
             shaped(3, 3, 2304, dtype=F32)],
        )

    def do_down():
        made["down_grad"] = down_done(line, flows["a"])

    def do_up():
        made["up_grad"] = up_done(line, flows["b"])

    def do_attend_done():
        made["qkv_grad"], made["out_grad"] = attend_done(line, flows["c"], flows["d"])

    tasks = {
        "F_a": do_feed, "F_b": do_feed_back, "N": do_norm_back,
        "A0": step(do_attend_back, 0, "out", "c"), "A1": step(do_attend_back, 1, None, None),
        "A2": step(do_attend_back, 2, ("parts", 1), "d"), "fb": do_first_back,
        "finish": do_finish, "inp": do_input,
        "join1": step(do_join, "block_out", "near", "far"),
        "join2": step(do_join, "tokens_grad", "near_grad", "far_grad"),
        "cond": do_cond, "small": do_small, "add1": do_add_first, "add2": step(do_add, 2),
        "add3": step(do_add, 4), "add4": do_add_last, "small_done": do_small_done,
        "down_done": do_down, "up_done": do_up, "attend_done": do_attend_done,
    }
    for name in "abcd":
        given = {"a": "d_normed", "d": "first_send"}.get(name)
        tasks["h2" + name] = step(do_halve, name, 1, given)
        tasks["h3" + name] = step(do_halve, name, 2)
        tasks["h4" + name] = step(do_halve, name, 3)
        tasks["tot" + name] = lambda name=name: flows[name].total()
        for k in range(4):
            tasks["s%d" % (k + 1) + name] = lambda name=name, k=k: flows[name].stack(3 - k)
    for name in ORDER:
        tasks[name]()

    cond_grad, shift_grad, ffn_grad, attn_grad = made["small_out"]
    return (
        made["block_out"], made["tokens_grad"], cond_grad, shift_grad, made["qkv_grad"], attn_grad,
        made["out_grad"], made["up_grad"], ffn_grad, made["down_grad"],
    )


def solution(mesh):
    rows = P("wide", "narrow", None, None)
    in_specs = (rows, rows, P("wide", None)) + (P(),) * 8
    out_specs = (rows, rows, P("wide", None), P("wide", None)) + (P(),) * 6
    return jax.shard_map(
        on_device, mesh=mesh, in_specs=in_specs, out_specs=out_specs, check_vma=False
    )
```

```python
import functools

import jax
import jax.numpy as jnp
from jax import lax
from jax.experimental import pallas as pl
from jax.experimental.pallas import tpu as pltpu
from jax.sharding import PartitionSpec as P

HEAD_DIM = 64
TAPS = 16
WIDE = "wide"
NARROW = "narrow"
LANES = 128
GROUPS = 4
MARGIN = 16

masked_score = -1000000000.0
norm_epsilon = 1e-06
gelu_root = 0.7978845608028654
gelu_cube = 0.044715

BF = jnp.bfloat16
F32 = jnp.float32
SCRATCH = 16 * 1024 * 1024
ALL_VMEM = 61 * 1024 * 1024
COST = 1150000000


def dot(left, right, left_dim=1, right_dim=0):
    return lax.dot_general(
        left, right, (((left_dim,), (right_dim,)), ((), ())), preferred_element_type=F32
    )


ANYWHERE = pl.BlockSpec(memory_space=pl.ANY)
DISTANT = pl.BlockSpec(memory_space=pltpu.HBM)
SCALARS = pl.BlockSpec(memory_space=pltpu.SMEM)
HERE = pl.BlockSpec(memory_space=pltpu.VMEM)


def shaped(*shape, dtype=BF):
    return jax.ShapeDtypeStruct(shape, dtype)


HALVINGS = ("x", "y", "z", "w"), ("y", "z", "x", "w")


class Place:
    def __init__(self, aspect=None, bucket=None):
        wide, narrow = lax.axis_index(WIDE), lax.axis_index(NARROW)
        self.wide = wide
        self.pair, self.core = narrow // 2, narrow % 2
        bits = {"x": self.pair, "y": wide % 2, "z": (wide // 2) % 2, "w": (wide // 4) % 2}
        self.bits = [
            jnp.where(self.core == 0, bits[first], bits[second]) for first, second in zip(*HALVINGS)
        ]
        self.chip = self.chip_of(self.bits)
        self.other_chip = self.chip_of(
            [jnp.where(self.core == 0, bits[second], bits[first]) for first, second in zip(*HALVINGS)]
        )
        self.pieces = (
            narrow, 2 * (1 - self.pair) + self.core, 2 * self.pair + 1 - self.core,
            2 * (1 - self.pair) + 1 - self.core,
        )
        if aspect is not None:
            item = 2 * wide + self.pair
            self.height, self.breadth = aspect[item, 0], aspect[item, 1]
            self.home = bucket[item]
            self.stays = self.home == wide

    def chip_of(self, bits):
        return 8 * bits[0] + 4 * bits[1] + 2 * bits[2] + bits[3]


class Line:
    def __init__(self, aspect, bucket):
        self.items = aspect, bucket
        self.token = None


def run(kernel, name, line, operands, outs, scratch=(), limit=SCRATCH, items=False, far=(), far_outs=(), us=1.0):
    count = len(operands)
    tokens = [] if line.token is None else [line.token]
    scalars = list(line.items) if items else []

    def body(*refs):
        place = Place(*refs[: len(scalars)])
        refs = refs[len(scalars) :]
        refs = refs[:count] + refs[count + len(tokens) :]
        refs[count + len(outs)][...] = jnp.zeros((8, LANES), F32)
        kernel(place, *refs[: count + len(outs)], *refs[count + len(outs) + 1 :])

    *made, line.token = pl.pallas_call(
        body,
        in_specs=[SCALARS] * len(scalars)
        + [DISTANT if k in far else HERE for k in range(count)]
        + [ANYWHERE] * len(tokens),
        out_specs=[DISTANT if k in far_outs else HERE for k in range(len(outs))] + [HERE],
        out_shape=[*outs, shaped(8, LANES, dtype=F32)],
        scratch_shapes=list(scratch),
        compiler_params=pltpu.CompilerParams(vmem_limit_bytes=limit),
        cost_estimate=pl.CostEstimate(flops=int(us * COST), bytes_accessed=1, transcendentals=0),
        name=name,
    )(*scalars, *operands, *tokens)
    return made


def step(f, *given):
    return functools.partial(f, *given)


def weave(*lists):
    order = sorted(
        ((at + 0.5) / len(steps), which, at)
        for which, steps in enumerate(lists)
        for at in range(len(steps))
    )
    for _, which, at in order:
        lists[which][at]()


def iota(shape, dim):
    return lax.broadcasted_iota(jnp.int32, shape, dim)


def live_rows(token, height, breadth):
    row = 2 * ((token >> 4) & 15) + (token >> 9)
    col = 2 * (token & 15) + ((token >> 8) & 1)
    return ((row < height) & (col < breadth)).astype(F32)


def live_run(start, height, breadth):
    return live_rows(start + iota((64, 1), 0), height, breadth)


def to_phase_matrix():
    row = iota((256, 256), 0)
    col = iota((256, 256), 1)
    grid_row = 2 * ((row >> 4) & 3) + (row >> 7)
    grid_col = 2 * (row & 15) + ((row >> 6) & 1)
    return (col == grid_row * 32 + grid_col).astype(F32).astype(BF)


def normal(values):
    center = values - jnp.mean(values, axis=-1, keepdims=True)
    scale = lax.rsqrt(jnp.mean(center * center, axis=-1, keepdims=True) + norm_epsilon)
    return center * scale, scale


def col_sum(values):
    return jnp.sum(values, axis=0, keepdims=True)


HELD = pltpu.VMEM((2 * GROUPS, 2 * MARGIN + 256, LANES), F32)
STEP = 64


def clear_margins(held):
    zero = jnp.zeros((2 * GROUPS, MARGIN, LANES), F32)
    held[:, 0:MARGIN, :] = zero
    held[:, MARGIN + 256 : 2 * MARGIN + 256, :] = zero


def hold_steps(held, read):
    place = iota((256, LANES), 0) & 15

    def one(g):
        values = read(g)
        held[2 * g, MARGIN : MARGIN + 256, :] = values
        if g % 2:
            moved = jnp.where(place == 0, 0.0, pltpu.roll(values, 1, 0))
        else:
            moved = jnp.where(place == 15, 0.0, pltpu.roll(values, 255, 0))
        held[2 * g + 1, MARGIN : MARGIN + 256, :] = moved

    return [step(one, g) for g in range(GROUPS)]


def taps(g):
    alpha, beta = g // 2, g % 2
    out = []
    for a in range(3):
        for b in range(3):
            row = alpha + a - 1
            col = beta + b - 1
            src = 2 * (row % 2) + col % 2
            out.append((a, b, 2 * src + (0 if 0 <= col <= 1 else 1), MARGIN * (row // 2)))
    return out


def tap_weights(kernel):
    return [[kernel[3 * a + b : 3 * a + b + 1, :] for b in range(3)] for a in range(3)]


def taps_at(kernel, start):
    cols = lanes_at(start)
    return jnp.concatenate([kernel[a, :, cols].astype(F32) for a in range(3)], axis=0)


def runs():
    return [(g, start) for g in range(GROUPS) for start in range(0, 256, STEP)]


def run_rows(g, start):
    return slice(g * 256 + start, g * 256 + start + STEP)


def conv_steps(held, kernel, write):
    weights = tap_weights(kernel)

    def one(g, start):
        total = None
        for a, b, src, off in taps(g):
            part = weights[a][b] * held[src, MARGIN + off + start : MARGIN + off + start + STEP, :]
            total = part if total is None else total + part
        write(run_rows(g, start), total)

    return [step(one, *at) for at in runs()]


def back_steps(held, kernel, read, write, write_sums):
    weights = tap_weights(kernel)
    sums = [None] * 9

    def one(g, start):
        given = read(run_rows(g, start))
        total = None
        for a, b, src, off in taps(g):
            window = held[src, MARGIN + off + start : MARGIN + off + start + STEP, :]
            part = weights[2 - a][2 - b] * window
            total = part if total is None else total + part
            at = 3 * (2 - a) + 2 - b
            prod = jnp.sum((given * window).reshape(STEP // 8, 8, LANES), axis=0)
            sums[at] = prod if sums[at] is None else sums[at] + prod
        write(run_rows(g, start), total)

    def last():
        write_sums(jnp.concatenate([col_sum(v) for v in sums], axis=0))

    return [step(one, *at) for at in runs()] + [last]


def lanes_at(start):
    return pl.ds(pl.multiple_of(start, LANES), LANES)


def attend_kernel(
    sc, p0, p1, p2, p3, cond, cond_right, weight, kernel,
    base_out, normed_out, qkv_out, conv_out, prob_out, mixed_out, mod,
    held,
):
    height, breadth, core = sc.height, sc.breadth, sc.core
    clear_margins(held)
    for k in range(6):
        cols = slice(768 * k, 768 * k + 768)
        mod[k : k + 1, :] = jnp.where(sc.stays, cond[:, cols].astype(F32), cond_right[:, cols].astype(F32))
    tokens = (height * breadth).astype(F32)
    mod[6:8, :] = jnp.full((2, 768), 1024.0, F32) / tokens
    shift, scale = mod[0:1, :], 1.0 + mod[1:2, :]
    matrix = to_phase_matrix()

    def norm(k, piece, g):
        start = pl.multiple_of(g * 256 + sc.pieces[k] * 64, 64)
        moved = dot(matrix[g * 64 : g * 64 + 64, :], piece[...])
        values = moved * live_run(start, height, breadth)
        base_out[pl.ds(start, 64), :] = values.astype(BF)
        normed_out[pl.ds(start, 64), :] = (normal(values)[0] * scale + shift).astype(BF)

    weave([step(norm, k, piece, g) for k, piece in enumerate((p0, p1, p2, p3)) for g in range(GROUPS)])

    def project(col, r):
        cols = slice(col, min(col + 256, 1152))
        qkv_out[r : r + 256, cols] = dot(normed_out[r : r + 256, :], weight[:, cols]).astype(BF)

    def project_steps(cols):
        return [step(project, col, r) for col in cols for r in range(0, 1024, 256)]

    def conv_pair(pair):
        steps = []
        for s in range(3):
            at = (3 * pair + s) * LANES
            cols = slice(at, at + LANES)

            def read(g, cols=cols):
                return qkv_out[g * 256 : g * 256 + 256, cols].astype(F32)

            def write(rows, total, cols=cols):
                conv_out[rows, cols] = total.astype(BF)

            steps += hold_steps(held, read)
            weights = taps_at(kernel, 768 * s + 384 * core + LANES * pair)
            steps += conv_steps(held, weights, write)
        return steps

    token = iota((1, 256), 1)
    lane = iota((256, LANES), 1)

    def attend_pair(pair):
        at = 3 * pair * LANES
        parts = {}

        def one(g, h):
            rows = slice(g * 256, g * 256 + 256)
            live = live_rows(token + g * 256, height, breadth) > 0.5
            query = conv_out[rows, at : at + LANES] * BF(HEAD_DIM**-0.5)
            key = conv_out[rows, at + LANES : at + 2 * LANES]
            value = conv_out[rows, at + 2 * LANES : at + 3 * LANES]
            mine = (lane < HEAD_DIM) if h == 0 else (lane >= HEAD_DIM)
            score = dot(jnp.where(mine, query, BF(0)), key, 1, 1)
            score = jnp.where(live, score, masked_score)
            top = jnp.max(score, axis=-1, keepdims=True)
            raised = jnp.exp(score - top)
            prob = (raised * (1.0 / jnp.sum(raised, axis=-1, keepdims=True))).astype(BF)
            prob_out[pair, g, h] = prob
            parts[h] = dot(prob, value)
            if h == 1:
                both = jnp.where(lane < HEAD_DIM, parts[0], parts[1])
                mixed_out[rows, pair * LANES : pair * LANES + LANES] = both.astype(BF)

        return [step(one, g, h) for g in range(GROUPS) for h in range(2)]

    weave(project_steps((0, 256)))
    weave(conv_pair(0), project_steps((512, 768, 1024)))
    weave(attend_pair(0), conv_pair(1))
    weave(attend_pair(1), conv_pair(2))
    weave(attend_pair(2))


def attend(line, pieces, cond, cond_right, weight, attn_kernel):
    return run(
        attend_kernel, "attend", line, (*pieces, cond, cond_right, weight, attn_kernel),
        [shaped(1024, 768), shaped(1024, 768), shaped(1024, 1152), shaped(1024, 1152),
         shaped(3, GROUPS, 2, 256, 256), shaped(1024, 384), shaped(8, 768, dtype=F32)],
        [HELD], items=True, us=11.5
    )


def middle_kernel(
    sc, mixed_own, mixed_other, base, out_weight, mod, seeds, seeds_other,
    attended_out, normed_out, branch_grad_out, seed_out,
    mixed, attended,
):
    height, breadth, core = sc.height, sc.breadth, sc.core
    mixed[:, pl.ds(pl.multiple_of(core * 384, LANES), 384)] = mixed_own[...]
    mixed[:, pl.ds(pl.multiple_of((1 - core) * 384, LANES), 384)] = mixed_other[...]
    gate = mod[2:3, :]
    shift, scale = mod[3:4, :], 1.0 + mod[4:5, :]
    gate_two, factor = mod[5:6, :], mod[6:7, :]
    matrix = to_phase_matrix()

    def project(r):
        attended[r : r + 256, :] = dot(mixed[r : r + 256, :], out_weight[...])

    def norm(r):
        rows = slice(r, r + 64)
        got = attended[rows, :].astype(BF)
        attended_out[rows, :] = got
        middle = base[rows, :].astype(F32) + gate * got.astype(F32)
        normed_out[rows, :] = (normal(middle)[0] * scale + shift).astype(BF)

    def seed(k, piece, g):
        start = pl.multiple_of(g * 256 + sc.pieces[k] * 64, 64)
        moved = dot(matrix[g * 64 : g * 64 + 64, :], piece[256 * (k % 2) : 256 * (k % 2) + 256, :])
        values = moved * live_run(start, height, breadth)
        seed_out[pl.ds(start, 64), :] = values.astype(BF)
        branch_grad_out[pl.ds(start, 64), :] = (values * factor * gate_two).astype(BF)

    project(0)
    weave([step(project, r) for r in (256, 512, 768)], [step(norm, r) for r in range(0, 768, 64)],
          [step(seed, k, piece, g) for k, piece in enumerate((seeds, seeds, seeds_other, seeds_other))
           for g in range(GROUPS)])
    weave([step(norm, r) for r in range(768, 1024, 64)])


def project_out(sc, mixed_own, mixed_other, base, out_weight, mod, pieces):
    return run(
        middle_kernel, "project_out", sc, (mixed_own, mixed_other, base, out_weight, mod, *pieces),
        [shaped(1024, 768)] * 4,
        [pltpu.VMEM((1024, 768), BF), pltpu.VMEM((1024, 768), F32)], items=True, us=4.6
    )


BLOCK = 256


def keep_half(core, values, local):
    low = values[128 * local : 128 * local + 64, :]
    high = values[128 * local + 64 : 128 * local + 128, :]
    return jnp.where(core == 0, low, high), jnp.where(core == 0, high, low)


def gelu_parts(v):
    square = v * v
    bent = jnp.tanh(v * (gelu_root + (gelu_root * gelu_cube) * square))
    rise = 0.5 + 0.5 * bent
    value = v * rise
    slope = rise + value * (1.0 - bent) * (gelu_root + (3.0 * gelu_root * gelu_cube) * square)
    return value, slope


def feed_kernel(sc, normed, branch_grad, up, down, kernel, keep, send, acts, hid, d_conv, held, d_act):
    clear_margins(held)

    def project_steps(k):
        cols = slice(k * BLOCK, (k + 1) * BLOCK)
        place = k % 2

        def one(r):
            hid[r : r + 256, cols] = dot(normed[r : r + 256, :], up[:, cols]).astype(BF)

        def two(r):
            d_act[place, r : r + 256, :] = dot(branch_grad[r : r + 256, :], down[cols, :], 1, 1)

        return [step(f, r) for r in range(0, 1024, 256) for f in (one, two)]

    def local_steps(k):
        steps = []
        place = k % 2
        for lane_block in range(BLOCK // LANES):
            cols = slice(lane_block * LANES, (lane_block + 1) * LANES)
            at = k * BLOCK + lane_block * LANES
            dest = slice(at, at + LANES)

            def read(g, dest=dest):
                return hid[g * 256 : g * 256 + 256, dest].astype(F32)

            def activate(rows, v, cols=cols, dest=dest):
                value, slope = gelu_parts(v)
                acts[rows, dest] = value.astype(BF)
                d_conv[rows, dest] = (d_act[place, rows, cols] * slope).astype(BF)

            steps += hold_steps(held, read)
            steps += conv_steps(held, taps_at(kernel, sc.core * 1536 + at), activate)
        return steps

    def down_steps():
        def one(place, out, half, c):
            rows = pl.ds(pl.multiple_of(half * 768 + place * 384, LANES), 384)
            cols = slice(half * 768 + c, half * 768 + c + 256)
            out[:, cols] = dot(acts[:, rows], branch_grad[:, c : c + 256], 0, 0).astype(BF)

        return [
            step(one, place, out, half, c)
            for place, out in ((1 - sc.bits[0], send), (sc.bits[0], keep))
            for half in range(2)
            for c in range(0, 768, 256)
        ]

    weave(project_steps(0))
    for k in range(5):
        weave(local_steps(k), project_steps(k + 1))
    weave(local_steps(5))
    weave(down_steps())


def feed(line, normed, branch_grad, up, down, ffn_kernel):
    return run(
        feed_kernel, "feed", line, (normed, branch_grad, up, down, ffn_kernel),
        [shaped(384, 1536), shaped(384, 1536), shaped(1024, 1536), shaped(1024, 1536), shaped(1024, 1536)],
        [HELD, pltpu.VMEM((2, 1024, BLOCK), F32)], limit=18 * 1024 * 1024, us=13.0,
    )


def feed_back_kernel(
    sc, normed, up, down, kernel, acts, hid, d_conv,
    keep, send, kernel_grad, branch_keep, branch_send, normed_grad_out, held, d_hids,
):
    core = sc.core
    clear_margins(held)
    kernel_grad[...] = jnp.zeros(kernel_grad.shape, F32)

    def local_steps(at):
        cols = slice(at, at + LANES)

        def write(rows, total):
            d_hids[rows, cols] = total.astype(BF)

        def write_sums(values):
            kernel_grad[0:9, cols] = values

        return hold_steps(held, lambda g: d_conv[g * 256 : g * 256 + 256, cols].astype(F32)) + back_steps(
            held, taps_at(kernel, core * 1536 + at), lambda rows: hid[rows, cols].astype(F32), write,
            write_sums,
        )

    def up_steps(k):
        cols = slice(k * BLOCK, (k + 1) * BLOCK)

        def one(pair, out):
            at = pl.ds(pl.multiple_of(pair * 384, 384), 384)
            out[0:384, cols] = dot(normed[:, at], d_hids[:, cols], 0, 0).astype(BF)

        return [step(one, 1 - sc.bits[0], send), step(one, sc.bits[0], keep)]

    def branch_steps():
        def one(g):
            total = dot(acts[g * 256 : g * 256 + 256, :], down[...])
            for local in range(2):
                kept, sent = keep_half(core, total, local)
                branch_keep[2 * g + local] = kept
                branch_send[2 * g + local] = sent.astype(BF)

        return [step(one, g) for g in range(GROUPS)]

    branch = branch_steps()
    for k in range(6):
        weave(
            local_steps(k * BLOCK) + local_steps(k * BLOCK + LANES),
            (up_steps(k - 1) if k else []) + branch[k : k + 1],
        )
    weave(up_steps(5))
    for r in range(0, 1024, 256):
        normed_grad_out[r : r + 256, :] = dot(d_hids[r : r + 256, :], up[...], 1, 1).astype(BF)
    send[384 : 384 + TAPS, :] = kernel_grad[...].astype(BF)


def feed_back(line, normed, up, down, ffn_kernel, acts, hid, d_conv):
    return run(
        feed_back_kernel, "feed_back", line, (normed, up, down, ffn_kernel, acts, hid, d_conv),
        [shaped(384, 1536), shaped(384 + TAPS, 1536), shaped(TAPS, 1536, dtype=F32), shaped(8, 64, 768, dtype=F32),
         shaped(8, 64, 768), shaped(1024, 768)],
        [HELD, pltpu.VMEM((1024, 1536), BF)], limit=18 * 1024 * 1024, us=14.0,
    )


def norm_back_kernel(
    sc, normed_grad, normed_grad_other, base, attended, seed, mod, mixed,
    middle_grad, att_grad, sums_out, out_keep, out_send,
):
    gate, scale, factor = mod[2:3, :], 1.0 + mod[4:5, :], mod[6:7, :]
    sums = [jnp.zeros((1, 768), F32) for _ in range(3)]

    def norm(r):
        rows = slice(r, r + 64)
        grad = normed_grad[rows, :].astype(F32) + normed_grad_other[rows, :].astype(F32)
        got = attended[rows, :].astype(F32)
        unit, inverse = normal(base[rows, :].astype(F32) + gate * got)
        both = grad * unit
        sums[0] = sums[0] + col_sum(grad)
        sums[1] = sums[1] + col_sum(both)
        grad = grad * scale
        mean = jnp.mean(grad, axis=-1, keepdims=True)
        along = jnp.mean(both * scale, axis=-1, keepdims=True)
        total = seed[rows, :].astype(F32) * factor + inverse * (grad - mean - unit * along)
        middle_grad[rows, :] = total
        sums[2] = sums[2] + col_sum(total * got)
        att_grad[rows, :] = (total * gate).astype(BF)

    for r in range(0, 1024, 64):
        norm(r)
    for k in range(3):
        sums_out[k : k + 1, :] = 0.5 * sums[k]
    for place, out in ((sc.bits[0], out_keep), (1 - sc.bits[0], out_send)):
        cols = pl.ds(pl.multiple_of(place * 384, 384), 384)
        out[...] = dot(mixed[...], att_grad[:, cols], 0, 0).astype(BF)


def norm_back(sc, normed_grad, normed_grad_other, base, attended, seed, mod, mixed):
    return run(
        norm_back_kernel, "norm_back", sc,
        (normed_grad, normed_grad_other, base, attended, seed, mod, mixed),
        [shaped(1024, 768, dtype=F32), shaped(1024, 768), shaped(3, 768, dtype=F32),
         shaped(384, 384), shaped(384, 384)], us=4.4
    )


def attend_back_kernel(
    heads, last, sc, att_grad, out_weight, normed, qkv, conv, prob, kernel, *rest,
):
    (*before, qkv_grad, weight_keep, weight_send, kernel_grad, held, d_mixed, d_conv) = rest
    kernel_grad[...] = jnp.zeros(kernel_grad.shape, F32)
    for given, out in zip(before, (weight_keep, weight_send, kernel_grad)):
        out[0 : given.shape[0], 384 : 384 + given.shape[1]] = given[...]
    core = sc.core
    at = 3 * heads * LANES
    clear_margins(held)
    mine_rows = slice(heads * LANES, heads * LANES + LANES)
    for r in range(0, 1024, 256):
        d_mixed[r : r + 256, :] = dot(att_grad[r : r + 256, :], out_weight[mine_rows, :], 1, 1).astype(BF)

    lane = iota((256, LANES), 1)
    low = lane < HEAD_DIM
    parts = {}

    def one(g, h):
        rows = slice(g * 256, g * 256 + 256)
        grad = d_mixed[rows, :]
        query = conv[rows, at : at + LANES]
        key = conv[rows, at + LANES : at + 2 * LANES]
        value = conv[rows, at + 2 * LANES : at + 3 * LANES]
        mine = low if h == 0 else jnp.logical_not(low)
        p = prob[heads, g, h]
        d_value = dot(p, grad, 0, 0)
        d_prob = dot(jnp.where(mine, grad, BF(0)), value, 1, 1)
        wide_p = p.astype(F32)
        inner = jnp.sum(d_prob * wide_p, axis=-1, keepdims=True)
        d_score = (wide_p * (d_prob - inner)).astype(BF)
        parts[h] = (dot(d_score, key), dot(d_score, query, 0, 0), d_value)
        if h == 1:
            for k in range(3):
                picked = jnp.where(low, parts[0][k], parts[1][k])
                if k < 2:
                    picked = picked * HEAD_DIM**-0.5
                d_conv[rows, k * LANES : (k + 1) * LANES] = picked.astype(BF)

    def local_steps(s):
        cols = slice(s * LANES, (s + 1) * LANES)
        source_cols = slice(at + s * LANES, at + (s + 1) * LANES)

        def write(rows, total):
            qkv_grad[rows, cols] = total.astype(BF)

        def write_sums(values):
            kernel_grad[0:9, cols] = values

        weights = taps_at(kernel, 768 * s + 384 * core + LANES * heads)
        return hold_steps(
            held, lambda g: d_conv[g * 256 : g * 256 + 256, cols].astype(F32)
        ) + back_steps(held, weights, lambda rows: qkv[rows, source_cols].astype(F32), write, write_sums)

    weave([step(one, g, h) for g in range(GROUPS) for h in range(2)])
    for s in range(3):
        weave(local_steps(s))
    for place, out in ((sc.bits[0], weight_keep), (1 - sc.bits[0], weight_send)):
        rows = pl.ds(pl.multiple_of(place * 384, 384), 384)
        out[0:384, 0:384] = dot(normed[:, rows], qkv_grad[...], 0, 0).astype(BF)
    if last:
        weight_send[384 : 384 + TAPS, :] = kernel_grad[...].astype(BF)


def attend_back(line, heads, last, att_grad, out_weight, normed, qkv, conv, prob, attn_kernel, before):
    width = 384 + (before[0].shape[1] if before else 0)
    return run(
        functools.partial(attend_back_kernel, heads, last), "attend_back", line,
        (att_grad, out_weight, normed, qkv, conv, prob, attn_kernel, *before),
        [shaped(1024, 384), shaped(384, width), shaped(384 + (TAPS if last else 0), width),
         shaped(TAPS, width, dtype=F32)],
        [HELD, pltpu.VMEM((1024, LANES), BF), pltpu.VMEM((1024, 384), BF)], us=6.3,
    )


def first_back_kernel(sc, g0, g1, g2, weight, branch, keep, send):
    core = sc.core
    send[8:16] = branch[...]
    for g in range(GROUPS):
        rows = slice(g * 256, g * 256 + 256)
        total = None
        for k, grad in enumerate((g0, g1, g2)):
            part = dot(grad[rows, :], weight[:, 384 * k : 384 * k + 384], 1, 1)
            total = part if total is None else total + part
        for local in range(2):
            kept, sent = keep_half(core, total, local)
            keep[2 * g + local] = kept
            send[2 * g + local] = sent.astype(BF)


def first_back(line, grads, weight, branch):
    return run(
        first_back_kernel, "first_back", line, (*grads, weight, branch),
        [shaped(8, 64, 768, dtype=F32), shaped(16, 64, 768)], us=2.7
    )


def finish_kernel(
    sc, base, attended, branch, grad, other, seed, middle_grad, sums_two, mod, near_out, far_out, cond,
):
    height, breadth, core = sc.height, sc.breadth, sc.core
    scale, gate_one, gate, factor = 1.0 + mod[1:2, :], mod[2:3, :], mod[5:6, :], mod[6:7, :]
    matrix = to_phase_matrix()
    d_shift, d_scale, d_gate = [jnp.zeros((1, 768), F32) for _ in range(3)]
    done = []
    for local in range(2):
        outs, grads = [], []
        for g in range(GROUPS):
            at = 2 * g + local
            start = pl.multiple_of(g * 256 + (2 * local + core) * 64, 64)
            rows = pl.ds(start, 64)
            live = live_run(start, height, breadth)
            first = base[rows, :].astype(F32)
            whole = branch[at] + other[8 + at].astype(F32)
            d_gate = d_gate + col_sum(seed[rows, :].astype(F32) * whole)
            result = first + gate_one * attended[rows, :].astype(F32) + gate * whole
            outs.append((result * live).astype(BF))
            total = grad[at] + other[at].astype(F32)
            unit, inverse = normal(first)
            both = total * unit
            d_shift = d_shift + col_sum(total)
            d_scale = d_scale + col_sum(both)
            total = total * scale
            mean = jnp.mean(total, axis=-1, keepdims=True)
            along = jnp.mean(both * scale, axis=-1, keepdims=True)
            total = middle_grad[rows, :] + inverse * (total - mean - unit * along)
            grads.append((total * live).astype(BF))
        done.append([
            dot(matrix, jnp.concatenate(parts, axis=0), 0, 0).astype(BF) for parts in (outs, grads)
        ])

    @pl.when(sc.pair == 0)
    def _():
        for k in range(2):
            near_out[k] = done[0][k]
            far_out[k] = done[1][k]

    @pl.when(sc.pair != 0)
    def _():
        for k in range(2):
            near_out[k] = done[1][k]
            far_out[k] = done[0][k]

    rows = d_shift, d_scale, sums_two[2:3, :], sums_two[1:2, :], d_gate * factor, sums_two[0:1, :]
    for k, row in enumerate(rows):
        cond[k : k + 1, :] = row


def finish(line, *operands):
    return run(
        finish_kernel, "finish", line, operands,
        [shaped(2, 256, 768), shaped(2, 256, 768), shaped(6, 768, dtype=F32)], items=True, us=4.5,
    )


def swap(values, axis, bit):
    count = lax.axis_size(axis)
    return lax.ppermute(values, axis, [(i, i ^ bit) for i in range(count)])


def swap_at(values, k):
    wide, narrow = lax.axis_size(WIDE), lax.axis_size(NARROW)
    steps = {"x": (0, 2), "y": (1, 0), "z": (2, 0), "w": (4, 0)}
    pairs = []
    for w in range(wide):
        for n in range(narrow):
            dw, dn = steps[HALVINGS[n % 2][k]]
            pairs.append((w * narrow + n, (w ^ dw) * narrow + (n ^ dn)))
    return lax.ppermute(values, (WIDE, NARROW), pairs)


def bits_of(count):
    return [1 << k for k in range(count.bit_length() - 1)]


def halve_kernel(k, tapped, sc, kept, got, *rest):
    taps, rest = (rest[0], rest[1:]) if tapped else (None, rest)
    keep, send = rest[-3:-1] if tapped else rest[-2:]
    half = keep.shape[0]
    if tapped:
        rest[-1][...] = taps[...].astype(BF).astype(F32) + got[2 * half : 2 * half + TAPS, :].astype(F32)
        send[half : half + TAPS, :] = rest[-1][...].astype(BF)
    for d, out in enumerate((keep, send)):
        rows = pl.ds(pl.multiple_of((sc.bits[k] ^ d) * half, 16), half)
        out[0:half, :] = (kept[rows, :].astype(F32) + got[rows, :].astype(F32)).astype(BF)


def total_kernel(tapped, sc, kept, got, *rest):
    rows, width = kept.shape
    if tapped:
        taps, *rest, taps_out = rest
        taps_out[...] = taps[...].astype(BF).astype(F32) + got[rows : rows + TAPS, :].astype(F32)
    *cond, out = rest
    out[0:rows, :] = (kept[...].astype(F32) + got[0:rows, :].astype(F32)).astype(BF)
    if cond:
        count = (out.shape[0] - rows) * width // (6 * 768)
        hot = [jnp.where(sc.home == k, cond[0][...], 0.0) for k in range(count)]
        hot = jnp.concatenate(hot, axis=0).astype(BF)
        part = 6 * count * 768 // width
        for k in range(width // 768):
            out[rows : rows + part, 768 * k : 768 * k + 768] = hot[k * part : (k + 1) * part, :]


def stack_kernel(extra, tapped, sc, kept, got, *rest):
    *taps, out = rest
    half = kept.shape[0] - extra
    out[0:half, :] = kept[0:half, :]
    out[half : 2 * half, :] = got[0:half, :]
    if extra:
        below = slice(half, half + extra)
        out[2 * half : 2 * half + extra, :] = (
            kept[below, :].astype(F32) + got[below, :].astype(F32)
        ).astype(BF)
    if taps:
        out[2 * half + extra : 2 * half + extra + TAPS, :] = taps[0][...].astype(BF)


class Flow:
    def __init__(self, line, keep, send, taps=None):
        self.line = line
        self.taps = () if taps is None else (taps,)
        self.extra = 0
        for bit in bits_of(lax.axis_size(WIDE))[3:]:
            keep, send = [
                (v.astype(F32) + swap(v, WIDE, bit).astype(F32)).astype(BF) for v in (keep, send)
            ]
            self.taps = tuple(v + swap(v, WIDE, bit) for v in self.taps)
        self.kept, self.got = keep, swap_at(send, 0)

    def below(self):
        return [shaped(*v.shape, dtype=F32) for v in self.taps]

    def halve(self, k):
        rows, width = self.kept.shape
        tapped = len(self.taps) > 0
        self.kept, send, *self.taps = run(
            functools.partial(halve_kernel, k, tapped), "halve", self.line,
            (self.kept, self.got, *self.taps),
            [shaped(rows // 2, width), shaped(rows // 2 + (TAPS if tapped else 0), width)] + self.below(),
        )
        self.got = swap_at(send, k)

    def total(self, cond=None):
        rows, width = self.kept.shape
        if cond is not None:
            self.extra = 6 * lax.axis_size(WIDE) * 768 // width
        operands = (self.kept, self.got, *self.taps, *(() if cond is None else (cond,)))
        self.kept, *self.taps = run(
            functools.partial(total_kernel, len(self.taps) > 0), "total", self.line, operands,
            [shaped(rows + self.extra, width)] + self.below(), items=cond is not None,
        )
        self.got = swap_at(self.kept, 3)

    def stack(self, k):
        rows, width = self.kept.shape
        rows = 2 * (rows - self.extra) + self.extra
        taps = () if k else tuple(self.taps)
        (self.kept,) = run(
            functools.partial(stack_kernel, self.extra, len(taps) > 0), "stack", self.line,
            (self.kept, self.got, *taps), [shaped(rows + TAPS * len(taps), width)],
        )
        self.got = swap_at(self.kept, k - 1) if k else swap(self.kept, NARROW, 1)


def by_core(core, write, own, other):
    @pl.when(core == 0)
    def _():
        write(own, other)

    @pl.when(core != 0)
    def _():
        write(other, own)


def row_runs(chip, rows):
    for i in range(16):
        yield slice(rows * i, rows * i + rows), (i ^ chip)


def leave(buffers, outs, sems):
    return [pltpu.make_async_copy(src, dst, sems.at[k]) for k, (src, dst) in enumerate(zip(buffers, outs))]


def down_done_kernel(sc, own, other, out, buffer, sems):
    copies = leave([buffer.at[k] for k in range(2)], [out.at[sc.core], out.at[1 - sc.core]], sems)
    for k, (part, chip) in enumerate(((own, sc.chip), (other, sc.other_chip))):
        for rows, place in row_runs(chip, 48):
            dest = pl.ds(pl.multiple_of(place * 48, 16), 48)
            for half in range(2):
                buffer[k, half, dest, :] = part[rows, 768 * half : 768 * half + 768].astype(F32)
        copies[k].start()
    for copy in copies:
        copy.wait()


def down_done(line, flow):
    (out,) = run(
        down_done_kernel, "down_done", line, (flow.kept, flow.got), [shaped(2, 2, 768, 768, dtype=F32)],
        [pltpu.VMEM((2, 2, 768, 768), F32), pltpu.SemaphoreType.DMA((2,))], far_outs=(0,),
        limit=12 * 1024 * 1024, us=4.0,
    )
    return out.reshape(3072, 768)


def up_done_kernel(sc, own, other, out, taps_out, buffer, sems):
    def at(core):
        return out.at[:, pl.ds(pl.multiple_of(core * 1536, 1536), 1536)]

    copies = leave([buffer.at[k] for k in range(2)], [at(sc.core), at(1 - sc.core)], sems)
    for k, (part, chip) in enumerate(((own, sc.chip), (other, sc.other_chip))):
        for rows, place in row_runs(chip, 48):
            buffer[k, pl.ds(pl.multiple_of(place * 48, 16), 48), :] = part[rows, :].astype(F32)
        copies[k].start()

    def write(first, second):
        for core, part in enumerate((first, second)):
            taps = part[768 : 768 + TAPS, :].astype(F32)
            for a in range(3):
                taps_out[a, :, 1536 * core : 1536 * core + 1536] = taps[3 * a : 3 * a + 3, :]

    by_core(sc.core, write, own, other)
    for copy in copies:
        copy.wait()


def up_done(line, flow):
    return run(
        up_done_kernel, "up_done", line, (flow.kept, flow.got),
        [shaped(768, 3072, dtype=F32), shaped(3, 3, 3072, dtype=F32)],
        [pltpu.VMEM((2, 768, 1536), F32), pltpu.SemaphoreType.DMA((2,))], far_outs=(0,),
        limit=14 * 1024 * 1024, us=4.0,
    )


def attend_done_kernel(where, sc, *refs):
    count = (len(refs) - 8) // 2
    own, other = refs[:count], refs[count : 2 * count]
    qkv_grad, out_grad, taps_out, cond_out, shift_out, qkv, out, sems = refs[2 * count :]
    copies = leave(
        [qkv.at[k] for k in range(6)] + [out.at[k] for k in range(2)],
        [
            qkv_grad.at[:, pl.ds(pl.multiple_of(768 * s + 384 * core, LANES), 384)]
            for core in (sc.core, 1 - sc.core)
            for s in range(3)
        ]
        + [out_grad.at[core] for core in (sc.core, 1 - sc.core)],
        sems,
    )
    for k, (parts, chip) in enumerate(((own, sc.chip), (other, sc.other_chip))):
        for rows, place in row_runs(chip, 48):
            dest = pl.ds(pl.multiple_of(place * 48, 16), 48)
            for s in range(3):
                for heads in range(3):
                    flow, col = where[heads]
                    col = col + LANES * s
                    qkv[3 * k + s, dest, LANES * heads : LANES * heads + LANES] = parts[flow][
                        rows, col : col + LANES
                    ].astype(F32)
            dest = pl.ds(pl.multiple_of((place & 7) * 48, 16), 48)
            cols = pl.ds(pl.multiple_of((place >> 3) * 384, LANES), 384)
            flow, col = where[3]
            out[k, dest, cols] = parts[flow][rows, col : col + 384].astype(F32)
        for copy in (*copies[3 * k : 3 * k + 3], copies[6 + k]):
            copy.start()

    def write(first, second):
        for core, parts in enumerate((first, second)):
            taps = [part[part.shape[0] - TAPS :, :].astype(F32) for part in parts]
            for a in range(3):
                for heads in range(3):
                    flow, col = where[heads]
                    for s in range(3):
                        to = 768 * s + 384 * core + LANES * heads
                        at = col + LANES * s
                        taps_out[a, :, to : to + LANES] = taps[flow][3 * a : 3 * a + 3, at : at + LANES]

    by_core(sc.core, write, own, other)
    mine, its = own[-1], other[-1]
    width = mine.shape[1]
    extra = mine.shape[0] - 768 - TAPS
    total = mine[768 : 768 + extra, :].astype(F32) + its[768 : 768 + extra, :].astype(F32)
    total = jnp.concatenate([total[:, 768 * k : 768 * k + 768] for k in range(width // 768)], axis=0)
    rows = jnp.zeros((6, 768), F32)
    for k in range(total.shape[0] // 6):
        rows = rows + jnp.where(sc.wide == k, total[6 * k : 6 * k + 6, :], 0.0)
    for k in range(5):
        cond_out[:, 768 * k : 768 * k + 768] = rows[k : k + 1, :]
    shift_out[...] = rows[5:6, :]
    for copy in copies:
        copy.wait()


def attend_done(line, where, flows):
    qkv_grad, out_grad, attn_grad, cond_grad, shift_grad = run(
        functools.partial(attend_done_kernel, where), "attend_done", line,
        [flow.kept for flow in flows] + [flow.got for flow in flows],
        [shaped(768, 2304, dtype=F32), shaped(2, 384, 768, dtype=F32), shaped(3, 3, 2304, dtype=F32),
         shaped(1, 3840, dtype=F32), shaped(1, 768, dtype=F32)],
        [pltpu.VMEM((6, 768, 384), F32), pltpu.VMEM((2, 384, 768), F32), pltpu.SemaphoreType.DMA((8,))],
        far_outs=(0, 1), limit=16 * 1024 * 1024, us=4.0,
    )
    return qkv_grad, out_grad.reshape(768, 768), attn_grad, cond_grad, shift_grad


def join_kernel(sc, near, far, out, grad_out):
    for k, target in enumerate((out, grad_out)):
        target[sc.pair] = near[k]
        target[1 - sc.pair] = far[k]


def join(line, near, far):
    out, grad = run(join_kernel, "join", line, (near, far), [shaped(2, 256, 768)] * 2)
    return out.reshape(2, 8, 32, 768), grad.reshape(2, 8, 32, 768)


def copy_all(sems, pairs):
    copies = [pltpu.make_async_copy(src, dst, sems.at[k]) for k, (src, dst) in enumerate(pairs)]
    for copy in copies:
        copy.start()
    for copy in copies:
        copy.wait()


def cut_pieces_kernel(sc, block, far, own, sems):
    copy_all(sems, [(block.at[1 - sc.pair], far), (block.at[sc.pair], own)])


def cut_pieces(line, block):
    return run(
        cut_pieces_kernel, "cut_pieces", line, (block.reshape(2, 256, 768),), [shaped(256, 768)] * 2,
        [pltpu.SemaphoreType.DMA((2,))], far=(0,), limit=ALL_VMEM,
    )


def pass_kernel(sc, *refs):
    count = len(refs) // 2
    for k in range(count):
        refs[count + k][...] = refs[k][...]


def pass_on(line, *arrays):
    return run(pass_kernel, "pass_on", line, arrays, [shaped(*v.shape) for v in arrays])


def pack_kernel(sc, one, two, out):
    out[0:256, :] = one[...]
    out[256:512, :] = two[...]


def cut_weights_kernel(sc, qkv, out, up, down, qkv_part, out_part, up_part, down_part, sems):
    core = sc.core
    pairs = [
        (
            qkv.at[:, lanes_at(768 * s + 384 * core + LANES * pair)],
            qkv_part.at[:, pl.ds((3 * pair + s) * LANES, LANES)],
        )
        for pair in range(3)
        for s in range(3)
    ]
    pairs += [
        (out.at[pl.ds(pl.multiple_of(384 * core, 384), 384), :], out_part),
        (up.at[:, pl.ds(pl.multiple_of(1536 * core, 1536), 1536)], up_part),
        (down.at[pl.ds(pl.multiple_of(1536 * core, 1536), 1536), :], down_part),
    ]
    copy_all(sems, pairs)


def cut_weights(line, qkv_weight, out_weight, up_weight, down_weight):
    return run(
        cut_weights_kernel, "cut_weights", line, (qkv_weight, out_weight, up_weight, down_weight),
        [shaped(768, 1152), shaped(384, 768), shaped(768, 1536), shaped(1536, 768)],
        [pltpu.SemaphoreType.DMA((12,))], far=(0, 1, 2, 3), limit=ALL_VMEM, us=2.5
    )


def on_device(
    tokens, cotangent, conditioning, aspect, bucket,
    qkv_weight, attn_kernel, out_weight, up_weight, ffn_kernel, down_weight,
):
    wide_count = lax.axis_size(WIDE)
    line = Line(aspect, bucket)
    far, own = cut_pieces(line, tokens)
    got = swap(far, NARROW, 2)
    own_other = swap(own, NARROW, 1)
    cond_right = lax.ppermute(conditioning, WIDE, [(i + 1, i) for i in range(wide_count - 1)])
    weights = cut_weights(line, qkv_weight, out_weight, up_weight, down_weight)
    qkv_part, out_part, up_part, down_part = weights
    seed_far, seed_own = cut_pieces(line, cotangent)
    got, cond_right = pass_on(line, got, cond_right)
    token_pieces = own, got, own_other, swap(got, NARROW, 1)
    base, normed_one, qkv, conv, prob, mixed, mod = attend(
        line, token_pieces, conditioning, cond_right, qkv_part, attn_kernel
    )
    (seeds,) = run(pack_kernel, "pack", line, (seed_own, swap(seed_far, NARROW, 2)), [shaped(512, 768)])
    mixed_other = swap(mixed, NARROW, 1)
    seed_pieces = seeds, swap(seeds, NARROW, 1)
    attended, normed_two, d_branch, seed = project_out(
        line, mixed, mixed_other, base, out_weight, mod, seed_pieces
    )

    def back(heads, last, d_att, before):
        return attend_back(
            line, heads, last, d_att, out_part, normed_one, qkv, conv, prob, attn_kernel, before
        )

    keep, send, *saved = feed(line, normed_two, d_branch, up_part, down_part, ffn_kernel)
    a = Flow(line, keep, send)
    keep, send, taps, branch, branch_send, d_normed = feed_back(
        line, normed_two, up_part, down_part, ffn_kernel, *saved
    )
    b = Flow(line, keep, send, taps)
    a.halve(1)
    (d_normed_send,) = pass_on(line, d_normed)
    d_normed_other = swap(d_normed_send, NARROW, 1)
    d_middle, d_att, sums_two, *parts = norm_back(
        line, d_normed, d_normed_other, base, attended, seed, mod, mixed
    )
    g0, *parts = back(0, True, d_att, parts)
    c = Flow(line, *parts)
    b.halve(1)
    g1, *parts = back(1, False, d_att, ())
    a.halve(2)
    g2, *parts = back(2, True, d_att, parts)
    d = Flow(line, *parts)
    a.halve(3)
    c.halve(1)
    d_first, d_first_send = first_back(line, (g0, g1, g2), qkv_part, branch_send)
    b.halve(2)
    a.total()
    d.halve(1)
    (d_first_send,) = pass_on(line, d_first_send)
    d_first_other = swap(d_first_send, NARROW, 1)
    near, far, cond = finish(
        line, base, attended, branch, d_first, d_first_other, seed, d_middle, sums_two, mod
    )
    far = swap(far, NARROW, 2)
    a.stack(3)
    b.halve(3)
    c.halve(2)
    a.stack(2)
    b.total()
    b.stack(3)
    d.halve(2)
    a.stack(1)
    c.halve(3)
    block_out, tokens_grad = join(line, near, far)
    b.stack(2)
    d.halve(3)
    c.total()
    d.total(cond)
    c.stack(3)
    c.stack(2)
    b.stack(1)
    a.stack(0)
    d.stack(3)
    b.stack(0)
    c.stack(1)
    d.stack(2)
    d.stack(1)
    c.stack(0)
    down_grad = down_done(line, a)
    d.stack(0)
    up_grad, ffn_grad = up_done(line, b)
    where = (0, 0), (1, 384), (1, 0), (0, 384)
    qkv_grad, out_grad, attn_grad, cond_grad, shift_grad = attend_done(line, where, (c, d))

    return (
        block_out, tokens_grad, cond_grad, shift_grad, qkv_grad, attn_grad, out_grad, up_grad, ffn_grad,
        down_grad,
    )


def solution(mesh):
    rows = P(WIDE, NARROW, None, None)
    in_specs = (rows, rows, P(WIDE, None)) + (P(),) * 8
    out_specs = (rows, rows, P(WIDE, None), P(WIDE, None)) + (P(),) * 6
    return jax.shard_map(
        on_device, mesh=mesh, in_specs=in_specs, out_specs=out_specs, check_vma=False
    )
```

```python
import functools

import jax
import jax.numpy as jnp
from jax import lax
from jax.experimental import pallas as pl
from jax.experimental.pallas import tpu as pltpu
from jax.sharding import PartitionSpec as P

HEAD_DIM = 64
TAPS = 16
WIDE = "wide"
NARROW = "narrow"
LANES = 128
GROUPS = 4
MARGIN = 16

masked_score = -1000000000.0
norm_epsilon = 1e-06
gelu_root = 0.7978845608028654
gelu_cube = 0.044715

BF = jnp.bfloat16
F32 = jnp.float32
SCRATCH = 16 * 1024 * 1024
ALL_VMEM = 61 * 1024 * 1024
COST = 1150000000


def dot(left, right, left_dim=1, right_dim=0):
    return lax.dot_general(
        left, right, (((left_dim,), (right_dim,)), ((), ())), preferred_element_type=F32
    )


ANYWHERE = pl.BlockSpec(memory_space=pl.ANY)
DISTANT = pl.BlockSpec(memory_space=pltpu.HBM)
SCALARS = pl.BlockSpec(memory_space=pltpu.SMEM)
HERE = pl.BlockSpec(memory_space=pltpu.VMEM)


def shaped(*shape, dtype=BF):
    return jax.ShapeDtypeStruct(shape, dtype)


HALVINGS = ("x", "y", "z", "w"), ("y", "z", "x", "w")


class Place:
    def __init__(self, aspect=None, bucket=None):
        wide, narrow = lax.axis_index(WIDE), lax.axis_index(NARROW)
        self.wide = wide
        self.pair, self.core = narrow // 2, narrow % 2
        bits = {"x": self.pair, "y": wide % 2, "z": (wide // 2) % 2, "w": (wide // 4) % 2}
        self.bits = [
            jnp.where(self.core == 0, bits[first], bits[second]) for first, second in zip(*HALVINGS)
        ]
        self.chip = self.chip_of(self.bits)
        self.other_chip = self.chip_of(
            [jnp.where(self.core == 0, bits[second], bits[first]) for first, second in zip(*HALVINGS)]
        )
        self.pieces = (
            narrow, 2 * (1 - self.pair) + self.core, 2 * self.pair + 1 - self.core,
            2 * (1 - self.pair) + 1 - self.core,
        )
        if aspect is not None:
            item = 2 * wide + self.pair
            self.height, self.breadth = aspect[item, 0], aspect[item, 1]
            self.home = bucket[item]
            self.stays = self.home == wide

    def chip_of(self, bits):
        return 8 * bits[0] + 4 * bits[1] + 2 * bits[2] + bits[3]


class Line:
    def __init__(self, aspect, bucket):
        self.items = aspect, bucket
        self.token = None


def run(kernel, name, line, operands, outs, scratch=(), limit=SCRATCH, items=False, far=(), far_outs=(), us=1.0):
    count = len(operands)
    tokens = [] if line.token is None else [line.token]
    scalars = list(line.items) if items else []

    def body(*refs):
        place = Place(*refs[: len(scalars)])
        refs = refs[len(scalars) :]
        refs = refs[:count] + refs[count + len(tokens) :]
        refs[count + len(outs)][...] = jnp.zeros((8, LANES), F32)
        kernel(place, *refs[: count + len(outs)], *refs[count + len(outs) + 1 :])

    *made, line.token = pl.pallas_call(
        body,
        in_specs=[SCALARS] * len(scalars)
        + [DISTANT if k in far else HERE for k in range(count)]
        + [ANYWHERE] * len(tokens),
        out_specs=[DISTANT if k in far_outs else HERE for k in range(len(outs))] + [HERE],
        out_shape=[*outs, shaped(8, LANES, dtype=F32)],
        scratch_shapes=list(scratch),
        compiler_params=pltpu.CompilerParams(vmem_limit_bytes=limit),
        cost_estimate=pl.CostEstimate(flops=int(us * COST), bytes_accessed=1, transcendentals=0),
        name=name,
    )(*scalars, *operands, *tokens)
    return made


def step(f, *given):
    return functools.partial(f, *given)


def weave(*lists):
    order = sorted(
        ((at + 0.5) / len(steps), which, at)
        for which, steps in enumerate(lists)
        for at in range(len(steps))
    )
    for _, which, at in order:
        lists[which][at]()


def iota(shape, dim):
    return lax.broadcasted_iota(jnp.int32, shape, dim)


def live_rows(token, height, breadth):
    row = 2 * ((token >> 4) & 15) + (token >> 9)
    col = 2 * (token & 15) + ((token >> 8) & 1)
    return ((row < height) & (col < breadth)).astype(F32)


def live_run(start, height, breadth):
    return live_rows(start + iota((64, 1), 0), height, breadth)


def to_phase_matrix():
    row = iota((256, 256), 0)
    col = iota((256, 256), 1)
    grid_row = 2 * ((row >> 4) & 3) + (row >> 7)
    grid_col = 2 * (row & 15) + ((row >> 6) & 1)
    return (col == grid_row * 32 + grid_col).astype(F32).astype(BF)


def normal(values):
    center = values - jnp.mean(values, axis=-1, keepdims=True)
    scale = lax.rsqrt(jnp.mean(center * center, axis=-1, keepdims=True) + norm_epsilon)
    return center * scale, scale


def col_sum(values):
    return jnp.sum(values, axis=0, keepdims=True)


HELD = pltpu.VMEM((2 * GROUPS, 2 * MARGIN + 256, LANES), F32)
STEP = 64


def clear_margins(held):
    zero = jnp.zeros((2 * GROUPS, MARGIN, LANES), F32)
    held[:, 0:MARGIN, :] = zero
    held[:, MARGIN + 256 : 2 * MARGIN + 256, :] = zero


def hold_steps(held, read):
    place = iota((256, LANES), 0) & 15

    def one(g):
        values = read(g)
        held[2 * g, MARGIN : MARGIN + 256, :] = values
        if g % 2:
            moved = jnp.where(place == 0, 0.0, pltpu.roll(values, 1, 0))
        else:
            moved = jnp.where(place == 15, 0.0, pltpu.roll(values, 255, 0))
        held[2 * g + 1, MARGIN : MARGIN + 256, :] = moved

    return [step(one, g) for g in range(GROUPS)]


def taps(g):
    alpha, beta = g // 2, g % 2
    out = []
    for a in range(3):
        for b in range(3):
            row = alpha + a - 1
            col = beta + b - 1
            src = 2 * (row % 2) + col % 2
            out.append((a, b, 2 * src + (0 if 0 <= col <= 1 else 1), MARGIN * (row // 2)))
    return out


def tap_weights(kernel):
    return [[kernel[3 * a + b : 3 * a + b + 1, :] for b in range(3)] for a in range(3)]


def taps_at(kernel, start):
    cols = lanes_at(start)
    return jnp.concatenate([kernel[a, :, cols].astype(F32) for a in range(3)], axis=0)


def runs():
    return [(g, start) for g in range(GROUPS) for start in range(0, 256, STEP)]


def run_rows(g, start):
    return slice(g * 256 + start, g * 256 + start + STEP)


def conv_steps(held, kernel, write):
    weights = tap_weights(kernel)

    def one(g, start):
        total = None
        for a, b, src, off in taps(g):
            part = weights[a][b] * held[src, MARGIN + off + start : MARGIN + off + start + STEP, :]
            total = part if total is None else total + part
        write(run_rows(g, start), total)

    return [step(one, *at) for at in runs()]


def back_steps(held, kernel, read, write, write_sums):
    weights = tap_weights(kernel)
    sums = [None] * 9

    def one(g, start):
        given = read(run_rows(g, start))
        total = None
        for a, b, src, off in taps(g):
            window = held[src, MARGIN + off + start : MARGIN + off + start + STEP, :]
            part = weights[2 - a][2 - b] * window
            total = part if total is None else total + part
            at = 3 * (2 - a) + 2 - b
            prod = jnp.sum((given * window).reshape(STEP // 8, 8, LANES), axis=0)
            sums[at] = prod if sums[at] is None else sums[at] + prod
        write(run_rows(g, start), total)

    def last():
        write_sums(jnp.concatenate([col_sum(v) for v in sums], axis=0))

    return [step(one, *at) for at in runs()] + [last]


def lanes_at(start):
    return pl.ds(pl.multiple_of(start, LANES), LANES)


def attend_kernel(
    sc, p0, p1, p2, p3, cond, cond_right, weight, kernel,
    base_out, normed_out, qkv_out, conv_out, prob_out, mixed_out, mod,
    held,
):
    height, breadth, core = sc.height, sc.breadth, sc.core
    clear_margins(held)
    for k in range(6):
        cols = slice(768 * k, 768 * k + 768)
        mod[k : k + 1, :] = jnp.where(sc.stays, cond[:, cols].astype(F32), cond_right[:, cols].astype(F32))
    tokens = (height * breadth).astype(F32)
    mod[6:8, :] = jnp.full((2, 768), 1024.0, F32) / tokens
    shift, scale = mod[0:1, :], 1.0 + mod[1:2, :]
    matrix = to_phase_matrix()

    def norm(k, piece, g):
        start = pl.multiple_of(g * 256 + sc.pieces[k] * 64, 64)
        moved = dot(matrix[g * 64 : g * 64 + 64, :], piece[...])
        values = moved * live_run(start, height, breadth)
        base_out[pl.ds(start, 64), :] = values.astype(BF)
        normed_out[pl.ds(start, 64), :] = (normal(values)[0] * scale + shift).astype(BF)

    def norm_steps(g):
        return [step(norm, k, piece, g) for k, piece in enumerate((p0, p1, p2, p3))]

    def project(col, r):
        cols = slice(col, min(col + 256, 1152))
        qkv_out[r : r + 256, cols] = dot(normed_out[r : r + 256, :], weight[:, cols]).astype(BF)

    def project_steps(cols, rows=range(0, 1024, 256)):
        return [step(project, col, r) for col in cols for r in rows]

    def conv_pair(pair):
        steps = []
        for s in range(3):
            at = (3 * pair + s) * LANES
            cols = slice(at, at + LANES)

            def read(g, cols=cols):
                return qkv_out[g * 256 : g * 256 + 256, cols].astype(F32)

            def write(rows, total, cols=cols):
                conv_out[rows, cols] = total.astype(BF)

            steps += hold_steps(held, read)
            weights = taps_at(kernel, 768 * s + 384 * core + LANES * pair)
            steps += conv_steps(held, weights, write)
        return steps

    token = iota((1, 256), 1)
    lane = iota((256, LANES), 1)

    def attend_pair(pair):
        at = 3 * pair * LANES
        parts = {}

        def one(g, h):
            rows = slice(g * 256, g * 256 + 256)
            live = live_rows(token + g * 256, height, breadth) > 0.5
            query = conv_out[rows, at : at + LANES] * BF(HEAD_DIM**-0.5)
            key = conv_out[rows, at + LANES : at + 2 * LANES]
            value = conv_out[rows, at + 2 * LANES : at + 3 * LANES]
            mine = (lane < HEAD_DIM) if h == 0 else (lane >= HEAD_DIM)
            score = dot(jnp.where(mine, query, BF(0)), key, 1, 1)
            score = jnp.where(live, score, masked_score)
            top = jnp.max(score, axis=-1, keepdims=True)
            raised = jnp.exp(score - top)
            prob = (raised * (1.0 / jnp.sum(raised, axis=-1, keepdims=True))).astype(BF)
            prob_out[pair, g, h] = prob
            parts[h] = dot(prob, value)
            if h == 1:
                both = jnp.where(lane < HEAD_DIM, parts[0], parts[1])
                mixed_out[rows, pair * LANES : pair * LANES + LANES] = both.astype(BF)

        return [step(one, g, h) for g in range(GROUPS) for h in range(2)]

    weave(norm_steps(0))
    for g in range(1, GROUPS):
        weave(norm_steps(g), project_steps((0, 256), (256 * g - 256,)))
    weave(project_steps((0, 256), (768,)))
    weave(conv_pair(0), project_steps((512, 768, 1024)))
    weave(attend_pair(0), conv_pair(1))
    weave(attend_pair(1), conv_pair(2))
    weave(attend_pair(2))


def attend(line, pieces, cond, cond_right, weight, attn_kernel):
    return run(
        attend_kernel, "attend", line, (*pieces, cond, cond_right, weight, attn_kernel),
        [shaped(1024, 768), shaped(1024, 768), shaped(1024, 1152), shaped(1024, 1152),
         shaped(3, GROUPS, 2, 256, 256), shaped(1024, 384), shaped(8, 768, dtype=F32)],
        [HELD], items=True, us=11.5
    )


def middle_kernel(
    sc, mixed_own, mixed_other, base, out_weight, mod, seeds, seeds_other,
    attended_out, normed_out, branch_grad_out, seed_out,
    mixed, attended,
):
    height, breadth, core = sc.height, sc.breadth, sc.core
    mixed[:, pl.ds(pl.multiple_of(core * 384, LANES), 384)] = mixed_own[...]
    mixed[:, pl.ds(pl.multiple_of((1 - core) * 384, LANES), 384)] = mixed_other[...]
    gate = mod[2:3, :]
    shift, scale = mod[3:4, :], 1.0 + mod[4:5, :]
    gate_two, factor = mod[5:6, :], mod[6:7, :]
    matrix = to_phase_matrix()

    def project(r):
        attended[r : r + 256, :] = dot(mixed[r : r + 256, :], out_weight[...])

    def norm(r):
        rows = slice(r, r + 64)
        got = attended[rows, :].astype(BF)
        attended_out[rows, :] = got
        middle = base[rows, :].astype(F32) + gate * got.astype(F32)
        normed_out[rows, :] = (normal(middle)[0] * scale + shift).astype(BF)

    def seed(k, piece, g):
        start = pl.multiple_of(g * 256 + sc.pieces[k] * 64, 64)
        moved = dot(matrix[g * 64 : g * 64 + 64, :], piece[256 * (k % 2) : 256 * (k % 2) + 256, :])
        values = moved * live_run(start, height, breadth)
        seed_out[pl.ds(start, 64), :] = values.astype(BF)
        branch_grad_out[pl.ds(start, 64), :] = (values * factor * gate_two).astype(BF)

    project(0)
    weave([step(project, r) for r in (256, 512, 768)], [step(norm, r) for r in range(0, 768, 64)],
          [step(seed, k, piece, g) for k, piece in enumerate((seeds, seeds, seeds_other, seeds_other))
           for g in range(GROUPS)])
    weave([step(norm, r) for r in range(768, 1024, 64)])


def project_out(sc, mixed_own, mixed_other, base, out_weight, mod, pieces):
    return run(
        middle_kernel, "project_out", sc, (mixed_own, mixed_other, base, out_weight, mod, *pieces),
        [shaped(1024, 768)] * 4,
        [pltpu.VMEM((1024, 768), BF), pltpu.VMEM((1024, 768), F32)], items=True, us=4.6
    )


BLOCK = 256


def keep_half(core, values, local):
    low = values[128 * local : 128 * local + 64, :]
    high = values[128 * local + 64 : 128 * local + 128, :]
    return jnp.where(core == 0, low, high), jnp.where(core == 0, high, low)


def gelu_parts(v):
    square = v * v
    bent = jnp.tanh(v * (gelu_root + (gelu_root * gelu_cube) * square))
    rise = 0.5 + 0.5 * bent
    value = v * rise
    slope = rise + value * (1.0 - bent) * (gelu_root + (3.0 * gelu_root * gelu_cube) * square)
    return value, slope


def feed_kernel(sc, normed, branch_grad, up, down, kernel, keep, send, acts, hid, d_conv, held, d_act):
    clear_margins(held)

    def project_steps(k):
        cols = slice(k * BLOCK, (k + 1) * BLOCK)
        place = k % 2

        def one(r):
            hid[r : r + 256, cols] = dot(normed[r : r + 256, :], up[:, cols]).astype(BF)

        def two(r):
            d_act[place, r : r + 256, :] = dot(branch_grad[r : r + 256, :], down[cols, :], 1, 1)

        return [step(f, r) for r in range(0, 1024, 256) for f in (one, two)]

    def local_steps(k):
        steps = []
        place = k % 2
        for lane_block in range(BLOCK // LANES):
            cols = slice(lane_block * LANES, (lane_block + 1) * LANES)
            at = k * BLOCK + lane_block * LANES
            dest = slice(at, at + LANES)

            def read(g, dest=dest):
                return hid[g * 256 : g * 256 + 256, dest].astype(F32)

            def activate(rows, v, cols=cols, dest=dest):
                value, slope = gelu_parts(v)
                acts[rows, dest] = value.astype(BF)
                d_conv[rows, dest] = (d_act[place, rows, cols] * slope).astype(BF)

            steps += hold_steps(held, read)
            steps += conv_steps(held, taps_at(kernel, sc.core * 1536 + at), activate)
        return steps

    def down_steps():
        def one(place, out, half, c):
            rows = pl.ds(pl.multiple_of(half * 768 + place * 384, LANES), 384)
            cols = slice(half * 768 + c, half * 768 + c + 256)
            out[:, cols] = dot(acts[:, rows], branch_grad[:, c : c + 256], 0, 0).astype(BF)

        return [
            step(one, place, out, half, c)
            for place, out in ((1 - sc.bits[0], send), (sc.bits[0], keep))
            for half in range(2)
            for c in range(0, 768, 256)
        ]

    weave(project_steps(0))
    for k in range(5):
        weave(local_steps(k), project_steps(k + 1))
    weave(local_steps(5))
    weave(down_steps())


def feed(line, normed, branch_grad, up, down, ffn_kernel):
    return run(
        feed_kernel, "feed", line, (normed, branch_grad, up, down, ffn_kernel),
        [shaped(384, 1536), shaped(384, 1536), shaped(1024, 1536), shaped(1024, 1536), shaped(1024, 1536)],
        [HELD, pltpu.VMEM((2, 1024, BLOCK), F32)], limit=18 * 1024 * 1024, us=13.0,
    )


def feed_back_kernel(
    sc, normed, up, down, kernel, acts, hid, d_conv,
    keep, send, kernel_grad, branch_keep, branch_send, normed_grad_out, held, d_hids, normed_grad,
):
    core = sc.core
    clear_margins(held)
    kernel_grad[...] = jnp.zeros(kernel_grad.shape, F32)

    def local_steps(at):
        cols = slice(at, at + LANES)

        def write(rows, total):
            d_hids[rows, cols] = total.astype(BF)

        def write_sums(values):
            kernel_grad[0:9, cols] = values

        return hold_steps(held, lambda g: d_conv[g * 256 : g * 256 + 256, cols].astype(F32)) + back_steps(
            held, taps_at(kernel, core * 1536 + at), lambda rows: hid[rows, cols].astype(F32), write,
            write_sums,
        )

    def up_steps(k):
        cols = slice(k * BLOCK, (k + 1) * BLOCK)

        def one(pair, out):
            at = pl.ds(pl.multiple_of(pair * 384, 384), 384)
            out[0:384, cols] = dot(normed[:, at], d_hids[:, cols], 0, 0).astype(BF)

        return [step(one, 1 - sc.bits[0], send), step(one, sc.bits[0], keep)]

    def branch_steps():
        def one(g):
            total = dot(acts[g * 256 : g * 256 + 256, :], down[...])
            for local in range(2):
                kept, sent = keep_half(core, total, local)
                branch_keep[2 * g + local] = kept
                branch_send[2 * g + local] = sent.astype(BF)

        return [step(one, g) for g in range(GROUPS)]

    def normed_steps():
        def one(r):
            normed_grad[r : r + 256, :] = dot(d_hids[r : r + 256, 0:768], up[:, 0:768], 1, 1)

        return [step(one, r) for r in range(0, 1024, 256)]

    branch = branch_steps()
    first = normed_steps()
    beside = branch[0:1], branch[1:3], branch[3:4], first[0:1], first[1:3], first[3:4]
    for k in range(6):
        weave(
            local_steps(k * BLOCK) + local_steps(k * BLOCK + LANES),
            (up_steps(k - 1) if k else []) + beside[k],
        )
    weave(up_steps(5))
    for r in range(0, 1024, 256):
        rows = slice(r, r + 256)
        total = normed_grad[rows, :] + dot(d_hids[rows, 768:1536], up[:, 768:1536], 1, 1)
        normed_grad_out[rows, :] = total.astype(BF)
    send[384 : 384 + TAPS, :] = kernel_grad[...].astype(BF)


def feed_back(line, normed, up, down, ffn_kernel, acts, hid, d_conv):
    return run(
        feed_back_kernel, "feed_back", line, (normed, up, down, ffn_kernel, acts, hid, d_conv),
        [shaped(384, 1536), shaped(384 + TAPS, 1536), shaped(TAPS, 1536, dtype=F32), shaped(8, 64, 768, dtype=F32),
         shaped(8, 64, 768), shaped(1024, 768)],
        [HELD, pltpu.VMEM((1024, 1536), BF), pltpu.VMEM((1024, 768), F32)], limit=20 * 1024 * 1024, us=14.0,
    )


def norm_back_kernel(
    sc, normed_grad, normed_grad_other, base, attended, seed, mod, mixed,
    middle_grad, att_grad, sums_out, out_keep, out_send,
):
    gate, scale, factor = mod[2:3, :], 1.0 + mod[4:5, :], mod[6:7, :]
    sums = [jnp.zeros((1, 768), F32) for _ in range(3)]

    def norm(r):
        rows = slice(r, r + 64)
        grad = normed_grad[rows, :].astype(F32) + normed_grad_other[rows, :].astype(F32)
        got = attended[rows, :].astype(F32)
        unit, inverse = normal(base[rows, :].astype(F32) + gate * got)
        both = grad * unit
        sums[0] = sums[0] + col_sum(grad)
        sums[1] = sums[1] + col_sum(both)
        grad = grad * scale
        mean = jnp.mean(grad, axis=-1, keepdims=True)
        along = jnp.mean(both * scale, axis=-1, keepdims=True)
        total = seed[rows, :].astype(F32) * factor + inverse * (grad - mean - unit * along)
        middle_grad[rows, :] = total
        sums[2] = sums[2] + col_sum(total * got)
        att_grad[rows, :] = (total * gate).astype(BF)

    for r in range(0, 1024, 64):
        norm(r)
    for k in range(3):
        sums_out[k : k + 1, :] = 0.5 * sums[k]
    for place, out in ((sc.bits[0], out_keep), (1 - sc.bits[0], out_send)):
        cols = pl.ds(pl.multiple_of(place * 384, 384), 384)
        out[...] = dot(mixed[...], att_grad[:, cols], 0, 0).astype(BF)


def norm_back(sc, normed_grad, normed_grad_other, base, attended, seed, mod, mixed):
    return run(
        norm_back_kernel, "norm_back", sc,
        (normed_grad, normed_grad_other, base, attended, seed, mod, mixed),
        [shaped(1024, 768, dtype=F32), shaped(1024, 768), shaped(3, 768, dtype=F32),
         shaped(384, 384), shaped(384, 384)], us=4.4
    )


def attend_back_kernel(
    heads, last, sc, att_grad, out_weight, normed, qkv, conv, prob, kernel, *rest,
):
    (*before, qkv_grad, weight_keep, weight_send, kernel_grad, held, d_mixed, d_conv) = rest
    kernel_grad[...] = jnp.zeros(kernel_grad.shape, F32)
    for given, out in zip(before, (weight_keep, weight_send, kernel_grad)):
        out[0 : given.shape[0], 384 : 384 + given.shape[1]] = given[...]
    core = sc.core
    at = 3 * heads * LANES
    clear_margins(held)
    mine_rows = slice(heads * LANES, heads * LANES + LANES)
    for r in range(0, 1024, 256):
        d_mixed[r : r + 256, :] = dot(att_grad[r : r + 256, :], out_weight[mine_rows, :], 1, 1).astype(BF)

    lane = iota((256, LANES), 1)
    low = lane < HEAD_DIM
    parts = {}

    def one(g, h):
        rows = slice(g * 256, g * 256 + 256)
        grad = d_mixed[rows, :]
        query = conv[rows, at : at + LANES]
        key = conv[rows, at + LANES : at + 2 * LANES]
        value = conv[rows, at + 2 * LANES : at + 3 * LANES]
        mine = low if h == 0 else jnp.logical_not(low)
        p = prob[heads, g, h]
        d_prob = dot(jnp.where(mine, grad, BF(0)), value, 1, 1)
        wide_p = p.astype(F32)
        inner = jnp.sum(d_prob * wide_p, axis=-1, keepdims=True)
        d_score = (wide_p * (d_prob - inner)).astype(BF)
        parts[h] = (dot(d_score, key), dot(d_score, query, 0, 0))
        if h == 1:
            for k in range(2):
                picked = jnp.where(low, parts[0][k], parts[1][k]) * HEAD_DIM**-0.5
                d_conv[rows, k * LANES : (k + 1) * LANES] = picked.astype(BF)

    def value_steps():
        def one(g):
            rows = slice(g * 256, g * 256 + 256)
            both = [dot(prob[heads, g, h], d_mixed[rows, :], 0, 0) for h in range(2)]
            d_conv[rows, 2 * LANES : 3 * LANES] = jnp.where(low, both[0], both[1]).astype(BF)

        return [step(one, g) for g in range(GROUPS)]

    def local_steps(s):
        cols = slice(s * LANES, (s + 1) * LANES)
        source_cols = slice(at + s * LANES, at + (s + 1) * LANES)

        def write(rows, total):
            qkv_grad[rows, cols] = total.astype(BF)

        def write_sums(values):
            kernel_grad[0:9, cols] = values

        weights = taps_at(kernel, 768 * s + 384 * core + LANES * heads)
        return hold_steps(
            held, lambda g: d_conv[g * 256 : g * 256 + 256, cols].astype(F32)
        ) + back_steps(held, weights, lambda rows: qkv[rows, source_cols].astype(F32), write, write_sums)

    def grad_steps(s):
        cols = slice(s * LANES, (s + 1) * LANES)

        def one(place, out):
            rows = pl.ds(pl.multiple_of(place * 384, 384), 384)
            out[0:384, cols] = dot(normed[:, rows], qkv_grad[:, cols], 0, 0).astype(BF)

        return [step(one, sc.bits[0], weight_keep), step(one, 1 - sc.bits[0], weight_send)]

    weave(value_steps())
    weave([step(one, g, h) for g in range(GROUPS) for h in range(2)], local_steps(2))
    weave(local_steps(0), grad_steps(2))
    weave(local_steps(1), grad_steps(0))
    weave(grad_steps(1))
    if last:
        weight_send[384 : 384 + TAPS, :] = kernel_grad[...].astype(BF)


def attend_back(line, heads, last, att_grad, out_weight, normed, qkv, conv, prob, attn_kernel, before):
    width = 384 + (before[0].shape[1] if before else 0)
    return run(
        functools.partial(attend_back_kernel, heads, last), "attend_back", line,
        (att_grad, out_weight, normed, qkv, conv, prob, attn_kernel, *before),
        [shaped(1024, 384), shaped(384, width), shaped(384 + (TAPS if last else 0), width),
         shaped(TAPS, width, dtype=F32)],
        [HELD, pltpu.VMEM((1024, LANES), BF), pltpu.VMEM((1024, 384), BF)], us=6.3,
    )


def first_back_kernel(sc, g0, g1, g2, weight, branch, keep, send):
    core = sc.core
    send[8:16] = branch[...]
    for g in range(GROUPS):
        rows = slice(g * 256, g * 256 + 256)
        total = None
        for k, grad in enumerate((g0, g1, g2)):
            part = dot(grad[rows, :], weight[:, 384 * k : 384 * k + 384], 1, 1)
            total = part if total is None else total + part
        for local in range(2):
            kept, sent = keep_half(core, total, local)
            keep[2 * g + local] = kept
            send[2 * g + local] = sent.astype(BF)


def first_back(line, grads, weight, branch):
    return run(
        first_back_kernel, "first_back", line, (*grads, weight, branch),
        [shaped(8, 64, 768, dtype=F32), shaped(16, 64, 768)], us=2.7
    )


def finish_kernel(
    sc, base, attended, branch, grad, other, seed, middle_grad, sums_two, mod, near_out, far_out, cond,
):
    height, breadth, core = sc.height, sc.breadth, sc.core
    scale, gate_one, gate, factor = 1.0 + mod[1:2, :], mod[2:3, :], mod[5:6, :], mod[6:7, :]
    matrix = to_phase_matrix()
    d_shift, d_scale, d_gate = [jnp.zeros((1, 768), F32) for _ in range(3)]
    done = []
    for local in range(2):
        outs, grads = [], []
        for g in range(GROUPS):
            at = 2 * g + local
            start = pl.multiple_of(g * 256 + (2 * local + core) * 64, 64)
            rows = pl.ds(start, 64)
            live = live_run(start, height, breadth)
            first = base[rows, :].astype(F32)
            whole = branch[at] + other[8 + at].astype(F32)
            d_gate = d_gate + col_sum(seed[rows, :].astype(F32) * whole)
            result = first + gate_one * attended[rows, :].astype(F32) + gate * whole
            outs.append((result * live).astype(BF))
            total = grad[at] + other[at].astype(F32)
            unit, inverse = normal(first)
            both = total * unit
            d_shift = d_shift + col_sum(total)
            d_scale = d_scale + col_sum(both)
            total = total * scale
            mean = jnp.mean(total, axis=-1, keepdims=True)
            along = jnp.mean(both * scale, axis=-1, keepdims=True)
            total = middle_grad[rows, :] + inverse * (total - mean - unit * along)
            grads.append((total * live).astype(BF))
        done.append([
            dot(matrix, jnp.concatenate(parts, axis=0), 0, 0).astype(BF) for parts in (outs, grads)
        ])

    @pl.when(sc.pair == 0)
    def _():
        for k in range(2):
            near_out[k] = done[0][k]
            far_out[k] = done[1][k]

    @pl.when(sc.pair != 0)
    def _():
        for k in range(2):
            near_out[k] = done[1][k]
            far_out[k] = done[0][k]

    rows = d_shift, d_scale, sums_two[2:3, :], sums_two[1:2, :], d_gate * factor, sums_two[0:1, :]
    for k, row in enumerate(rows):
        cond[k : k + 1, :] = row


def finish(line, *operands):
    return run(
        finish_kernel, "finish", line, operands,
        [shaped(2, 256, 768), shaped(2, 256, 768), shaped(6, 768, dtype=F32)], items=True, us=4.5,
    )


def swap(values, axis, bit):
    count = lax.axis_size(axis)
    return lax.ppermute(values, axis, [(i, i ^ bit) for i in range(count)])


def swap_at(values, k):
    wide, narrow = lax.axis_size(WIDE), lax.axis_size(NARROW)
    steps = {"x": (0, 2), "y": (1, 0), "z": (2, 0), "w": (4, 0)}
    pairs = []
    for w in range(wide):
        for n in range(narrow):
            dw, dn = steps[HALVINGS[n % 2][k]]
            pairs.append((w * narrow + n, (w ^ dw) * narrow + (n ^ dn)))
    return lax.ppermute(values, (WIDE, NARROW), pairs)


def bits_of(count):
    return [1 << k for k in range(count.bit_length() - 1)]


def halve_kernel(k, tapped, sc, kept, got, *rest):
    taps, rest = (rest[0], rest[1:]) if tapped else (None, rest)
    keep, send = rest[-3:-1] if tapped else rest[-2:]
    half = keep.shape[0]
    if tapped:
        rest[-1][...] = taps[...].astype(BF).astype(F32) + got[2 * half : 2 * half + TAPS, :].astype(F32)
        send[half : half + TAPS, :] = rest[-1][...].astype(BF)
    for d, out in enumerate((keep, send)):
        rows = pl.ds(pl.multiple_of((sc.bits[k] ^ d) * half, 16), half)
        out[0:half, :] = (kept[rows, :].astype(F32) + got[rows, :].astype(F32)).astype(BF)


def total_kernel(tapped, sc, kept, got, *rest):
    rows, width = kept.shape
    if tapped:
        taps, *rest, taps_out = rest
        taps_out[...] = taps[...].astype(BF).astype(F32) + got[rows : rows + TAPS, :].astype(F32)
    *cond, out = rest
    out[0:rows, :] = (kept[...].astype(F32) + got[0:rows, :].astype(F32)).astype(BF)
    if cond:
        count = (out.shape[0] - rows) * width // (6 * 768)
        hot = [jnp.where(sc.home == k, cond[0][...], 0.0) for k in range(count)]
        hot = jnp.concatenate(hot, axis=0).astype(BF)
        part = 6 * count * 768 // width
        for k in range(width // 768):
            out[rows : rows + part, 768 * k : 768 * k + 768] = hot[k * part : (k + 1) * part, :]


def stack_kernel(extra, tapped, sc, kept, got, *rest):
    *taps, out = rest
    half = kept.shape[0] - extra
    out[0:half, :] = kept[0:half, :]
    out[half : 2 * half, :] = got[0:half, :]
    if extra:
        below = slice(half, half + extra)
        out[2 * half : 2 * half + extra, :] = (
            kept[below, :].astype(F32) + got[below, :].astype(F32)
        ).astype(BF)
    if taps:
        out[2 * half + extra : 2 * half + extra + TAPS, :] = taps[0][...].astype(BF)


class Flow:
    def __init__(self, line, keep, send, taps=None):
        self.line = line
        self.taps = () if taps is None else (taps,)
        self.extra = 0
        for bit in bits_of(lax.axis_size(WIDE))[3:]:
            keep, send = [
                (v.astype(F32) + swap(v, WIDE, bit).astype(F32)).astype(BF) for v in (keep, send)
            ]
            self.taps = tuple(v + swap(v, WIDE, bit) for v in self.taps)
        self.kept, self.got = keep, swap_at(send, 0)

    def below(self):
        return [shaped(*v.shape, dtype=F32) for v in self.taps]

    def halve(self, k):
        rows, width = self.kept.shape
        tapped = len(self.taps) > 0
        self.kept, send, *self.taps = run(
            functools.partial(halve_kernel, k, tapped), "halve", self.line,
            (self.kept, self.got, *self.taps),
            [shaped(rows // 2, width), shaped(rows // 2 + (TAPS if tapped else 0), width)] + self.below(),
        )
        self.got = swap_at(send, k)

    def total(self, cond=None):
        rows, width = self.kept.shape
        if cond is not None:
            self.extra = 6 * lax.axis_size(WIDE) * 768 // width
        operands = (self.kept, self.got, *self.taps, *(() if cond is None else (cond,)))
        self.kept, *self.taps = run(
            functools.partial(total_kernel, len(self.taps) > 0), "total", self.line, operands,
            [shaped(rows + self.extra, width)] + self.below(), items=cond is not None,
        )
        self.got = swap_at(self.kept, 3)

    def stack(self, k):
        rows, width = self.kept.shape
        rows = 2 * (rows - self.extra) + self.extra
        taps = () if k else tuple(self.taps)
        (self.kept,) = run(
            functools.partial(stack_kernel, self.extra, len(taps) > 0), "stack", self.line,
            (self.kept, self.got, *taps), [shaped(rows + TAPS * len(taps), width)],
        )
        self.got = swap_at(self.kept, k - 1) if k else swap(self.kept, NARROW, 1)


def by_core(core, write, own, other):
    @pl.when(core == 0)
    def _():
        write(own, other)

    @pl.when(core != 0)
    def _():
        write(other, own)


def copy_each(steps, sems):
    copies = []
    for k, (fill, src, dst) in enumerate(steps):
        fill()
        copies.append(pltpu.make_async_copy(src, dst, sems.at[k]))
        copies[-1].start()
    for copy in copies:
        copy.wait()


def gathered_runs(chip):
    for group in range(4):
        runs_here = [
            (slice(48 * (4 * group + k), 48 * (4 * group + k + 1)),
             pl.ds(pl.multiple_of((k ^ (chip & 3)) * 48, 16), 48))
            for k in range(4)
        ]
        yield group, group ^ (chip >> 2), runs_here


def rows_at(start):
    return pl.ds(pl.multiple_of(start * 192, 64), 192)


def down_done_kernel(sc, own, other, out, buffer, sems):
    def fill(part, k, group, runs_here):
        for rows, dest in runs_here:
            for half in range(2):
                buffer[k, group, half, dest, :] = part[rows, 768 * half : 768 * half + 768].astype(F32)

    copy_each(
        [
            (step(fill, part, k, group, runs_here), buffer.at[k, group],
             out.at[core, :, rows_at(place), :])
            for k, (part, chip, core) in enumerate(
                ((own, sc.chip, sc.core), (other, sc.other_chip, 1 - sc.core))
            )
            for group, place, runs_here in gathered_runs(chip)
        ],
        sems,
    )


def down_done(line, flow):
    (out,) = run(
        down_done_kernel, "down_done", line, (flow.kept, flow.got), [shaped(2, 2, 768, 768, dtype=F32)],
        [pltpu.VMEM((2, 4, 2, 192, 768), F32), pltpu.SemaphoreType.DMA((8,))], far_outs=(0,),
        limit=12 * 1024 * 1024, us=4.0,
    )
    return out.reshape(3072, 768)


def up_done_kernel(sc, own, other, out, taps_out, buffer, sems):
    def write(first, second):
        for core, part in enumerate((first, second)):
            taps = part[768 : 768 + TAPS, :].astype(F32)
            for a in range(3):
                taps_out[a, :, 1536 * core : 1536 * core + 1536] = taps[3 * a : 3 * a + 3, :]

    by_core(sc.core, write, own, other)

    def fill(part, k, group, runs_here):
        for rows, dest in runs_here:
            buffer[k, group, dest, :] = part[rows, :].astype(F32)

    copy_each(
        [
            (step(fill, part, k, group, runs_here), buffer.at[k, group],
             out.at[rows_at(place), pl.ds(pl.multiple_of(core * 1536, 1536), 1536)])
            for k, (part, chip, core) in enumerate(
                ((own, sc.chip, sc.core), (other, sc.other_chip, 1 - sc.core))
            )
            for group, place, runs_here in gathered_runs(chip)
        ],
        sems,
    )


def up_done(line, flow):
    return run(
        up_done_kernel, "up_done", line, (flow.kept, flow.got),
        [shaped(768, 3072, dtype=F32), shaped(3, 3, 3072, dtype=F32)],
        [pltpu.VMEM((2, 4, 192, 1536), F32), pltpu.SemaphoreType.DMA((8,))], far_outs=(0,),
        limit=14 * 1024 * 1024, us=4.0,
    )


def attend_done_kernel(where, sc, *refs):
    count = (len(refs) - 8) // 2
    own, other = refs[:count], refs[count : 2 * count]
    qkv_grad, out_grad, taps_out, cond_out, shift_out, qkv, out, sems = refs[2 * count :]

    def fill(parts, k, group, runs_here, s):
        for rows, dest in runs_here:
            for heads in range(3):
                flow, col = where[heads]
                col = col + LANES * s
                qkv[k, group, s, dest, LANES * heads : LANES * heads + LANES] = parts[flow][
                    rows, col : col + LANES
                ].astype(F32)

    def fill_out(parts, k, group, runs_here):
        for rows, dest in runs_here:
            flow, col = where[3]
            out[k, group, dest, :] = parts[flow][rows, col : col + 384].astype(F32)

    steps = []
    for k, (parts, chip, core) in enumerate(
        ((own, sc.chip, sc.core), (other, sc.other_chip, 1 - sc.core))
    ):
        for group, place, runs_here in gathered_runs(chip):
            for s in range(3):
                cols = pl.ds(pl.multiple_of(768 * s + 384 * core, LANES), 384)
                steps.append((
                    step(fill, parts, k, group, runs_here, s), qkv.at[k, group, s],
                    qkv_grad.at[rows_at(place), cols],
                ))
            cols = pl.ds(pl.multiple_of((place >> 1) * 384, LANES), 384)
            steps.append((
                step(fill_out, parts, k, group, runs_here), out.at[k, group],
                out_grad.at[core, rows_at(place & 1), cols],
            ))

    def write(first, second):
        for core, parts in enumerate((first, second)):
            taps = [part[part.shape[0] - TAPS :, :].astype(F32) for part in parts]
            for a in range(3):
                for heads in range(3):
                    flow, col = where[heads]
                    for s in range(3):
                        to = 768 * s + 384 * core + LANES * heads
                        at = col + LANES * s
                        taps_out[a, :, to : to + LANES] = taps[flow][3 * a : 3 * a + 3, at : at + LANES]

    by_core(sc.core, write, own, other)
    mine, its = own[-1], other[-1]
    extra = mine.shape[0] - 768 - TAPS
    total = mine[768 : 768 + extra, :].astype(F32) + its[768 : 768 + extra, :].astype(F32)
    rows = jnp.zeros((6, 768), F32)
    for k in range(extra // 6):
        rows = rows + jnp.where(sc.wide == k, total[6 * k : 6 * k + 6, :], 0.0)
    for k in range(5):
        cond_out[:, 768 * k : 768 * k + 768] = rows[k : k + 1, :]
    shift_out[...] = rows[5:6, :]
    copy_each(steps, sems)


def attend_done(line, where, flows):
    qkv_grad, out_grad, attn_grad, cond_grad, shift_grad = run(
        functools.partial(attend_done_kernel, where), "attend_done", line,
        [flow.kept for flow in flows] + [flow.got for flow in flows],
        [shaped(768, 2304, dtype=F32), shaped(2, 384, 768, dtype=F32), shaped(3, 3, 2304, dtype=F32),
         shaped(1, 3840, dtype=F32), shaped(1, 768, dtype=F32)],
        [pltpu.VMEM((2, 4, 3, 192, 384), F32), pltpu.VMEM((2, 4, 192, 384), F32),
         pltpu.SemaphoreType.DMA((32,))],
        far_outs=(0, 1), limit=16 * 1024 * 1024, us=4.0,
    )
    return qkv_grad, out_grad.reshape(768, 768), attn_grad, cond_grad, shift_grad


def join_kernel(sc, near, far, out, grad_out):
    for k, target in enumerate((out, grad_out)):
        target[sc.pair] = near[k]
        target[1 - sc.pair] = far[k]


def join(line, near, far):
    out, grad = run(join_kernel, "join", line, (near, far), [shaped(2, 256, 768)] * 2)
    return out.reshape(2, 8, 32, 768), grad.reshape(2, 8, 32, 768)


def copy_all(sems, pairs):
    copies = [pltpu.make_async_copy(src, dst, sems.at[k]) for k, (src, dst) in enumerate(pairs)]
    for copy in copies:
        copy.start()
    for copy in copies:
        copy.wait()


def cut_pieces_kernel(sc, block, far, own, sems):
    copy_all(sems, [(block.at[1 - sc.pair], far), (block.at[sc.pair], own)])


def cut_pieces(line, block):
    return run(
        cut_pieces_kernel, "cut_pieces", line, (block.reshape(2, 256, 768),), [shaped(256, 768)] * 2,
        [pltpu.SemaphoreType.DMA((2,))], far=(0,), limit=ALL_VMEM,
    )


def pass_kernel(sc, *refs):
    count = len(refs) // 2
    for k in range(count):
        refs[count + k][...] = refs[k][...]


def pass_on(line, *arrays):
    return run(pass_kernel, "pass_on", line, arrays, [shaped(*v.shape) for v in arrays])


def pack_kernel(sc, one, two, out):
    out[0:256, :] = one[...]
    out[256:512, :] = two[...]


def cut_weights_kernel(sc, qkv, out, up, down, qkv_part, out_part, up_part, down_part, sems):
    core = sc.core
    pairs = [
        (
            qkv.at[:, lanes_at(768 * s + 384 * core + LANES * pair)],
            qkv_part.at[:, pl.ds((3 * pair + s) * LANES, LANES)],
        )
        for pair in range(3)
        for s in range(3)
    ]
    pairs += [
        (out.at[pl.ds(pl.multiple_of(384 * core, 384), 384), :], out_part),
        (up.at[:, pl.ds(pl.multiple_of(1536 * core, 1536), 1536)], up_part),
        (down.at[pl.ds(pl.multiple_of(1536 * core, 1536), 1536), :], down_part),
    ]
    copy_all(sems, pairs)


def cut_weights(line, qkv_weight, out_weight, up_weight, down_weight):
    return run(
        cut_weights_kernel, "cut_weights", line, (qkv_weight, out_weight, up_weight, down_weight),
        [shaped(768, 1152), shaped(384, 768), shaped(768, 1536), shaped(1536, 768)],
        [pltpu.SemaphoreType.DMA((12,))], far=(0, 1, 2, 3), limit=ALL_VMEM, us=2.5
    )


def on_device(
    tokens, cotangent, conditioning, aspect, bucket,
    qkv_weight, attn_kernel, out_weight, up_weight, ffn_kernel, down_weight,
):
    wide_count = lax.axis_size(WIDE)
    line = Line(aspect, bucket)
    far, own = cut_pieces(line, tokens)
    got = swap(far, NARROW, 2)
    own_other = swap(own, NARROW, 1)
    cond_right = lax.ppermute(conditioning, WIDE, [(i + 1, i) for i in range(wide_count - 1)])
    weights = cut_weights(line, qkv_weight, out_weight, up_weight, down_weight)
    qkv_part, out_part, up_part, down_part = weights
    seed_far, seed_own = cut_pieces(line, cotangent)
    got, cond_right = pass_on(line, got, cond_right)
    token_pieces = own, got, own_other, swap(got, NARROW, 1)
    base, normed_one, qkv, conv, prob, mixed, mod = attend(
        line, token_pieces, conditioning, cond_right, qkv_part, attn_kernel
    )
    (seeds,) = run(pack_kernel, "pack", line, (seed_own, swap(seed_far, NARROW, 2)), [shaped(512, 768)])
    mixed_other = swap(mixed, NARROW, 1)
    seed_pieces = seeds, swap(seeds, NARROW, 1)
    attended, normed_two, d_branch, seed = project_out(
        line, mixed, mixed_other, base, out_weight, mod, seed_pieces
    )

    def back(heads, last, d_att, before):
        return attend_back(
            line, heads, last, d_att, out_part, normed_one, qkv, conv, prob, attn_kernel, before
        )

    keep, send, *saved = feed(line, normed_two, d_branch, up_part, down_part, ffn_kernel)
    a = Flow(line, keep, send)
    keep, send, taps, branch, branch_send, d_normed = feed_back(
        line, normed_two, up_part, down_part, ffn_kernel, *saved
    )
    b = Flow(line, keep, send, taps)
    a.halve(1)
    (d_normed_send,) = pass_on(line, d_normed)
    d_normed_other = swap(d_normed_send, NARROW, 1)
    d_middle, d_att, sums_two, *parts = norm_back(
        line, d_normed, d_normed_other, base, attended, seed, mod, mixed
    )
    g0, *parts = back(0, True, d_att, parts)
    c = Flow(line, *parts)
    g1, *parts = back(1, False, d_att, ())
    a.halve(2)
    a.halve(3)
    c.halve(1)
    b.halve(1)
    g2, *parts = back(2, True, d_att, parts)
    d = Flow(line, *parts)
    a.total()
    b.halve(2)
    d_first, d_first_send = first_back(line, (g0, g1, g2), qkv_part, branch_send)
    d.halve(1)
    b.halve(3)
    a.stack(3)
    c.halve(2)
    (d_first_send,) = pass_on(line, d_first_send)
    d_first_other = swap(d_first_send, NARROW, 1)
    a.stack(2)
    near, far, cond = finish(
        line, base, attended, branch, d_first, d_first_other, seed, d_middle, sums_two, mod
    )
    far = swap(far, NARROW, 2)
    d.halve(2)
    c.halve(3)
    b.total()
    a.stack(1)
    b.stack(3)
    c.total()
    d.halve(3)
    block_out, tokens_grad = join(line, near, far)
    c.stack(3)
    b.stack(2)
    b.stack(1)
    c.stack(2)
    d.total(cond)
    a.stack(0)
    d.stack(3)
    b.stack(0)
    d.stack(2)
    c.stack(1)
    d.stack(1)
    c.stack(0)
    down_grad = down_done(line, a)
    d.stack(0)
    up_grad, ffn_grad = up_done(line, b)
    where = (0, 0), (1, 384), (1, 0), (0, 384)
    qkv_grad, out_grad, attn_grad, cond_grad, shift_grad = attend_done(line, where, (c, d))

    return (
        block_out, tokens_grad, cond_grad, shift_grad, qkv_grad, attn_grad, out_grad, up_grad, ffn_grad,
        down_grad,
    )


def solution(mesh):
    rows = P(WIDE, NARROW, None, None)
    in_specs = (rows, rows, P(WIDE, None)) + (P(),) * 8
    out_specs = (rows, rows, P(WIDE, None), P(WIDE, None)) + (P(),) * 6
    return jax.shard_map(
        on_device, mesh=mesh, in_specs=in_specs, out_specs=out_specs, check_vma=False
    )
```

```python
import functools

import jax
import jax.numpy as jnp
from jax import lax
from jax.experimental import pallas as pl
from jax.experimental.pallas import tpu as pltpu
from jax.sharding import PartitionSpec as P

HEAD_DIM = 64
TAPS = 16
WIDE = "wide"
NARROW = "narrow"
LANES = 128
GROUPS = 4
MARGIN = 16

masked_score = -1000000000.0
norm_epsilon = 1e-06
gelu_root = 0.7978845608028654
gelu_cube = 0.044715

BF = jnp.bfloat16
F32 = jnp.float32
SCRATCH = 16 * 1024 * 1024
ALL_VMEM = 61 * 1024 * 1024
COST = 1150000000


def dot(left, right, left_dim=1, right_dim=0):
    return lax.dot_general(
        left, right, (((left_dim,), (right_dim,)), ((), ())), preferred_element_type=F32
    )


ANYWHERE = pl.BlockSpec(memory_space=pl.ANY)
DISTANT = pl.BlockSpec(memory_space=pltpu.HBM)
SCALARS = pl.BlockSpec(memory_space=pltpu.SMEM)
HERE = pl.BlockSpec(memory_space=pltpu.VMEM)


def shaped(*shape, dtype=BF):
    return jax.ShapeDtypeStruct(shape, dtype)


HALVINGS = ("x", "y", "z", "w"), ("y", "z", "x", "w")


class Place:
    def __init__(self, aspect=None, bucket=None):
        wide, narrow = lax.axis_index(WIDE), lax.axis_index(NARROW)
        self.wide = wide
        self.pair, self.core = narrow // 2, narrow % 2
        bits = {"x": self.pair, "y": wide % 2, "z": (wide // 2) % 2, "w": (wide // 4) % 2}
        self.bits = [
            jnp.where(self.core == 0, bits[first], bits[second]) for first, second in zip(*HALVINGS)
        ]
        self.chip = self.chip_of(self.bits)
        self.other_chip = self.chip_of(
            [jnp.where(self.core == 0, bits[second], bits[first]) for first, second in zip(*HALVINGS)]
        )
        self.pieces = (
            narrow, 2 * (1 - self.pair) + self.core, 2 * self.pair + 1 - self.core,
            2 * (1 - self.pair) + 1 - self.core,
        )
        if aspect is not None:
            item = 2 * wide + self.pair
            self.height, self.breadth = aspect[item, 0], aspect[item, 1]
            self.home = bucket[item]
            self.stays = self.home == wide

    def chip_of(self, bits):
        return 8 * bits[0] + 4 * bits[1] + 2 * bits[2] + bits[3]


class Line:
    def __init__(self, aspect, bucket):
        self.items = aspect, bucket
        self.token = None


def run(kernel, name, line, operands, outs, scratch=(), limit=SCRATCH, items=False, far=(), far_outs=(), us=1.0):
    count = len(operands)
    tokens = [] if line.token is None else [line.token]
    scalars = list(line.items) if items else []

    def body(*refs):
        place = Place(*refs[: len(scalars)])
        refs = refs[len(scalars) :]
        refs = refs[:count] + refs[count + len(tokens) :]
        refs[count + len(outs)][...] = jnp.zeros((8, LANES), F32)
        kernel(place, *refs[: count + len(outs)], *refs[count + len(outs) + 1 :])

    *made, line.token = pl.pallas_call(
        body,
        in_specs=[SCALARS] * len(scalars)
        + [DISTANT if k in far else HERE for k in range(count)]
        + [ANYWHERE] * len(tokens),
        out_specs=[DISTANT if k in far_outs else HERE for k in range(len(outs))] + [HERE],
        out_shape=[*outs, shaped(8, LANES, dtype=F32)],
        scratch_shapes=list(scratch),
        compiler_params=pltpu.CompilerParams(vmem_limit_bytes=limit),
        cost_estimate=pl.CostEstimate(flops=int(us * COST), bytes_accessed=1, transcendentals=0),
        name=name,
    )(*scalars, *operands, *tokens)
    return made


def step(f, *given):
    return functools.partial(f, *given)


def weave(*lists):
    order = sorted(
        ((at + 0.5) / len(steps), which, at)
        for which, steps in enumerate(lists)
        for at in range(len(steps))
    )
    for _, which, at in order:
        lists[which][at]()


def iota(shape, dim):
    return lax.broadcasted_iota(jnp.int32, shape, dim)


def live_rows(token, height, breadth):
    row = 2 * ((token >> 4) & 15) + (token >> 9)
    col = 2 * (token & 15) + ((token >> 8) & 1)
    return ((row < height) & (col < breadth)).astype(F32)


def live_run(start, height, breadth):
    return live_rows(start + iota((64, 1), 0), height, breadth)


def to_phase_matrix():
    row = iota((256, 256), 0)
    col = iota((256, 256), 1)
    grid_row = 2 * ((row >> 4) & 3) + (row >> 7)
    grid_col = 2 * (row & 15) + ((row >> 6) & 1)
    return (col == grid_row * 32 + grid_col).astype(F32).astype(BF)


def normal(values):
    center = values - jnp.mean(values, axis=-1, keepdims=True)
    scale = lax.rsqrt(jnp.mean(center * center, axis=-1, keepdims=True) + norm_epsilon)
    return center * scale, scale


def col_sum(values):
    return jnp.sum(values, axis=0, keepdims=True)


HELD = pltpu.VMEM((2 * GROUPS, 2 * MARGIN + 256, LANES), F32)
STEP = 64


def clear_margins(held):
    zero = jnp.zeros((2 * GROUPS, MARGIN, LANES), F32)
    held[:, 0:MARGIN, :] = zero
    held[:, MARGIN + 256 : 2 * MARGIN + 256, :] = zero


def hold_steps(held, read):
    place = iota((256, LANES), 0) & 15

    def one(g):
        values = read(g)
        held[2 * g, MARGIN : MARGIN + 256, :] = values
        if g % 2:
            moved = jnp.where(place == 0, 0.0, pltpu.roll(values, 1, 0))
        else:
            moved = jnp.where(place == 15, 0.0, pltpu.roll(values, 255, 0))
        held[2 * g + 1, MARGIN : MARGIN + 256, :] = moved

    return [step(one, g) for g in range(GROUPS)]


def taps(g):
    alpha, beta = g // 2, g % 2
    out = []
    for a in range(3):
        for b in range(3):
            row = alpha + a - 1
            col = beta + b - 1
            src = 2 * (row % 2) + col % 2
            out.append((a, b, 2 * src + (0 if 0 <= col <= 1 else 1), MARGIN * (row // 2)))
    return out


def tap_weights(kernel):
    return [[kernel[3 * a + b : 3 * a + b + 1, :] for b in range(3)] for a in range(3)]


def taps_at(kernel, start):
    cols = lanes_at(start)
    return jnp.concatenate([kernel[a, :, cols].astype(F32) for a in range(3)], axis=0)


def runs():
    return [(g, start) for g in range(GROUPS) for start in range(0, 256, STEP)]


def run_rows(g, start):
    return slice(g * 256 + start, g * 256 + start + STEP)


def conv_steps(held, kernel, write):
    weights = tap_weights(kernel)

    def one(g, start):
        total = None
        for a, b, src, off in taps(g):
            part = weights[a][b] * held[src, MARGIN + off + start : MARGIN + off + start + STEP, :]
            total = part if total is None else total + part
        write(run_rows(g, start), total)

    return [step(one, *at) for at in runs()]


def back_steps(held, kernel, read, write, write_sums):
    weights = tap_weights(kernel)
    sums = [None] * 9

    def one(g, start):
        given = read(run_rows(g, start))
        total = None
        for a, b, src, off in taps(g):
            window = held[src, MARGIN + off + start : MARGIN + off + start + STEP, :]
            part = weights[2 - a][2 - b] * window
            total = part if total is None else total + part
            at = 3 * (2 - a) + 2 - b
            prod = jnp.sum((given * window).reshape(STEP // 8, 8, LANES), axis=0)
            sums[at] = prod if sums[at] is None else sums[at] + prod
        write(run_rows(g, start), total)

    def last():
        write_sums(jnp.concatenate([col_sum(v) for v in sums], axis=0))

    return [step(one, *at) for at in runs()] + [last]


def lanes_at(start):
    return pl.ds(pl.multiple_of(start, LANES), LANES)


def attend_kernel(
    sc, p0, p1, p2, p3, cond, cond_right, weight, kernel,
    base_out, normed_out, qkv_out, conv_out, prob_out, mixed_out, mod,
    held,
):
    height, breadth, core = sc.height, sc.breadth, sc.core
    clear_margins(held)
    for k in range(6):
        cols = slice(768 * k, 768 * k + 768)
        mod[k : k + 1, :] = jnp.where(sc.stays, cond[:, cols].astype(F32), cond_right[:, cols].astype(F32))
    tokens = (height * breadth).astype(F32)
    mod[6:8, :] = jnp.full((2, 768), 1024.0, F32) / tokens
    shift, scale = mod[0:1, :], 1.0 + mod[1:2, :]
    matrix = to_phase_matrix()

    def norm(k, piece, g):
        start = pl.multiple_of(g * 256 + sc.pieces[k] * 64, 64)
        moved = dot(matrix[g * 64 : g * 64 + 64, :], piece[...])
        values = moved * live_run(start, height, breadth)
        base_out[pl.ds(start, 64), :] = values.astype(BF)
        normed_out[pl.ds(start, 64), :] = (normal(values)[0] * scale + shift).astype(BF)

    def norm_steps(g):
        return [step(norm, k, piece, g) for k, piece in enumerate((p0, p1, p2, p3))]

    def project(col, r):
        cols = slice(col, min(col + 256, 1152))
        qkv_out[r : r + 256, cols] = dot(normed_out[r : r + 256, :], weight[:, cols]).astype(BF)

    def project_steps(cols, rows=range(0, 1024, 256)):
        return [step(project, col, r) for col in cols for r in rows]

    def conv_pair(pair):
        steps = []
        for s in range(3):
            at = (3 * pair + s) * LANES
            cols = slice(at, at + LANES)

            def read(g, cols=cols):
                return qkv_out[g * 256 : g * 256 + 256, cols].astype(F32)

            def write(rows, total, cols=cols):
                conv_out[rows, cols] = total.astype(BF)

            steps += hold_steps(held, read)
            weights = taps_at(kernel, 768 * s + 384 * core + LANES * pair)
            steps += conv_steps(held, weights, write)
        return steps

    token = iota((1, 256), 1)
    lane = iota((256, LANES), 1)

    def attend_pair(pair):
        at = 3 * pair * LANES
        parts = {}

        def one(g, h):
            rows = slice(g * 256, g * 256 + 256)
            live = live_rows(token + g * 256, height, breadth) > 0.5
            query = conv_out[rows, at : at + LANES] * BF(HEAD_DIM**-0.5)
            key = conv_out[rows, at + LANES : at + 2 * LANES]
            value = conv_out[rows, at + 2 * LANES : at + 3 * LANES]
            mine = (lane < HEAD_DIM) if h == 0 else (lane >= HEAD_DIM)
            score = dot(jnp.where(mine, query, BF(0)), key, 1, 1)
            score = jnp.where(live, score, masked_score)
            top = jnp.max(score, axis=-1, keepdims=True)
            raised = jnp.exp(score - top)
            prob = (raised * (1.0 / jnp.sum(raised, axis=-1, keepdims=True))).astype(BF)
            prob_out[pair, g, h] = prob
            parts[h] = dot(prob, value)
            if h == 1:
                both = jnp.where(lane < HEAD_DIM, parts[0], parts[1])
                mixed_out[rows, pair * LANES : pair * LANES + LANES] = both.astype(BF)

        return [step(one, g, h) for g in range(GROUPS) for h in range(2)]

    weave(norm_steps(0))
    for g in range(1, GROUPS):
        weave(norm_steps(g), project_steps((0, 256), (256 * g - 256,)))
    weave(project_steps((0, 256), (768,)))
    weave(conv_pair(0), project_steps((512, 768, 1024)))
    weave(attend_pair(0), conv_pair(1))
    weave(attend_pair(1), conv_pair(2))
    weave(attend_pair(2))


def attend(line, pieces, cond, cond_right, weight, attn_kernel):
    return run(
        attend_kernel, "attend", line, (*pieces, cond, cond_right, weight, attn_kernel),
        [shaped(1024, 768), shaped(1024, 768), shaped(1024, 1152), shaped(1024, 1152),
         shaped(3, GROUPS, 2, 256, 256), shaped(1024, 384), shaped(8, 768, dtype=F32)],
        [HELD], items=True, us=11.5
    )


def middle_kernel(
    sc, mixed_own, mixed_other, base, out_weight, mod, seeds, seeds_other,
    attended_out, normed_out, branch_grad_out, seed_out,
    mixed, attended,
):
    height, breadth, core = sc.height, sc.breadth, sc.core
    mixed[:, pl.ds(pl.multiple_of(core * 384, LANES), 384)] = mixed_own[...]
    mixed[:, pl.ds(pl.multiple_of((1 - core) * 384, LANES), 384)] = mixed_other[...]
    gate = mod[2:3, :]
    shift, scale = mod[3:4, :], 1.0 + mod[4:5, :]
    gate_two, factor = mod[5:6, :], mod[6:7, :]
    matrix = to_phase_matrix()

    def project(r):
        attended[r : r + 256, :] = dot(mixed[r : r + 256, :], out_weight[...])

    def norm(r):
        rows = slice(r, r + 64)
        got = attended[rows, :].astype(BF)
        attended_out[rows, :] = got
        middle = base[rows, :].astype(F32) + gate * got.astype(F32)
        normed_out[rows, :] = (normal(middle)[0] * scale + shift).astype(BF)

    def seed(k, piece, g):
        start = pl.multiple_of(g * 256 + sc.pieces[k] * 64, 64)
        moved = dot(matrix[g * 64 : g * 64 + 64, :], piece[256 * (k % 2) : 256 * (k % 2) + 256, :])
        values = moved * live_run(start, height, breadth)
        seed_out[pl.ds(start, 64), :] = values.astype(BF)
        branch_grad_out[pl.ds(start, 64), :] = (values * factor * gate_two).astype(BF)

    project(0)
    weave([step(project, r) for r in (256, 512, 768)], [step(norm, r) for r in range(0, 768, 64)],
          [step(seed, k, piece, g) for k, piece in enumerate((seeds, seeds, seeds_other, seeds_other))
           for g in range(GROUPS)])
    weave([step(norm, r) for r in range(768, 1024, 64)])


def project_out(sc, mixed_own, mixed_other, base, out_weight, mod, pieces):
    return run(
        middle_kernel, "project_out", sc, (mixed_own, mixed_other, base, out_weight, mod, *pieces),
        [shaped(1024, 768)] * 4,
        [pltpu.VMEM((1024, 768), BF), pltpu.VMEM((1024, 768), F32)], items=True, us=4.6
    )


BLOCK = 256


def keep_half(core, values, local):
    low = values[128 * local : 128 * local + 64, :]
    high = values[128 * local + 64 : 128 * local + 128, :]
    return jnp.where(core == 0, low, high), jnp.where(core == 0, high, low)


def gelu_parts(v):
    square = v * v
    bent = jnp.tanh(v * (gelu_root + (gelu_root * gelu_cube) * square))
    rise = 0.5 + 0.5 * bent
    value = v * rise
    slope = rise + value * (1.0 - bent) * (gelu_root + (3.0 * gelu_root * gelu_cube) * square)
    return value, slope


def feed_kernel(sc, normed, branch_grad, up, down, kernel, keep, send, acts, hid, d_conv, held, d_act):
    clear_margins(held)

    def project_steps(k):
        cols = slice(k * BLOCK, (k + 1) * BLOCK)
        place = k % 2

        def one(r):
            hid[r : r + 256, cols] = dot(normed[r : r + 256, :], up[:, cols]).astype(BF)

        def two(r):
            d_act[place, r : r + 256, :] = dot(branch_grad[r : r + 256, :], down[cols, :], 1, 1)

        return [step(f, r) for r in range(0, 1024, 256) for f in (one, two)]

    def local_steps(k):
        steps = []
        place = k % 2
        for lane_block in range(BLOCK // LANES):
            cols = slice(lane_block * LANES, (lane_block + 1) * LANES)
            at = k * BLOCK + lane_block * LANES
            dest = slice(at, at + LANES)

            def read(g, dest=dest):
                return hid[g * 256 : g * 256 + 256, dest].astype(F32)

            def activate(rows, v, cols=cols, dest=dest):
                value, slope = gelu_parts(v)
                acts[rows, dest] = value.astype(BF)
                d_conv[rows, dest] = (d_act[place, rows, cols] * slope).astype(BF)

            steps += hold_steps(held, read)
            steps += conv_steps(held, taps_at(kernel, sc.core * 1536 + at), activate)
        return steps

    def down_steps():
        def one(place, out, half, c):
            rows = pl.ds(pl.multiple_of(half * 768 + place * 384, LANES), 384)
            cols = slice(half * 768 + c, half * 768 + c + 256)
            out[:, cols] = dot(acts[:, rows], branch_grad[:, c : c + 256], 0, 0).astype(BF)

        return [
            step(one, place, out, half, c)
            for place, out in ((1 - sc.bits[0], send), (sc.bits[0], keep))
            for half in range(2)
            for c in range(0, 768, 256)
        ]

    weave(project_steps(0))
    for k in range(5):
        weave(local_steps(k), project_steps(k + 1))
    weave(local_steps(5))
    weave(down_steps())


def feed(line, normed, branch_grad, up, down, ffn_kernel):
    return run(
        feed_kernel, "feed", line, (normed, branch_grad, up, down, ffn_kernel),
        [shaped(384, 1536), shaped(384, 1536), shaped(1024, 1536), shaped(1024, 1536), shaped(1024, 1536)],
        [HELD, pltpu.VMEM((2, 1024, BLOCK), F32)], limit=18 * 1024 * 1024, us=13.0,
    )


def feed_back_kernel(
    sc, normed, up, down, kernel, acts, hid, d_conv,
    keep, send, kernel_grad, branch_keep, branch_send, normed_grad_out, held, d_hids, normed_grad,
):
    core = sc.core
    clear_margins(held)
    kernel_grad[...] = jnp.zeros(kernel_grad.shape, F32)

    def local_steps(at):
        cols = slice(at, at + LANES)

        def write(rows, total):
            d_hids[rows, cols] = total.astype(BF)

        def write_sums(values):
            kernel_grad[0:9, cols] = values

        return hold_steps(held, lambda g: d_conv[g * 256 : g * 256 + 256, cols].astype(F32)) + back_steps(
            held, taps_at(kernel, core * 1536 + at), lambda rows: hid[rows, cols].astype(F32), write,
            write_sums,
        )

    def up_steps(k):
        cols = slice(k * BLOCK, (k + 1) * BLOCK)

        def one(pair, out):
            at = pl.ds(pl.multiple_of(pair * 384, 384), 384)
            out[0:384, cols] = dot(normed[:, at], d_hids[:, cols], 0, 0).astype(BF)

        return [step(one, 1 - sc.bits[0], send), step(one, sc.bits[0], keep)]

    def branch_steps():
        def one(g):
            total = dot(acts[g * 256 : g * 256 + 256, :], down[...])
            for local in range(2):
                kept, sent = keep_half(core, total, local)
                branch_keep[2 * g + local] = kept
                branch_send[2 * g + local] = sent.astype(BF)

        return [step(one, g) for g in range(GROUPS)]

    def normed_steps():
        def one(r):
            normed_grad[r : r + 256, :] = dot(d_hids[r : r + 256, 0:768], up[:, 0:768], 1, 1)

        return [step(one, r) for r in range(0, 1024, 256)]

    branch = branch_steps()
    first = normed_steps()
    beside = branch[0:1], branch[1:3], branch[3:4], first[0:1], first[1:3], first[3:4]
    for k in range(6):
        weave(
            local_steps(k * BLOCK) + local_steps(k * BLOCK + LANES),
            (up_steps(k - 1) if k else []) + beside[k],
        )
    weave(up_steps(5))
    for r in range(0, 1024, 256):
        rows = slice(r, r + 256)
        total = normed_grad[rows, :] + dot(d_hids[rows, 768:1536], up[:, 768:1536], 1, 1)
        normed_grad_out[rows, :] = total.astype(BF)
    send[384 : 384 + TAPS, :] = kernel_grad[...].astype(BF)


def feed_back(line, normed, up, down, ffn_kernel, acts, hid, d_conv):
    return run(
        feed_back_kernel, "feed_back", line, (normed, up, down, ffn_kernel, acts, hid, d_conv),
        [shaped(384, 1536), shaped(384 + TAPS, 1536), shaped(TAPS, 1536, dtype=F32), shaped(8, 64, 768, dtype=F32),
         shaped(8, 64, 768), shaped(1024, 768)],
        [HELD, pltpu.VMEM((1024, 1536), BF), pltpu.VMEM((1024, 768), F32)], limit=20 * 1024 * 1024, us=14.0,
    )


def norm_back_kernel(
    sc, normed_grad, normed_grad_other, base, attended, seed, mod, mixed,
    middle_grad, att_grad, sums_out, out_keep, out_send,
):
    gate, scale, factor = mod[2:3, :], 1.0 + mod[4:5, :], mod[6:7, :]
    sums = [jnp.zeros((1, 768), F32) for _ in range(3)]

    def norm(r):
        rows = slice(r, r + 64)
        grad = normed_grad[rows, :].astype(F32) + normed_grad_other[rows, :].astype(F32)
        got = attended[rows, :].astype(F32)
        unit, inverse = normal(base[rows, :].astype(F32) + gate * got)
        both = grad * unit
        sums[0] = sums[0] + col_sum(grad)
        sums[1] = sums[1] + col_sum(both)
        grad = grad * scale
        mean = jnp.mean(grad, axis=-1, keepdims=True)
        along = jnp.mean(both * scale, axis=-1, keepdims=True)
        total = seed[rows, :].astype(F32) * factor + inverse * (grad - mean - unit * along)
        middle_grad[rows, :] = total
        sums[2] = sums[2] + col_sum(total * got)
        att_grad[rows, :] = (total * gate).astype(BF)

    for r in range(0, 1024, 64):
        norm(r)
    for k in range(3):
        sums_out[k : k + 1, :] = 0.5 * sums[k]
    for place, out in ((sc.bits[0], out_keep), (1 - sc.bits[0], out_send)):
        cols = pl.ds(pl.multiple_of(place * 384, 384), 384)
        out[...] = dot(mixed[...], att_grad[:, cols], 0, 0).astype(BF)


def norm_back(sc, normed_grad, normed_grad_other, base, attended, seed, mod, mixed):
    return run(
        norm_back_kernel, "norm_back", sc,
        (normed_grad, normed_grad_other, base, attended, seed, mod, mixed),
        [shaped(1024, 768, dtype=F32), shaped(1024, 768), shaped(3, 768, dtype=F32),
         shaped(384, 384), shaped(384, 384)], us=4.4
    )


def attend_back_kernel(
    heads, last, sc, att_grad, out_weight, normed, qkv, conv, prob, kernel, *rest,
):
    (*before, qkv_grad, weight_keep, weight_send, kernel_grad, held, d_mixed, d_conv) = rest
    kernel_grad[...] = jnp.zeros(kernel_grad.shape, F32)
    for given, out in zip(before, (weight_keep, weight_send, kernel_grad)):
        out[0 : given.shape[0], 384 : 384 + given.shape[1]] = given[...]
    core = sc.core
    at = 3 * heads * LANES
    clear_margins(held)
    mine_rows = slice(heads * LANES, heads * LANES + LANES)
    for r in range(0, 1024, 256):
        d_mixed[r : r + 256, :] = dot(att_grad[r : r + 256, :], out_weight[mine_rows, :], 1, 1).astype(BF)

    lane = iota((256, LANES), 1)
    low = lane < HEAD_DIM
    parts = {}

    def one(g, h):
        rows = slice(g * 256, g * 256 + 256)
        grad = d_mixed[rows, :]
        query = conv[rows, at : at + LANES]
        key = conv[rows, at + LANES : at + 2 * LANES]
        value = conv[rows, at + 2 * LANES : at + 3 * LANES]
        mine = low if h == 0 else jnp.logical_not(low)
        p = prob[heads, g, h]
        d_prob = dot(jnp.where(mine, grad, BF(0)), value, 1, 1)
        wide_p = p.astype(F32)
        inner = jnp.sum(d_prob * wide_p, axis=-1, keepdims=True)
        d_score = (wide_p * (d_prob - inner)).astype(BF)
        parts[h] = (dot(d_score, key), dot(d_score, query, 0, 0))
        if h == 1:
            for k in range(2):
                picked = jnp.where(low, parts[0][k], parts[1][k]) * HEAD_DIM**-0.5
                d_conv[rows, k * LANES : (k + 1) * LANES] = picked.astype(BF)

    def value_steps():
        def one(g):
            rows = slice(g * 256, g * 256 + 256)
            both = [dot(prob[heads, g, h], d_mixed[rows, :], 0, 0) for h in range(2)]
            d_conv[rows, 2 * LANES : 3 * LANES] = jnp.where(low, both[0], both[1]).astype(BF)

        return [step(one, g) for g in range(GROUPS)]

    def local_steps(s):
        cols = slice(s * LANES, (s + 1) * LANES)
        source_cols = slice(at + s * LANES, at + (s + 1) * LANES)

        def write(rows, total):
            qkv_grad[rows, cols] = total.astype(BF)

        def write_sums(values):
            kernel_grad[0:9, cols] = values

        weights = taps_at(kernel, 768 * s + 384 * core + LANES * heads)
        return hold_steps(
            held, lambda g: d_conv[g * 256 : g * 256 + 256, cols].astype(F32)
        ) + back_steps(held, weights, lambda rows: qkv[rows, source_cols].astype(F32), write, write_sums)

    def grad_steps(s):
        cols = slice(s * LANES, (s + 1) * LANES)

        def one(place, out):
            rows = pl.ds(pl.multiple_of(place * 384, 384), 384)
            out[0:384, cols] = dot(normed[:, rows], qkv_grad[:, cols], 0, 0).astype(BF)

        return [step(one, sc.bits[0], weight_keep), step(one, 1 - sc.bits[0], weight_send)]

    weave(value_steps())
    weave([step(one, g, h) for g in range(GROUPS) for h in range(2)], local_steps(2))
    weave(local_steps(0), grad_steps(2))
    weave(local_steps(1), grad_steps(0))
    weave(grad_steps(1))
    if last:
        weight_send[384 : 384 + TAPS, :] = kernel_grad[...].astype(BF)


def attend_back(line, heads, last, att_grad, out_weight, normed, qkv, conv, prob, attn_kernel, before):
    width = 384 + (before[0].shape[1] if before else 0)
    return run(
        functools.partial(attend_back_kernel, heads, last), "attend_back", line,
        (att_grad, out_weight, normed, qkv, conv, prob, attn_kernel, *before),
        [shaped(1024, 384), shaped(384, width), shaped(384 + (TAPS if last else 0), width),
         shaped(TAPS, width, dtype=F32)],
        [HELD, pltpu.VMEM((1024, LANES), BF), pltpu.VMEM((1024, 384), BF)], us=6.3,
    )


def first_back_kernel(sc, g0, g1, g2, weight, branch, keep, send):
    core = sc.core
    send[8:16] = branch[...]
    for g in range(GROUPS):
        rows = slice(g * 256, g * 256 + 256)
        total = None
        for k, grad in enumerate((g0, g1, g2)):
            part = dot(grad[rows, :], weight[:, 384 * k : 384 * k + 384], 1, 1)
            total = part if total is None else total + part
        for local in range(2):
            kept, sent = keep_half(core, total, local)
            keep[2 * g + local] = kept
            send[2 * g + local] = sent.astype(BF)


def first_back(line, grads, weight, branch):
    return run(
        first_back_kernel, "first_back", line, (*grads, weight, branch),
        [shaped(8, 64, 768, dtype=F32), shaped(16, 64, 768)], us=2.7
    )


def finish_kernel(
    sc, base, attended, branch, grad, other, seed, middle_grad, sums_two, mod, near_out, far_out, cond,
):
    height, breadth, core = sc.height, sc.breadth, sc.core
    scale, gate_one, gate, factor = 1.0 + mod[1:2, :], mod[2:3, :], mod[5:6, :], mod[6:7, :]
    matrix = to_phase_matrix()
    d_shift, d_scale, d_gate = [jnp.zeros((1, 768), F32) for _ in range(3)]
    done = []
    for local in range(2):
        outs, grads = [], []
        for g in range(GROUPS):
            at = 2 * g + local
            start = pl.multiple_of(g * 256 + (2 * local + core) * 64, 64)
            rows = pl.ds(start, 64)
            live = live_run(start, height, breadth)
            first = base[rows, :].astype(F32)
            whole = branch[at] + other[8 + at].astype(F32)
            d_gate = d_gate + col_sum(seed[rows, :].astype(F32) * whole)
            result = first + gate_one * attended[rows, :].astype(F32) + gate * whole
            outs.append((result * live).astype(BF))
            total = grad[at] + other[at].astype(F32)
            unit, inverse = normal(first)
            both = total * unit
            d_shift = d_shift + col_sum(total)
            d_scale = d_scale + col_sum(both)
            total = total * scale
            mean = jnp.mean(total, axis=-1, keepdims=True)
            along = jnp.mean(both * scale, axis=-1, keepdims=True)
            total = middle_grad[rows, :] + inverse * (total - mean - unit * along)
            grads.append((total * live).astype(BF))
        done.append([
            dot(matrix, jnp.concatenate(parts, axis=0), 0, 0).astype(BF) for parts in (outs, grads)
        ])

    @pl.when(sc.pair == 0)
    def _():
        for k in range(2):
            near_out[k] = done[0][k]
            far_out[k] = done[1][k]

    @pl.when(sc.pair != 0)
    def _():
        for k in range(2):
            near_out[k] = done[1][k]
            far_out[k] = done[0][k]

    rows = d_shift, d_scale, sums_two[2:3, :], sums_two[1:2, :], d_gate * factor, sums_two[0:1, :]
    for k, row in enumerate(rows):
        cond[k : k + 1, :] = row


def finish(line, *operands):
    return run(
        finish_kernel, "finish", line, operands,
        [shaped(2, 256, 768), shaped(2, 256, 768), shaped(6, 768, dtype=F32)], items=True, us=4.5,
    )


def swap(values, axis, bit):
    count = lax.axis_size(axis)
    return lax.ppermute(values, axis, [(i, i ^ bit) for i in range(count)])


def swap_at(values, k):
    wide, narrow = lax.axis_size(WIDE), lax.axis_size(NARROW)
    steps = {"x": (0, 2), "y": (1, 0), "z": (2, 0), "w": (4, 0)}
    pairs = []
    for w in range(wide):
        for n in range(narrow):
            dw, dn = steps[HALVINGS[n % 2][k]]
            pairs.append((w * narrow + n, (w ^ dw) * narrow + (n ^ dn)))
    return lax.ppermute(values, (WIDE, NARROW), pairs)


def bits_of(count):
    return [1 << k for k in range(count.bit_length() - 1)]


def halve_kernel(k, tapped, sc, kept, got, *rest):
    taps, rest = (rest[0], rest[1:]) if tapped else (None, rest)
    keep, send = rest[-3:-1] if tapped else rest[-2:]
    half = keep.shape[0]
    if tapped:
        rest[-1][...] = taps[...].astype(BF).astype(F32) + got[2 * half : 2 * half + TAPS, :].astype(F32)
        send[half : half + TAPS, :] = rest[-1][...].astype(BF)
    for d, out in enumerate((keep, send)):
        rows = pl.ds(pl.multiple_of((sc.bits[k] ^ d) * half, 16), half)
        out[0:half, :] = (kept[rows, :].astype(F32) + got[rows, :].astype(F32)).astype(BF)


def total_kernel(tapped, sc, kept, got, *rest):
    rows, width = kept.shape
    if tapped:
        taps, *rest, taps_out = rest
        taps_out[...] = taps[...].astype(BF).astype(F32) + got[rows : rows + TAPS, :].astype(F32)
    *cond, out = rest
    out[0:rows, :] = (kept[...].astype(F32) + got[0:rows, :].astype(F32)).astype(BF)
    if cond:
        count = (out.shape[0] - rows) * width // (6 * 768)
        hot = [jnp.where(sc.home == k, cond[0][...], 0.0) for k in range(count)]
        hot = jnp.concatenate(hot, axis=0).astype(BF)
        part = 6 * count * 768 // width
        for k in range(width // 768):
            out[rows : rows + part, 768 * k : 768 * k + 768] = hot[k * part : (k + 1) * part, :]


def stack_kernel(extra, tapped, sc, kept, got, *rest):
    *taps, out = rest
    half = kept.shape[0] - extra
    out[0:half, :] = kept[0:half, :]
    out[half : 2 * half, :] = got[0:half, :]
    if extra:
        below = slice(half, half + extra)
        out[2 * half : 2 * half + extra, :] = (
            kept[below, :].astype(F32) + got[below, :].astype(F32)
        ).astype(BF)
    if taps:
        out[2 * half + extra : 2 * half + extra + TAPS, :] = taps[0][...].astype(BF)


class Flow:
    def __init__(self, line, keep, send, taps=None):
        self.line = line
        self.taps = () if taps is None else (taps,)
        self.extra = 0
        for bit in bits_of(lax.axis_size(WIDE))[3:]:
            keep, send = [
                (v.astype(F32) + swap(v, WIDE, bit).astype(F32)).astype(BF) for v in (keep, send)
            ]
            self.taps = tuple(v + swap(v, WIDE, bit) for v in self.taps)
        self.kept, self.got = keep, swap_at(send, 0)

    def below(self):
        return [shaped(*v.shape, dtype=F32) for v in self.taps]

    def halve(self, k):
        rows, width = self.kept.shape
        tapped = len(self.taps) > 0
        self.kept, send, *self.taps = run(
            functools.partial(halve_kernel, k, tapped), "halve", self.line,
            (self.kept, self.got, *self.taps),
            [shaped(rows // 2, width), shaped(rows // 2 + (TAPS if tapped else 0), width)] + self.below(),
        )
        self.got = swap_at(send, k)

    def total(self, cond=None):
        rows, width = self.kept.shape
        if cond is not None:
            self.extra = 6 * lax.axis_size(WIDE) * 768 // width
        operands = (self.kept, self.got, *self.taps, *(() if cond is None else (cond,)))
        self.kept, *self.taps = run(
            functools.partial(total_kernel, len(self.taps) > 0), "total", self.line, operands,
            [shaped(rows + self.extra, width)] + self.below(), items=cond is not None,
        )
        self.got = swap_at(self.kept, 3)

    def stack(self, k):
        rows, width = self.kept.shape
        rows = 2 * (rows - self.extra) + self.extra
        taps = () if k else tuple(self.taps)
        (self.kept,) = run(
            functools.partial(stack_kernel, self.extra, len(taps) > 0), "stack", self.line,
            (self.kept, self.got, *taps), [shaped(rows + TAPS * len(taps), width)],
        )
        self.got = swap_at(self.kept, k - 1) if k else swap(self.kept, NARROW, 1)


def by_core(core, write, own, other):
    @pl.when(core == 0)
    def _():
        write(own, other)

    @pl.when(core != 0)
    def _():
        write(other, own)


def copy_each(steps, sems):
    copies = []
    for k, (fill, src, dst) in enumerate(steps):
        fill()
        copies.append(pltpu.make_async_copy(src, dst, sems.at[k]))
        copies[-1].start()
    for copy in copies:
        copy.wait()


def gathered_runs(chip):
    for group in range(4):
        runs_here = [
            (slice(48 * (4 * group + k), 48 * (4 * group + k + 1)),
             pl.ds(pl.multiple_of((k ^ (chip & 3)) * 48, 16), 48))
            for k in range(4)
        ]
        yield group, group ^ (chip >> 2), runs_here


def rows_at(start):
    return pl.ds(pl.multiple_of(start * 192, 64), 192)


def down_done_kernel(sc, own, other, out, buffer, sems):
    def fill(part, k, group, runs_here):
        for rows, dest in runs_here:
            for half in range(2):
                buffer[k, group, half, dest, :] = part[rows, 768 * half : 768 * half + 768].astype(F32)

    copy_each(
        [
            (step(fill, part, k, group, runs_here), buffer.at[k, group],
             out.at[core, :, rows_at(place), :])
            for k, (part, chip, core) in enumerate(
                ((own, sc.chip, sc.core), (other, sc.other_chip, 1 - sc.core))
            )
            for group, place, runs_here in gathered_runs(chip)
        ],
        sems,
    )


def down_done(line, flow):
    (out,) = run(
        down_done_kernel, "down_done", line, (flow.kept, flow.got), [shaped(2, 2, 768, 768, dtype=F32)],
        [pltpu.VMEM((2, 4, 2, 192, 768), F32), pltpu.SemaphoreType.DMA((8,))], far_outs=(0,),
        limit=12 * 1024 * 1024, us=4.0,
    )
    return out.reshape(3072, 768)


def up_done_kernel(sc, own, other, out, taps_out, buffer, sems):
    def write(first, second):
        for core, part in enumerate((first, second)):
            taps = part[768 : 768 + TAPS, :].astype(F32)
            for a in range(3):
                taps_out[a, :, 1536 * core : 1536 * core + 1536] = taps[3 * a : 3 * a + 3, :]

    by_core(sc.core, write, own, other)

    def fill(part, k, group, runs_here):
        for rows, dest in runs_here:
            buffer[k, group, dest, :] = part[rows, :].astype(F32)

    copy_each(
        [
            (step(fill, part, k, group, runs_here), buffer.at[k, group],
             out.at[rows_at(place), pl.ds(pl.multiple_of(core * 1536, 1536), 1536)])
            for k, (part, chip, core) in enumerate(
                ((own, sc.chip, sc.core), (other, sc.other_chip, 1 - sc.core))
            )
            for group, place, runs_here in gathered_runs(chip)
        ],
        sems,
    )


def up_done(line, flow):
    return run(
        up_done_kernel, "up_done", line, (flow.kept, flow.got),
        [shaped(768, 3072, dtype=F32), shaped(3, 3, 3072, dtype=F32)],
        [pltpu.VMEM((2, 4, 192, 1536), F32), pltpu.SemaphoreType.DMA((8,))], far_outs=(0,),
        limit=14 * 1024 * 1024, us=4.0,
    )


def attend_done_kernel(where, sc, *refs):
    count = (len(refs) - 8) // 2
    own, other = refs[:count], refs[count : 2 * count]
    qkv_grad, out_grad, taps_out, cond_out, shift_out, qkv, out, sems = refs[2 * count :]

    def fill(parts, k, group, runs_here, s):
        for rows, dest in runs_here:
            for heads in range(3):
                flow, col = where[heads]
                col = col + LANES * s
                qkv[k, group, s, dest, LANES * heads : LANES * heads + LANES] = parts[flow][
                    rows, col : col + LANES
                ].astype(F32)

    def fill_out(parts, k, group, runs_here):
        for rows, dest in runs_here:
            flow, col = where[3]
            out[k, group, dest, :] = parts[flow][rows, col : col + 384].astype(F32)

    steps = []
    for k, (parts, chip, core) in enumerate(
        ((own, sc.chip, sc.core), (other, sc.other_chip, 1 - sc.core))
    ):
        for group, place, runs_here in gathered_runs(chip):
            for s in range(3):
                cols = pl.ds(pl.multiple_of(768 * s + 384 * core, LANES), 384)
                steps.append((
                    step(fill, parts, k, group, runs_here, s), qkv.at[k, group, s],
                    qkv_grad.at[rows_at(place), cols],
                ))
            cols = pl.ds(pl.multiple_of((place >> 1) * 384, LANES), 384)
            steps.append((
                step(fill_out, parts, k, group, runs_here), out.at[k, group],
                out_grad.at[core, rows_at(place & 1), cols],
            ))

    def write(first, second):
        for core, parts in enumerate((first, second)):
            taps = [part[part.shape[0] - TAPS :, :].astype(F32) for part in parts]
            for a in range(3):
                for heads in range(3):
                    flow, col = where[heads]
                    for s in range(3):
                        to = 768 * s + 384 * core + LANES * heads
                        at = col + LANES * s
                        taps_out[a, :, to : to + LANES] = taps[flow][3 * a : 3 * a + 3, at : at + LANES]

    by_core(sc.core, write, own, other)
    mine, its = own[-1], other[-1]
    extra = mine.shape[0] - 768 - TAPS
    total = mine[768 : 768 + extra, :].astype(F32) + its[768 : 768 + extra, :].astype(F32)
    rows = jnp.zeros((6, 768), F32)
    for k in range(extra // 6):
        rows = rows + jnp.where(sc.wide == k, total[6 * k : 6 * k + 6, :], 0.0)
    for k in range(5):
        cond_out[:, 768 * k : 768 * k + 768] = rows[k : k + 1, :]
    shift_out[...] = rows[5:6, :]
    copy_each(steps, sems)


def attend_done(line, where, flows):
    qkv_grad, out_grad, attn_grad, cond_grad, shift_grad = run(
        functools.partial(attend_done_kernel, where), "attend_done", line,
        [flow.kept for flow in flows] + [flow.got for flow in flows],
        [shaped(768, 2304, dtype=F32), shaped(2, 384, 768, dtype=F32), shaped(3, 3, 2304, dtype=F32),
         shaped(1, 3840, dtype=F32), shaped(1, 768, dtype=F32)],
        [pltpu.VMEM((2, 4, 3, 192, 384), F32), pltpu.VMEM((2, 4, 192, 384), F32),
         pltpu.SemaphoreType.DMA((32,))],
        far_outs=(0, 1), limit=16 * 1024 * 1024, us=4.0,
    )
    return qkv_grad, out_grad.reshape(768, 768), attn_grad, cond_grad, shift_grad


def join_kernel(sc, near, far, out, grad_out):
    for k, target in enumerate((out, grad_out)):
        target[sc.pair] = near[k]
        target[1 - sc.pair] = far[k]


def join(line, near, far):
    out, grad = run(join_kernel, "join", line, (near, far), [shaped(2, 256, 768)] * 2)
    return out.reshape(2, 8, 32, 768), grad.reshape(2, 8, 32, 768)


def copy_all(sems, pairs):
    copies = [pltpu.make_async_copy(src, dst, sems.at[k]) for k, (src, dst) in enumerate(pairs)]
    for copy in copies:
        copy.start()
    for copy in copies:
        copy.wait()


def cut_pieces_kernel(sc, block, far, own, sems):
    copy_all(sems, [(block.at[1 - sc.pair], far), (block.at[sc.pair], own)])


def cut_pieces(line, block):
    return run(
        cut_pieces_kernel, "cut_pieces", line, (block.reshape(2, 256, 768),), [shaped(256, 768)] * 2,
        [pltpu.SemaphoreType.DMA((2,))], far=(0,), limit=ALL_VMEM,
    )


def pass_kernel(sc, *refs):
    count = len(refs) // 2
    for k in range(count):
        refs[count + k][...] = refs[k][...]


def pass_on(line, *arrays):
    return run(pass_kernel, "pass_on", line, arrays, [shaped(*v.shape) for v in arrays])


def pack_kernel(sc, one, two, out):
    out[0:256, :] = one[...]
    out[256:512, :] = two[...]


def cut_weights_kernel(sc, qkv, out, up, down, qkv_part, out_part, up_part, down_part, sems):
    core = sc.core
    pairs = [
        (
            qkv.at[:, lanes_at(768 * s + 384 * core + LANES * pair)],
            qkv_part.at[:, pl.ds((3 * pair + s) * LANES, LANES)],
        )
        for pair in range(3)
        for s in range(3)
    ]
    pairs += [
        (out.at[pl.ds(pl.multiple_of(384 * core, 384), 384), :], out_part),
        (up.at[:, pl.ds(pl.multiple_of(1536 * core, 1536), 1536)], up_part),
        (down.at[pl.ds(pl.multiple_of(1536 * core, 1536), 1536), :], down_part),
    ]
    copy_all(sems, pairs)


def cut_weights(line, qkv_weight, out_weight, up_weight, down_weight):
    return run(
        cut_weights_kernel, "cut_weights", line, (qkv_weight, out_weight, up_weight, down_weight),
        [shaped(768, 1152), shaped(384, 768), shaped(768, 1536), shaped(1536, 768)],
        [pltpu.SemaphoreType.DMA((12,))], far=(0, 1, 2, 3), limit=ALL_VMEM, us=2.5
    )


def on_device(
    tokens, cotangent, conditioning, aspect, bucket,
    qkv_weight, attn_kernel, out_weight, up_weight, ffn_kernel, down_weight,
):
    wide_count = lax.axis_size(WIDE)
    line = Line(aspect, bucket)
    far, own = cut_pieces(line, tokens)
    got = swap(far, NARROW, 2)
    own_other = swap(own, NARROW, 1)
    cond_right = lax.ppermute(conditioning, WIDE, [(i + 1, i) for i in range(wide_count - 1)])
    weights = cut_weights(line, qkv_weight, out_weight, up_weight, down_weight)
    qkv_part, out_part, up_part, down_part = weights
    seed_far, seed_own = cut_pieces(line, cotangent)
    got, cond_right = pass_on(line, got, cond_right)
    token_pieces = own, got, own_other, swap(got, NARROW, 1)
    base, normed_one, qkv, conv, prob, mixed, mod = attend(
        line, token_pieces, conditioning, cond_right, qkv_part, attn_kernel
    )
    (seeds,) = run(pack_kernel, "pack", line, (seed_own, swap(seed_far, NARROW, 2)), [shaped(512, 768)])
    mixed_other = swap(mixed, NARROW, 1)
    seed_pieces = seeds, swap(seeds, NARROW, 1)
    attended, normed_two, d_branch, seed = project_out(
        line, mixed, mixed_other, base, out_weight, mod, seed_pieces
    )

    def back(heads, last, d_att, before):
        return attend_back(
            line, heads, last, d_att, out_part, normed_one, qkv, conv, prob, attn_kernel, before
        )

    keep, send, *saved = feed(line, normed_two, d_branch, up_part, down_part, ffn_kernel)
    a = Flow(line, keep, send)
    keep, send, taps, branch, branch_send, d_normed = feed_back(
        line, normed_two, up_part, down_part, ffn_kernel, *saved
    )
    b = Flow(line, keep, send, taps)
    a.halve(1)
    (d_normed_send,) = pass_on(line, d_normed)
    d_normed_other = swap(d_normed_send, NARROW, 1)
    d_middle, d_att, sums_two, *parts = norm_back(
        line, d_normed, d_normed_other, base, attended, seed, mod, mixed
    )
    g0, *parts = back(0, True, d_att, parts)
    c = Flow(line, *parts)
    g1, *parts = back(1, False, d_att, ())
    a.halve(2)
    a.halve(3)
    c.halve(1)
    b.halve(1)
    g2, *parts = back(2, True, d_att, parts)
    d = Flow(line, *parts)
    a.total()
    b.halve(2)
    d_first, d_first_send = first_back(line, (g0, g1, g2), qkv_part, branch_send)
    d.halve(1)
    b.halve(3)
    a.stack(3)
    c.halve(2)
    (d_first_send,) = pass_on(line, d_first_send)
    d_first_other = swap(d_first_send, NARROW, 1)
    a.stack(2)
    near, far, cond = finish(
        line, base, attended, branch, d_first, d_first_other, seed, d_middle, sums_two, mod
    )
    far = swap(far, NARROW, 2)
    d.halve(2)
    c.halve(3)
    b.total()
    a.stack(1)
    b.stack(3)
    c.total()
    d.halve(3)
    block_out, tokens_grad = join(line, near, far)
    d.total(cond)
    c.stack(3)
    b.stack(2)
    b.stack(1)
    c.stack(2)
    a.stack(0)
    d.stack(3)
    b.stack(0)
    d.stack(2)
    c.stack(1)
    d.stack(1)
    c.stack(0)
    down_grad = down_done(line, a)
    d.stack(0)
    up_grad, ffn_grad = up_done(line, b)
    where = (0, 0), (1, 384), (1, 0), (0, 384)
    qkv_grad, out_grad, attn_grad, cond_grad, shift_grad = attend_done(line, where, (c, d))

    return (
        block_out, tokens_grad, cond_grad, shift_grad, qkv_grad, attn_grad, out_grad, up_grad, ffn_grad,
        down_grad,
    )


def solution(mesh):
    rows = P(WIDE, NARROW, None, None)
    in_specs = (rows, rows, P(WIDE, None)) + (P(),) * 8
    out_specs = (rows, rows, P(WIDE, None), P(WIDE, None)) + (P(),) * 6
    return jax.shard_map(
        on_device, mesh=mesh, in_specs=in_specs, out_specs=out_specs, check_vma=False
    )
```
